32 devices in a mesh: section: 2 (over x), dp: 16 (over z, y, core).
Axes of the slice: x: 2, y: 2, z: 4, core: 2. Of those that a mesh axis runs over, the one named last changes fastest.
Arguments:
- tokens: bfloat16 [32, 256, 1152], P('dp'), may hold values from -6 to 6
- cotangent: bfloat16 [2, 32, 256, 1152], P('section', 'dp'), may hold values from -6 to 6
- labels: int32 [32], P('dp'), may hold values from 0 to 1000
- timesteps: int32 [32], P('dp'), may hold values from 0 to 999
- positions: int32 [32, 256], P('dp'), may hold values from 0 to 255, each once within a row
- label_table: bfloat16 [1001, 1152], replicated, may hold values from -6 to 6
- ada_weight: bfloat16 [2, 1152, 6912], P('section', 'dp'), may hold values from -0.25 to 0.25
- qkv_weight: bfloat16 [2, 1152, 3456], P('section', 'dp'), may hold values from -0.1875 to 0.1875
- out_weight: bfloat16 [2, 1152, 1152], P('section', 'dp'), may hold values from -1.5 to 1.5
- gate_weight: bfloat16 [2, 1152, 3072], P('section', 'dp'), may hold values from -0.1875 to 0.1875
- up_weight: bfloat16 [2, 1152, 3072], P('section', 'dp'), may hold values from -0.1875 to 0.1875
- down_weight: bfloat16 [2, 3072, 1152], P('section', 'dp'), may hold values from -0.109375 to 0.109375
- q_gain: float32 [2, 72], P('section'), may hold values from 0.1 to 1.9
- k_gain: float32 [2, 72], P('section'), may hold values from 0.1 to 1.9
Outputs:
- layer_outputs: bfloat16 [2, 32, 256, 1152], P('section', 'dp')
- input_grads: float32 [2, 32, 256, 1152], P('section', 'dp')
- table_grad: float32 [1001, 1152], replicated
- ada_grad: float32 [2, 1152, 6912], P('section', 'dp')
- qkv_grad: float32 [2, 1152, 3456], P('section', 'dp')
- out_grad: float32 [2, 1152, 1152], P('section', 'dp')
- gate_grad: float32 [2, 1152, 3072], P('section', 'dp')
- up_grad: float32 [2, 1152, 3072], P('section', 'dp')
- down_grad: float32 [2, 3072, 1152], P('section', 'dp')
- q_gain_grad: float32 [2, 72], P('section')
- k_gain_grad: float32 [2, 72], P('section')
The draws below stay inside these ranges and needn't reach their ends.
Inputs may be any that keep to these rules, and one draw needn't show every extreme that they name: `positions`: each image's row holds every grid position 0 to 255 once.
All inputs are finite; a program needn't handle non-finite values.
Results may differ from the reference program's by a relative error of at most 0.013.
Values may be sent and summed in bfloat16 or wider, within the bound.
No kernel may reach another device: no remote copies, remote signals or barrier semaphores. Data moves between devices by JAX's collectives and lax.ppermute only.
A program may use at most 640 MiB of HBM per device.

```python
import math
import jax
import jax.numpy as jnp
from jax import lax

D = 1152
HEADS = 16
HD = 72
FF = 3072
CLASSES = 1001
GRID = 16
PATCHES = 256
LAYERS = 2
IMAGES = 32


def touch_ends(drawn, own_key, low, top_value):
    extent = drawn.shape
    place = [jax.random.randint(jax.random.fold_in(own_key, axis), (), 0, extent[axis]) for axis in range(len(extent))]
    drawn = drawn.at[tuple(place)].set(low)
    longest = extent.index(max(extent))
    place[longest] = (place[longest] + 1) % extent[longest]
    return drawn.at[tuple(place)].set(top_value)


def block_scale(stream_key, extent, cuts, smallest, top_value):
    gain, own = 1.0, jax.random.fold_in(stream_key, 6)
    for dim, shards_of in cuts:
        draws = jnp.exp(jax.random.uniform(jax.random.fold_in(own, dim), (shards_of,), jnp.float32, smallest / len(cuts), top_value / len(cuts)))
        gain = gain * jnp.repeat(draws, extent[dim] // shards_of).reshape([-1 if axis == dim else 1 for axis in range(len(extent))])
    return gain


def centred(own_key, dims, deviation, most, cuts=(), kind=jnp.bfloat16):
    values = jax.random.normal(own_key, dims, jnp.float32) * deviation
    if len(cuts) > 0:
        values = block_scale(own_key, dims, cuts, -0.22, 0.18) * values
    return jnp.clip(values, min=-most, max=most).astype(kind)


def setup_inputs(seed: int = 0) -> dict:
    key_of = jax.random.split(jax.random.key(seed), 15)
    return {
        "tokens": centred(key_of[0], (IMAGES, PATCHES, D), 1.0, 6.0, ((0, 16),)),
        "cotangent": centred(key_of[1], (LAYERS, IMAGES, PATCHES, D), 1.0, 6.0, ((0, 2), (1, 16))),
        "labels": touch_ends(jax.random.randint(key_of[2], (IMAGES,), 0, CLASSES), jax.random.fold_in(key_of[2], 1), 0, CLASSES - 1).astype(jnp.int32),
        "timesteps": touch_ends(jax.random.randint(key_of[3], (IMAGES,), 0, 1000), jax.random.fold_in(key_of[3], 1), 0, 999).astype(jnp.int32),
        "positions": jax.vmap(lambda own: jax.random.permutation(own, PATCHES))(jax.random.split(key_of[4], IMAGES)).reshape((IMAGES, PATCHES)).astype(jnp.int32),
        "label_table": centred(key_of[5], (CLASSES, D), 1.0, 6.0),
        "ada_weight": centred(key_of[6], (LAYERS, D, 6 * D), (D // 2) ** -0.5, 0.25, ((0, 2), (1, 16))),
        "qkv_weight": centred(key_of[7], (LAYERS, D, 3 * D), D ** -0.5, 0.1875, ((0, 2), (1, 16))),
        "out_weight": centred(key_of[8], (LAYERS, D, D), (D // 64) ** -0.5, 1.5, ((0, 2), (1, 16))),
        "gate_weight": centred(key_of[9], (LAYERS, D, FF), D ** -0.5, 0.1875, ((0, 2), (1, 16))),
        "up_weight": centred(key_of[10], (LAYERS, D, FF), D ** -0.5, 0.1875, ((0, 2), (1, 16))),
        "down_weight": centred(key_of[11], (LAYERS, FF, D), FF ** -0.5, 0.109375, ((0, 2), (1, 16))),
        "q_gain": jnp.clip(1.0 + 0.18 * jax.random.normal(key_of[12], (LAYERS, HD), jnp.float32), 0.1, 1.9),
        "k_gain": jnp.clip(1.0 + 0.18 * jax.random.normal(key_of[13], (LAYERS, HD), jnp.float32), 0.1, 1.9),
    }


epsilon = 1e-06

@jax.custom_vjp
def lower_precision_copy(v):
    return lax.optimization_barrier(v.astype(jnp.bfloat16)).astype(jnp.float32)

@jax.custom_vjp
def lower_precision_backward(v):
    return v

def low_keep(v):
    return (lower_precision_copy(v), None)

def low_pass(kept, grad):
    return (grad,)

def back_keep(v):
    return (v, None)

def back_low(kept, grad):
    return (lower_precision_copy(grad),)
lower_precision_copy.defvjp(low_keep, low_pass)
lower_precision_backward.defvjp(back_keep, back_low)

def product(left, right):
    return jnp.matmul(left, right, precision=lax.Precision.HIGHEST)

def rms_norm(values):
    return values * lax.rsqrt(lax.optimization_barrier(jnp.mean(values * values, axis=-1, keepdims=True)) + epsilon)

def rope_angles(positions):
    quarter = HD // 4
    frequency = jnp.exp(-math.log(10000.0) * jnp.arange(quarter, dtype=jnp.float32) / quarter)
    row_pos = (positions // GRID).astype(jnp.float32)
    col_pos = (positions % GRID).astype(jnp.float32)
    return (row_pos[..., None] * frequency, col_pos[..., None] * frequency)

def rotate(tensor, row_rotation, column_rotation):
    first_a, first_b, second_a, second_b = jnp.split(tensor, 4, axis=-1)
    row_cos = jnp.cos(row_rotation)[:, :, None, :]
    row_sin = jnp.sin(row_rotation)[:, :, None, :]
    col_cos = jnp.cos(column_rotation)[:, :, None, :]
    col_sin = jnp.sin(column_rotation)[:, :, None, :]
    return jnp.concatenate([first_a * row_cos - first_b * row_sin, first_a * row_sin + first_b * row_cos, second_a * col_cos - second_b * col_sin, second_a * col_sin + second_b * col_cos], axis=-1)

def time_features(timestep_ids):
    half_width = D // 2
    frequency = jnp.exp(-math.log(10000.0) * jnp.arange(half_width, dtype=jnp.float32) / half_width)
    angle_rows = timestep_ids.astype(jnp.float32)[:, None] * frequency[None, :]
    return jnp.concatenate([jnp.cos(angle_rows), jnp.sin(angle_rows)], axis=-1)

def diffusion_transformer_block(residual_flow, swish_condition, weights_per_layer, row_rotation, column_rotation):
    ada_matrix, qkv_matrix, out_matrix, gate_matrix, up_matrix, down_matrix, query_gain, key_gain = weights_per_layer
    modulation = lower_precision_backward(product(swish_condition, ada_matrix))
    shift_one, scale_one, gate_one, shift_two, scale_two, gate_two = jnp.split(modulation[:, None, :], 6, axis=-1)
    normed = lower_precision_copy(rms_norm(residual_flow) * (1.0 + scale_one) + shift_one)
    projected = lower_precision_backward(product(normed, qkv_matrix))
    images, patches = (residual_flow.shape[0], residual_flow.shape[1])
    split_heads = projected.reshape(images, patches, 3, HEADS, HD)
    queries = lower_precision_copy(rotate(rms_norm(split_heads[:, :, 0]) * query_gain, row_rotation, column_rotation))
    keys_rot = lower_precision_copy(rotate(rms_norm(split_heads[:, :, 1]) * key_gain, row_rotation, column_rotation))
    values = lower_precision_copy(split_heads[:, :, 2])
    scores = lower_precision_backward(jnp.einsum('blhd,bmhd->bhlm', queries, keys_rot, precision=lax.Precision.HIGHEST) * HD ** (-0.5))
    attention = jax.nn.softmax(scores, axis=-1)
    attended = jnp.einsum('bhlm,bmhd->blhd', lower_precision_copy(attention), values, precision=lax.Precision.HIGHEST)
    attended = lower_precision_copy(lower_precision_backward(attended)).reshape(images, patches, D)
    after_attn = residual_flow + gate_one * lower_precision_backward(product(attended, out_matrix))
    normed_two = lower_precision_copy(rms_norm(after_attn) * (1.0 + scale_two) + shift_two)
    gate_val = lower_precision_backward(product(normed_two, gate_matrix))
    up_val = lower_precision_backward(product(normed_two, up_matrix))
    activated = lower_precision_copy(jax.nn.silu(gate_val) * up_val)
    return after_attn + gate_two * lower_precision_backward(product(activated, down_matrix))

def reference(tokens, cotangent, labels, timesteps, positions, label_table, ada_weight, qkv_weight, out_weight, gate_weight, up_weight, down_weight, q_gain, k_gain):
    group = math.gcd(IMAGES, max(1, 4096 // PATCHES))
    group_count = IMAGES // group
    floats = (label_table.astype(jnp.float32), ada_weight.astype(jnp.float32), qkv_weight.astype(jnp.float32), out_weight.astype(jnp.float32), gate_weight.astype(jnp.float32), up_weight.astype(jnp.float32), down_weight.astype(jnp.float32), q_gain.astype(jnp.float32), k_gain.astype(jnp.float32))

    def one_group(totals, pieces):
        tok_rows, cot_rows, label_rows, time_rows, pos_rows = pieces
        row_rotation, column_rotation = rope_angles(pos_rows)

        def forward(residual_flow, params, reserve_buffer):
            table, ada_all, qkv_all, out_all, gate_all, up_all, down_all, qgain_all, kgain_all = params
            label_hot = (label_rows[:, None] == jnp.arange(CLASSES)[None, :]).astype(jnp.float32)
            condition = product(label_hot, table) + time_features(time_rows)
            swish_condition = lower_precision_copy(jax.nn.silu(condition))
            leading_block_weights = (ada_all[0], qkv_all[0], out_all[0], gate_all[0], up_all[0], down_all[0], qgain_all[0], kgain_all[0])
            trailing_block_weights = (ada_all[1], qkv_all[1], out_all[1], gate_all[1], up_all[1], down_all[1], qgain_all[1], kgain_all[1])
            hidden_tokens = lower_precision_copy(diffusion_transformer_block(residual_flow, swish_condition, leading_block_weights, row_rotation, column_rotation))
            closing_output = diffusion_transformer_block(lower_precision_backward(hidden_tokens + reserve_buffer), swish_condition, trailing_block_weights, row_rotation, column_rotation)
            return (hidden_tokens, closing_output)
        reserve_buffer = jnp.zeros(tok_rows.shape, jnp.float32)
        outputs, pull = jax.vjp(forward, tok_rows.astype(jnp.float32), floats, reserve_buffer)
        grad_tokens, grad_params, grad_spare = pull((cot_rows[0].astype(jnp.float32), cot_rows[1].astype(jnp.float32)))
        totals = jax.tree.map(jnp.add, totals, grad_params)
        return (totals, (outputs[0], outputs[1], grad_tokens, grad_spare))
    token_groups = tokens.reshape(group_count, group, PATCHES, D)
    cot_groups = jnp.moveaxis(cotangent.reshape(2, group_count, group, PATCHES, D), 1, 0)
    label_groups = labels.reshape(group_count, group)
    time_groups = timesteps.reshape(group_count, group)
    pos_groups = positions.reshape(group_count, group, PATCHES)
    start = jax.tree.map(jnp.zeros_like, floats)
    totals, stacked = lax.scan(one_group, start, (token_groups, cot_groups, label_groups, time_groups, pos_groups))
    hidden_all = stacked[0].reshape(IMAGES, PATCHES, D)
    final_all = stacked[1].reshape(IMAGES, PATCHES, D)
    grad_first = stacked[2].reshape(IMAGES, PATCHES, D)
    grad_second = stacked[3].reshape(IMAGES, PATCHES, D)
    layer_outputs = jnp.stack([hidden_all, final_all]).astype(jnp.bfloat16)
    input_grads = jnp.stack([grad_first, grad_second])
    return (layer_outputs, input_grads, totals[0], totals[1], totals[2], totals[3], totals[4], totals[5], totals[6], totals[7], totals[8])
```

```python
import math

import jax
import jax.numpy as jnp
from jax import lax
from jax.sharding import PartitionSpec as P

HD = 72
GRID = 16
epsilon = 1e-06
f32 = jnp.float32
bf16 = jnp.bfloat16


def product(left, right):
    return jnp.dot(left, right, preferred_element_type=f32)


def product_right(left, right):
    return lax.dot_general(
        left, right, (((left.ndim - 1,), (1,)), ((), ())), preferred_element_type=f32
    )


def weight_grad(inputs, grads):
    return lax.dot_general(
        inputs, grads, (((0, 1), (0, 1)), ((), ())), preferred_element_type=f32
    )


def walk_of(count):
    chips = count // 2
    order = [chip for chip in range(chips) if chip % 2 == 0]
    order += [chip for chip in reversed(range(chips)) if chip % 2 == 1]
    return [2 * chip + core for chip in order for core in (0, 1)]


def chip_place(chip, chips):
    return chip // 2 if chip % 2 == 0 else chips - 1 - chip // 2


def from_walk(rows, count):
    chips = count // 2
    blocks = rows.reshape(chips, -1, rows.shape[-1])
    picked = [blocks[chip_place(chip, chips)] for chip in range(chips)]
    return jnp.concatenate(picked, axis=0)


def to_walk(rows, count):
    chips = count // 2
    blocks = rows.reshape(chips, -1, rows.shape[-1])
    return jnp.concatenate([blocks[device // 2] for device in walk_of(count)[::2]], axis=0)


def gather_walk(rows, count):
    return lax.all_gather(rows, "dp", axis=0, tiled=True, axis_index_groups=[walk_of(count)])


def scatter_walk(rows, count):
    part = lax.psum_scatter(
        rows, "dp", scatter_dimension=0, tiled=True, axis_index_groups=[walk_of(count)]
    )
    return lax.optimization_barrier(part)


def swapped(block, bit, count):
    return lax.ppermute(block, "dp", [(device, device ^ bit) for device in range(count)])


def gather_small(block, count):
    me = lax.axis_index("dp")
    block = block[None]
    bit = 1
    while bit < count:
        other = swapped(block, bit, count)
        low = (me & bit) == 0
        block = jnp.concatenate(
            [jnp.where(low, block, other), jnp.where(low, other, block)], axis=0
        )
        bit *= 2
    return block


def scatter_small(blocks, count):
    me = lax.axis_index("dp")
    bit = 1
    while bit < count:
        pairs = blocks.reshape(blocks.shape[0] // 2, 2, *blocks.shape[1:])
        mine = jnp.where((me & bit) == 0, 0, 1)
        give = lax.dynamic_index_in_dim(pairs, 1 - mine, 1, keepdims=False)
        keep = lax.dynamic_index_in_dim(pairs, mine, 1, keepdims=False)
        blocks = keep + swapped(give, bit, count)
        bit *= 2
    return blocks[0]


def rms_norm(values):
    return values * lax.rsqrt(jnp.mean(values * values, axis=-1, keepdims=True) + epsilon)


def rope_angles(positions):
    quarter = HD // 4
    frequency = jnp.exp(-math.log(10000.0) * jnp.arange(quarter, dtype=f32) / quarter)
    row_pos = (positions // GRID).astype(f32)
    col_pos = (positions % GRID).astype(f32)
    return (row_pos[..., None] * frequency, col_pos[..., None] * frequency)


def rotate(tensor, row_rotation, column_rotation):
    first_a, first_b, second_a, second_b = jnp.split(tensor, 4, axis=-1)
    row_cos = jnp.cos(row_rotation)[:, :, None, :]
    row_sin = jnp.sin(row_rotation)[:, :, None, :]
    col_cos = jnp.cos(column_rotation)[:, :, None, :]
    col_sin = jnp.sin(column_rotation)[:, :, None, :]
    return jnp.concatenate(
        [
            first_a * row_cos - first_b * row_sin,
            first_a * row_sin + first_b * row_cos,
            second_a * col_cos - second_b * col_sin,
            second_a * col_sin + second_b * col_cos,
        ],
        axis=-1,
    )


def time_features(timestep_ids, width):
    half_width = width // 2
    frequency = jnp.exp(-math.log(10000.0) * jnp.arange(half_width, dtype=f32) / half_width)
    angle_rows = timestep_ids.astype(f32)[:, None] * frequency[None, :]
    return jnp.concatenate([jnp.cos(angle_rows), jnp.sin(angle_rows)], axis=-1)


def prenorm(residual_flow, shift, scale):
    return rms_norm(residual_flow) * (1.0 + scale[:, None, :]) + shift[:, None, :]


def prepare(raw_heads, gain, angles):
    return rotate(rms_norm(raw_heads) * gain, *angles)


def layer_forward(layer_in, modulation, angles, weights):
    qkv_matrix, out_matrix, gate_up_matrix, down_matrix, query_gain, key_gain = weights
    flow = layer_in.astype(f32)
    shift_one, scale_one, gate_one, shift_two, scale_two, gate_two = jnp.split(
        modulation, 6, axis=-1
    )
    normed = prenorm(flow, shift_one, scale_one).astype(bf16)
    projected = product(normed, qkv_matrix)
    images, patches, width = flow.shape
    head_size = query_gain.shape[0]
    split_heads = projected.reshape(images, patches, 3, width // head_size, head_size)
    query_raw = split_heads[:, :, 0]
    key_raw = split_heads[:, :, 1]
    queries = prepare(query_raw, query_gain, angles).astype(bf16)
    keys = prepare(key_raw, key_gain, angles).astype(bf16)
    values = split_heads[:, :, 2].astype(bf16)
    scores = jnp.einsum("blhd,bmhd->bhlm", queries, keys, preferred_element_type=f32)
    scores = scores * head_size ** (-0.5)
    highest = jnp.max(scores, axis=-1, keepdims=True)
    expon = jnp.exp(scores - highest)
    total = jnp.sum(expon, axis=-1, keepdims=True)
    probs = expon / total
    mixed = jnp.einsum("bhlm,bmhd->blhd", probs.astype(bf16), values, preferred_element_type=f32)
    attended = mixed.astype(bf16).reshape(images, patches, width)
    branch = product(attended, out_matrix)
    middle = flow + gate_one[:, None, :] * branch
    normed_two = prenorm(middle, shift_two, scale_two).astype(bf16)
    gate_up = product(normed_two, gate_up_matrix)
    hidden_width = gate_up.shape[-1] // 2
    gate_val, up_val = gate_up[..., :hidden_width], gate_up[..., hidden_width:]
    activated = (jax.nn.silu(gate_val) * up_val).astype(bf16)
    mlp_out = product(activated, down_matrix)
    result = (middle + gate_two[:, None, :] * mlp_out).astype(bf16)
    kept = (
        normed,
        query_raw,
        key_raw,
        queries,
        keys,
        values,
        highest + jnp.log(total),
        attended,
        branch,
        middle,
        normed_two,
        gate_val,
        up_val,
        activated,
        mlp_out,
    )
    return result, kept


def layer_backward(layer_in, modulation, angles, out_grad, weights, kept):
    qkv_matrix, out_matrix, gate_up_matrix, down_matrix, query_gain, key_gain = weights
    (
        normed,
        query_raw,
        key_raw,
        queries,
        keys,
        values,
        log_total,
        attended,
        branch,
        middle,
        normed_two,
        gate_val,
        up_val,
        activated,
        mlp_out,
    ) = kept
    flow = layer_in.astype(f32)
    shift_one, scale_one, gate_one, shift_two, scale_two, gate_two = jnp.split(
        modulation, 6, axis=-1
    )
    images, patches, width = flow.shape
    head_size = query_gain.shape[0]
    heads = width // head_size
    factor = head_size ** (-0.5)
    grad_gate_two = jnp.sum(out_grad * mlp_out, axis=1)
    mlp_grad = (gate_two[:, None, :] * out_grad).astype(bf16)
    act_grad = product_right(mlp_grad, down_matrix)
    sigma = jax.nn.sigmoid(gate_val)
    gate_grad = (act_grad * up_val * sigma * (1.0 + gate_val * (1.0 - sigma))).astype(bf16)
    up_grad = (act_grad * gate_val * sigma).astype(bf16)
    gate_up_grad = jnp.concatenate([gate_grad, up_grad], axis=-1)
    normed_two_grad = product_right(gate_up_grad, gate_up_matrix)
    unused, pull_two = jax.vjp(prenorm, middle, shift_two, scale_two)
    extra_two, grad_shift_two, grad_scale_two = pull_two(normed_two_grad)
    middle_grad = out_grad + extra_two
    grad_gate_one = jnp.sum(middle_grad * branch, axis=1)
    branch_grad = (gate_one[:, None, :] * middle_grad).astype(bf16)
    mixed_grad = product_right(branch_grad, out_matrix).astype(bf16)
    mixed_grad = mixed_grad.reshape(images, patches, heads, head_size)
    scores = jnp.einsum("blhd,bmhd->bhlm", queries, keys, preferred_element_type=f32) * factor
    probs = jnp.exp(scores - log_total)
    value_grad = jnp.einsum(
        "bhlm,blhd->bmhd", probs.astype(bf16), mixed_grad, preferred_element_type=f32
    )
    prob_grad = jnp.einsum("blhd,bmhd->bhlm", mixed_grad, values, preferred_element_type=f32)
    score_grad = probs * (prob_grad - jnp.sum(probs * prob_grad, axis=-1, keepdims=True))
    score_grad = score_grad.astype(bf16)
    query_grad = jnp.einsum("bhlm,bmhd->blhd", score_grad, keys, preferred_element_type=f32)
    key_grad = jnp.einsum("bhlm,blhd->bmhd", score_grad, queries, preferred_element_type=f32)
    unused_q, pull_query = jax.vjp(
        lambda raw, gain: prepare(raw, gain, angles), query_raw, query_gain
    )
    query_raw_grad, query_gain_grad = pull_query(query_grad * factor)
    unused_k, pull_key = jax.vjp(lambda raw, gain: prepare(raw, gain, angles), key_raw, key_gain)
    key_raw_grad, key_gain_grad = pull_key(key_grad * factor)
    qkv_grad = jnp.stack([query_raw_grad, key_raw_grad, value_grad], axis=2).astype(bf16)
    qkv_grad = qkv_grad.reshape(images, patches, 3 * width)
    normed_grad = product_right(qkv_grad, qkv_matrix)
    unused_one, pull_one = jax.vjp(prenorm, flow, shift_one, scale_one)
    extra_one, grad_shift_one, grad_scale_one = pull_one(normed_grad)
    flow_grad = middle_grad + extra_one
    mod_grad = jnp.concatenate(
        [
            grad_shift_one,
            grad_scale_one,
            grad_gate_one,
            grad_shift_two,
            grad_scale_two,
            grad_gate_two,
        ],
        axis=-1,
    )
    gains = jnp.stack([query_gain_grad, key_gain_grad])
    return flow_grad, mod_grad, gains, (mlp_grad, gate_up_grad, branch_grad, qkv_grad)


def per_device(
    tokens,
    cotangent,
    labels,
    timesteps,
    positions,
    label_table,
    ada_weight,
    qkv_weight,
    out_weight,
    gate_weight,
    up_weight,
    down_weight,
    q_gain,
    k_gain,
):
    first_section = lax.axis_index("section") == 0
    count = lax.axis_size("dp")
    me = lax.axis_index("dp")
    width = tokens.shape[2]
    rows = ada_weight.shape[1]
    classes = label_table.shape[0]

    ids = gather_small(jnp.stack([labels, timesteps]), count)
    all_labels = ids[:, 0].reshape(-1)
    all_times = ids[:, 1].reshape(-1)
    label_hot = all_labels[:, None] == jnp.arange(classes, dtype=jnp.int32)[None, :]
    condition = product(label_hot.astype(bf16), label_table) + time_features(all_times, width)
    sigma_cond = jax.nn.sigmoid(condition)
    silu_cond = (condition * sigma_cond).astype(bf16)
    silu_rows = lax.dynamic_slice_in_dim(silu_cond, me * rows, rows, 1)
    mod_part = product(silu_rows, ada_weight[0])
    modulation = scatter_small(mod_part.reshape(count, -1, mod_part.shape[1]), count)
    angles = rope_angles(positions)

    qkv_full = from_walk(gather_walk(qkv_weight[0], count), count)
    joined = jnp.concatenate([out_weight[0], gate_weight[0], up_weight[0]], axis=1)
    joined_full = from_walk(gather_walk(joined, count), count)
    down_full = from_walk(gather_walk(down_weight[0], count), count)
    weights = (
        qkv_full,
        joined_full[:, :width],
        joined_full[:, width:],
        down_full,
        q_gain[0],
        k_gain[0],
    )

    early, unused = layer_forward(tokens, modulation, angles, weights)
    received = lax.ppermute(early, "section", [(0, 1)])
    layer_in = jnp.where(first_section, tokens, received)
    result, kept = layer_forward(layer_in, modulation, angles, weights)

    grads = cotangent[0].astype(f32)
    late_grad = layer_backward(layer_in, modulation, angles, grads, weights, kept)[0]
    back = lax.ppermute(late_grad.astype(bf16), "section", [(1, 0)])
    flow_grad, mod_grad, gains, kept_grads = layer_backward(
        layer_in, modulation, angles, grads + back.astype(f32), weights, kept
    )
    input_grads = jnp.where(first_section, flow_grad, flow_grad.astype(bf16).astype(f32))
    mlp_grad, gate_up_grad, branch_grad, qkv_grad = kept_grads

    normed, attended, normed_two, activated = kept[0], kept[7], kept[10], kept[13]
    down_part = scatter_walk(to_walk(weight_grad(activated, mlp_grad).astype(bf16), count), count)
    gate_up_part = scatter_walk(
        to_walk(weight_grad(normed_two, gate_up_grad).astype(bf16), count), count
    )
    rest = jnp.concatenate(
        [
            weight_grad(attended, branch_grad).astype(bf16),
            weight_grad(normed, qkv_grad).astype(bf16),
        ],
        axis=1,
    )
    rest_part = scatter_walk(to_walk(rest, count), count)
    hidden_width = gate_up_part.shape[1] // 2

    mod_all = gather_small(mod_grad.astype(bf16), count).reshape(-1, mod_grad.shape[1])
    ada_part = lax.dot_general(
        silu_rows, mod_all, (((0,), (0,)), ((), ())), preferred_element_type=f32
    )
    silu_grad = product_right(mod_all, ada_weight[0])
    silu_grad = silu_grad + lax.ppermute(silu_grad, "section", [(0, 1), (1, 0)])
    silu_all = gather_small(silu_grad, count)
    gain_all = jnp.sum(gather_small(gains, count), axis=0)
    silu_all = jnp.swapaxes(silu_all, 0, 1).reshape(condition.shape)
    cond_grad = silu_all * sigma_cond * (1.0 + condition * (1.0 - sigma_cond))
    table_grad = lax.dot_general(
        label_hot.astype(f32),
        cond_grad,
        (((0,), (0,)), ((), ())),
        precision=lax.Precision.HIGHEST,
        preferred_element_type=f32,
    )
    return (
        result[None],
        input_grads[None],
        table_grad,
        ada_part[None],
        rest_part[None, :, width:].astype(f32),
        rest_part[None, :, :width].astype(f32),
        gate_up_part[None, :, :hidden_width].astype(f32),
        gate_up_part[None, :, hidden_width:].astype(f32),
        down_part[None].astype(f32),
        gain_all[None, 0],
        gain_all[None, 1],
    )


def solution(mesh):
    placed = (
        P("dp", None, None),
        P("section", "dp", None, None),
        P("dp"),
        P("dp"),
        P("dp", None),
        P(),
        P("section", "dp", None),
        P("section", "dp", None),
        P("section", "dp", None),
        P("section", "dp", None),
        P("section", "dp", None),
        P("section", "dp", None),
        P("section", None),
        P("section", None),
    )
    return jax.shard_map(
        per_device,
        mesh=mesh,
        in_specs=placed,
        out_specs=(
            P("section", "dp", None, None),
            P("section", "dp", None, None),
            P(),
            P("section", "dp", None),
            P("section", "dp", None),
            P("section", "dp", None),
            P("section", "dp", None),
            P("section", "dp", None),
            P("section", "dp", None),
            P("section", None),
            P("section", None),
        ),
        check_vma=False,
    )
```

```python
import math

import jax
import jax.numpy as jnp
from jax import lax
from jax.sharding import PartitionSpec as P

HD = 72
GRID = 16
epsilon = 1e-06
f32 = jnp.float32
bf16 = jnp.bfloat16


def product(left, right):
    return jnp.dot(left, right, preferred_element_type=f32)


def product_right(left, right):
    return lax.dot_general(
        left, right, (((left.ndim - 1,), (1,)), ((), ())), preferred_element_type=f32
    )


def weight_grad(inputs, grads):
    return lax.dot_general(
        inputs, grads, (((0, 1), (0, 1)), ((), ())), preferred_element_type=f32
    )


def walk_of(count):
    chips = count // 2
    order = [chip for chip in range(chips) if chip % 2 == 0]
    order += [chip for chip in reversed(range(chips)) if chip % 2 == 1]
    return [2 * chip + core for chip in order for core in (0, 1)]


def chip_place(chip, chips):
    return chip // 2 if chip % 2 == 0 else chips - 1 - chip // 2


def from_walk(rows, count):
    chips = count // 2
    blocks = rows.reshape(chips, -1, rows.shape[-1])
    picked = [blocks[chip_place(chip, chips)] for chip in range(chips)]
    return jnp.concatenate(picked, axis=0)


def to_walk(rows, count):
    chips = count // 2
    blocks = rows.reshape(chips, -1, rows.shape[-1])
    return jnp.concatenate([blocks[device // 2] for device in walk_of(count)[::2]], axis=0)


def gather_walk(rows, count):
    return lax.all_gather(rows, "dp", axis=0, tiled=True, axis_index_groups=[walk_of(count)])


def scatter_walk(rows, count):
    part = lax.psum_scatter(
        rows, "dp", scatter_dimension=0, tiled=True, axis_index_groups=[walk_of(count)]
    )
    return lax.optimization_barrier(part)


def swapped(block, bit, count):
    return lax.ppermute(block, "dp", [(device, device ^ bit) for device in range(count)])


def gather_small(block, count):
    me = lax.axis_index("dp")
    block = block[None]
    bit = 1
    while bit < count:
        other = swapped(block, bit, count)
        low = (me & bit) == 0
        block = jnp.concatenate(
            [jnp.where(low, block, other), jnp.where(low, other, block)], axis=0
        )
        bit *= 2
    return block


def scatter_small(blocks, count):
    me = lax.axis_index("dp")
    bit = 1
    while bit < count:
        pairs = blocks.reshape(blocks.shape[0] // 2, 2, *blocks.shape[1:])
        mine = jnp.where((me & bit) == 0, 0, 1)
        give = lax.dynamic_index_in_dim(pairs, 1 - mine, 1, keepdims=False)
        keep = lax.dynamic_index_in_dim(pairs, mine, 1, keepdims=False)
        blocks = keep + swapped(give, bit, count)
        bit *= 2
    return blocks[0]


def rms_norm(values):
    return values * lax.rsqrt(jnp.mean(values * values, axis=-1, keepdims=True) + epsilon)


def rope_angles(positions):
    quarter = HD // 4
    frequency = jnp.exp(-math.log(10000.0) * jnp.arange(quarter, dtype=f32) / quarter)
    row_pos = (positions // GRID).astype(f32)
    col_pos = (positions % GRID).astype(f32)
    return (row_pos[..., None] * frequency, col_pos[..., None] * frequency)


def rotate(tensor, row_rotation, column_rotation):
    first_a, first_b, second_a, second_b = jnp.split(tensor, 4, axis=-1)
    row_cos = jnp.cos(row_rotation)[:, :, None, :]
    row_sin = jnp.sin(row_rotation)[:, :, None, :]
    col_cos = jnp.cos(column_rotation)[:, :, None, :]
    col_sin = jnp.sin(column_rotation)[:, :, None, :]
    return jnp.concatenate(
        [
            first_a * row_cos - first_b * row_sin,
            first_a * row_sin + first_b * row_cos,
            second_a * col_cos - second_b * col_sin,
            second_a * col_sin + second_b * col_cos,
        ],
        axis=-1,
    )


def time_features(timestep_ids, width):
    half_width = width // 2
    frequency = jnp.exp(-math.log(10000.0) * jnp.arange(half_width, dtype=f32) / half_width)
    angle_rows = timestep_ids.astype(f32)[:, None] * frequency[None, :]
    return jnp.concatenate([jnp.cos(angle_rows), jnp.sin(angle_rows)], axis=-1)


def prenorm(residual_flow, shift, scale):
    return rms_norm(residual_flow) * (1.0 + scale[:, None, :]) + shift[:, None, :]


def prepare(raw_heads, gain, angles):
    return rotate(rms_norm(raw_heads) * gain, *angles)


def layer_forward(layer_in, modulation, angles, weights):
    qkv_matrix, out_matrix, gate_up_matrix, down_matrix, query_gain, key_gain = weights
    flow = layer_in.astype(f32)
    shift_one, scale_one, gate_one, shift_two, scale_two, gate_two = jnp.split(
        modulation, 6, axis=-1
    )
    normed = prenorm(flow, shift_one, scale_one).astype(bf16)
    projected = product(normed, qkv_matrix)
    images, patches, width = flow.shape
    head_size = query_gain.shape[0]
    split_heads = projected.reshape(images, patches, 3, width // head_size, head_size)
    query_raw = split_heads[:, :, 0]
    key_raw = split_heads[:, :, 1]
    queries = prepare(query_raw, query_gain, angles).astype(bf16)
    keys = prepare(key_raw, key_gain, angles).astype(bf16)
    values = split_heads[:, :, 2].astype(bf16)
    scores = jnp.einsum("blhd,bmhd->bhlm", queries, keys, preferred_element_type=f32)
    scores = scores * head_size ** (-0.5)
    highest = jnp.max(scores, axis=-1, keepdims=True)
    expon = jnp.exp(scores - highest)
    total = jnp.sum(expon, axis=-1, keepdims=True)
    probs = expon / total
    mixed = jnp.einsum("bhlm,bmhd->blhd", probs.astype(bf16), values, preferred_element_type=f32)
    attended = mixed.astype(bf16).reshape(images, patches, width)
    branch = product(attended, out_matrix)
    middle = flow + gate_one[:, None, :] * branch
    normed_two = prenorm(middle, shift_two, scale_two).astype(bf16)
    gate_up = product(normed_two, gate_up_matrix)
    hidden_width = gate_up.shape[-1] // 2
    gate_val, up_val = gate_up[..., :hidden_width], gate_up[..., hidden_width:]
    activated = (jax.nn.silu(gate_val) * up_val).astype(bf16)
    mlp_out = product(activated, down_matrix)
    result = (middle + gate_two[:, None, :] * mlp_out).astype(bf16)
    kept = (
        normed,
        query_raw,
        key_raw,
        queries,
        keys,
        values,
        highest + jnp.log(total),
        attended,
        branch,
        middle,
        normed_two,
        gate_val,
        up_val,
        activated,
        mlp_out,
    )
    return result, kept


def layer_backward(layer_in, modulation, angles, out_grad, weights, kept, with_weights):
    qkv_matrix, out_matrix, gate_up_matrix, down_matrix, query_gain, key_gain = weights
    (
        normed,
        query_raw,
        key_raw,
        queries,
        keys,
        values,
        log_total,
        attended,
        branch,
        middle,
        normed_two,
        gate_val,
        up_val,
        activated,
        mlp_out,
    ) = kept
    flow = layer_in.astype(f32)
    shift_one, scale_one, gate_one, shift_two, scale_two, gate_two = jnp.split(
        modulation, 6, axis=-1
    )
    images, patches, width = flow.shape
    head_size = query_gain.shape[0]
    heads = width // head_size
    factor = head_size ** (-0.5)
    grad_gate_two = jnp.sum(out_grad * mlp_out, axis=1)
    mlp_grad = (gate_two[:, None, :] * out_grad).astype(bf16)
    if with_weights:
        down_term = weight_grad(activated, mlp_grad).astype(bf16)
        down_term, mlp_grad = lax.optimization_barrier((down_term, mlp_grad))
    else:
        down_term = None
    act_grad = lax.optimization_barrier(product_right(mlp_grad, down_matrix))
    sigma = jax.nn.sigmoid(gate_val)
    gate_grad = (act_grad * up_val * sigma * (1.0 + gate_val * (1.0 - sigma))).astype(bf16)
    up_grad = (act_grad * gate_val * sigma).astype(bf16)
    gate_up_grad = jnp.concatenate([gate_grad, up_grad], axis=-1)
    normed_two_grad = product_right(gate_up_grad, gate_up_matrix)
    unused, pull_two = jax.vjp(prenorm, middle, shift_two, scale_two)
    extra_two, grad_shift_two, grad_scale_two = pull_two(normed_two_grad)
    middle_grad = out_grad + extra_two
    grad_gate_one = jnp.sum(middle_grad * branch, axis=1)
    branch_grad = (gate_one[:, None, :] * middle_grad).astype(bf16)
    mixed_grad = product_right(branch_grad, out_matrix).astype(bf16)
    mixed_grad = mixed_grad.reshape(images, patches, heads, head_size)
    scores = jnp.einsum("blhd,bmhd->bhlm", queries, keys, preferred_element_type=f32) * factor
    probs = jnp.exp(scores - log_total)
    value_grad = jnp.einsum(
        "bhlm,blhd->bmhd", probs.astype(bf16), mixed_grad, preferred_element_type=f32
    )
    prob_grad = jnp.einsum("blhd,bmhd->bhlm", mixed_grad, values, preferred_element_type=f32)
    score_grad = probs * (prob_grad - jnp.sum(probs * prob_grad, axis=-1, keepdims=True))
    score_grad = score_grad.astype(bf16)
    query_grad = jnp.einsum("bhlm,bmhd->blhd", score_grad, keys, preferred_element_type=f32)
    key_grad = jnp.einsum("bhlm,blhd->bmhd", score_grad, queries, preferred_element_type=f32)
    unused_q, pull_query = jax.vjp(
        lambda raw, gain: prepare(raw, gain, angles), query_raw, query_gain
    )
    query_raw_grad, query_gain_grad = pull_query(query_grad * factor)
    unused_k, pull_key = jax.vjp(lambda raw, gain: prepare(raw, gain, angles), key_raw, key_gain)
    key_raw_grad, key_gain_grad = pull_key(key_grad * factor)
    qkv_grad = jnp.stack([query_raw_grad, key_raw_grad, value_grad], axis=2).astype(bf16)
    qkv_grad = qkv_grad.reshape(images, patches, 3 * width)
    normed_grad = product_right(qkv_grad, qkv_matrix)
    unused_one, pull_one = jax.vjp(prenorm, flow, shift_one, scale_one)
    extra_one, grad_shift_one, grad_scale_one = pull_one(normed_grad)
    flow_grad = middle_grad + extra_one
    mod_grad = jnp.concatenate(
        [
            grad_shift_one,
            grad_scale_one,
            grad_gate_one,
            grad_shift_two,
            grad_scale_two,
            grad_gate_two,
        ],
        axis=-1,
    )
    gains = jnp.stack([query_gain_grad, key_gain_grad])
    return flow_grad, mod_grad, gains, (down_term, gate_up_grad, branch_grad, qkv_grad)


def per_device(
    tokens,
    cotangent,
    labels,
    timesteps,
    positions,
    label_table,
    ada_weight,
    qkv_weight,
    out_weight,
    gate_weight,
    up_weight,
    down_weight,
    q_gain,
    k_gain,
):
    first_section = lax.axis_index("section") == 0
    count = lax.axis_size("dp")
    me = lax.axis_index("dp")
    width = tokens.shape[2]
    rows = ada_weight.shape[1]
    classes = label_table.shape[0]

    ids = gather_small(jnp.stack([labels, timesteps]), count)
    all_labels = ids[:, 0].reshape(-1)
    all_times = ids[:, 1].reshape(-1)
    label_hot = all_labels[:, None] == jnp.arange(classes, dtype=jnp.int32)[None, :]
    condition = product(label_hot.astype(bf16), label_table) + time_features(all_times, width)
    sigma_cond = jax.nn.sigmoid(condition)
    silu_cond = (condition * sigma_cond).astype(bf16)
    silu_rows = lax.dynamic_slice_in_dim(silu_cond, me * rows, rows, 1)
    mod_part = product(silu_rows, ada_weight[0])
    modulation = scatter_small(mod_part.reshape(count, -1, mod_part.shape[1]), count)
    angles = rope_angles(positions)

    joined = jnp.concatenate(
        [qkv_weight[0], out_weight[0], gate_weight[0], up_weight[0]], axis=1
    )
    joined_full = gather_walk(joined, count)
    down_rows, joined_full = lax.optimization_barrier((down_weight[0], joined_full))
    joined_full = from_walk(joined_full, count)
    down_full = from_walk(gather_walk(down_rows, count), count)
    weights = (
        joined_full[:, : 3 * width],
        joined_full[:, 3 * width : 4 * width],
        joined_full[:, 4 * width :],
        down_full,
        q_gain[0],
        k_gain[0],
    )

    early, unused = layer_forward(tokens, modulation, angles, weights)
    received = lax.ppermute(early, "section", [(0, 1)])
    layer_in = jnp.where(first_section, tokens, received)
    result, kept = layer_forward(layer_in, modulation, angles, weights)

    grads = cotangent[0].astype(f32)
    late_grad = layer_backward(layer_in, modulation, angles, grads, weights, kept, False)[0]
    back = lax.ppermute(late_grad.astype(bf16), "section", [(1, 0)])
    flow_grad, mod_grad, gains, kept_grads = layer_backward(
        layer_in, modulation, angles, grads + back.astype(f32), weights, kept, True
    )
    input_grads = jnp.where(first_section, flow_grad, flow_grad.astype(bf16).astype(f32))
    down_term, gate_up_grad, branch_grad, qkv_grad = kept_grads

    normed, attended, normed_two = kept[0], kept[7], kept[10]
    down_part = scatter_walk(to_walk(down_term, count), count)
    gate_up_term = to_walk(weight_grad(normed_two, gate_up_grad).astype(bf16), count)
    gate_up_term, down_part = lax.optimization_barrier((gate_up_term, down_part))
    gate_up_part = scatter_walk(gate_up_term, count)
    rest = jnp.concatenate(
        [
            weight_grad(attended, branch_grad).astype(bf16),
            weight_grad(normed, qkv_grad).astype(bf16),
        ],
        axis=1,
    )
    rest, gate_up_part = lax.optimization_barrier((to_walk(rest, count), gate_up_part))
    rest_part = scatter_walk(rest, count)
    hidden_width = gate_up_part.shape[1] // 2

    mod_all = gather_small(mod_grad.astype(bf16), count).reshape(-1, mod_grad.shape[1])
    ada_part = lax.dot_general(
        silu_rows, mod_all, (((0,), (0,)), ((), ())), preferred_element_type=f32
    )
    silu_grad = product_right(mod_all, ada_weight[0])
    silu_grad = silu_grad + lax.ppermute(silu_grad, "section", [(0, 1), (1, 0)])
    silu_all = gather_small(silu_grad, count)
    gain_all = jnp.sum(gather_small(gains, count), axis=0)
    silu_all = jnp.swapaxes(silu_all, 0, 1).reshape(condition.shape)
    cond_grad = silu_all * sigma_cond * (1.0 + condition * (1.0 - sigma_cond))
    table_grad = lax.dot_general(
        label_hot.astype(f32),
        cond_grad,
        (((0,), (0,)), ((), ())),
        precision=lax.Precision.HIGHEST,
        preferred_element_type=f32,
    )
    return (
        result[None],
        input_grads[None],
        table_grad,
        ada_part[None],
        rest_part[None, :, width:].astype(f32),
        rest_part[None, :, :width].astype(f32),
        gate_up_part[None, :, :hidden_width].astype(f32),
        gate_up_part[None, :, hidden_width:].astype(f32),
        down_part[None].astype(f32),
        gain_all[None, 0],
        gain_all[None, 1],
    )


def solution(mesh):
    placed = (
        P("dp", None, None),
        P("section", "dp", None, None),
        P("dp"),
        P("dp"),
        P("dp", None),
        P(),
        P("section", "dp", None),
        P("section", "dp", None),
        P("section", "dp", None),
        P("section", "dp", None),
        P("section", "dp", None),
        P("section", "dp", None),
        P("section", None),
        P("section", None),
    )
    return jax.shard_map(
        per_device,
        mesh=mesh,
        in_specs=placed,
        out_specs=(
            P("section", "dp", None, None),
            P("section", "dp", None, None),
            P(),
            P("section", "dp", None),
            P("section", "dp", None),
            P("section", "dp", None),
            P("section", "dp", None),
            P("section", "dp", None),
            P("section", "dp", None),
            P("section", None),
            P("section", None),
        ),
        check_vma=False,
    )
```

```python
import functools
import math

import jax
import jax.numpy as jnp
from jax import lax
from jax.experimental import pallas as pl
from jax.experimental.pallas import tpu as pltpu
from jax.sharding import PartitionSpec as P

GRID = 16
epsilon = 1e-06
f32 = jnp.float32
bf16 = jnp.bfloat16
LANES = 128
VMEM_BYTES = 56 * 1024 * 1024


def params():
    return pltpu.CompilerParams(vmem_limit_bytes=VMEM_BYTES)


def cost(flops, moved):
    return pl.CostEstimate(flops=int(flops), bytes_accessed=int(moved), transcendentals=0)


def dot(left, right):
    return jnp.dot(left, right, preferred_element_type=f32)


def dot_right(left, right):
    return lax.dot_general(left, right, (((1,), (1,)), ((), ())), preferred_element_type=f32)


def dot_left(left, right):
    return lax.dot_general(left, right, (((0,), (0,)), ((), ())), preferred_element_type=f32)


def whole_rows(ref, places):
    if len(places) == 1:
        return ref[places[0]]
    return jnp.concatenate([ref[place] for place in places], axis=0)


def part_place(index, parts, walked):
    if not walked:
        return index
    return index // 2 + (index % 2) * (parts - 1 - 2 * (index // 2))


def places_of(parts, walked):
    return [part_place(index, parts, walked) for index in range(parts)]


def two_terms(left, right):
    high = left.astype(bf16)
    low = (left - high.astype(f32)).astype(bf16)
    return dot(high, right) + dot(low, right)


def inverse_rms(values):
    return lax.rsqrt(jnp.mean(values * values, axis=-1, keepdims=True) + epsilon)


def partner(values, first_half, quarter):
    width = values.shape[1]
    return jnp.where(
        first_half, pltpu.roll(values, width - quarter, 1), pltpu.roll(values, quarter, 1)
    )


def first_half_mask(shape, quarter):
    lane = lax.broadcasted_iota(jnp.int32, shape, 1)
    return lane % (2 * quarter) < quarter


def head_window(head, head_size, width):
    span = min(2 * LANES, width)
    start = min(head * head_size // LANES * LANES, width - span)
    return start, span


def head_mask(head, head_size, start, span):
    lane = lax.broadcasted_iota(jnp.int32, (1, span), 1) + start
    inside = jnp.logical_and(lane >= head * head_size, lane < (head + 1) * head_size)
    return inside.astype(f32).astype(bf16)


def attention_forward_kernel(
    heads,
    places,
    keep,
    received_ref,
    x_ref,
    mod_ref,
    cos_ref,
    sin_ref,
    gain_ref,
    sum_ref,
    spread_ref,
    joined_ref,
    *rest,
):
    if keep:
        normed_ref, raw_ref, value_ref, attended_ref, branch_ref, middle_ref, normed_two_ref = rest[:7]
        flow_ref = rest[7]
        rest = rest[8:]
    else:
        middle_ref, normed_two_ref = rest[:2]
        rest = rest[2:]
    weight, mixed, sems = rest
    width = x_ref.shape[1]
    head_size = width // heads
    quarter = head_size // 4

    def fetch(part):
        return pltpu.make_async_copy(
            joined_ref.at[:, :, pl.ds(part * width, width)], weight.at[part], sems.at[part]
        )

    @pl.when(pl.program_id(0) == 0)
    def _():
        for part in range(4):
            fetch(part).start()

    def arrived(part):
        @pl.when(pl.program_id(0) == 0)
        def _():
            fetch(part).wait()

    flow = x_ref[...].astype(f32)
    if keep:
        flow = flow + received_ref[...].astype(f32)
        flow_ref[...] = flow.astype(bf16)
    mod = mod_ref[0]
    normed = (flow * inverse_rms(flow) * (1.0 + mod[1:2]) + mod[0:1]).astype(bf16)
    if keep:
        normed_ref[...] = normed
    summing, spreading = sum_ref[...], spread_ref[...]
    first_half = first_half_mask((1, width), quarter)

    def prepared(part):
        arrived(part)
        raw = dot(normed, whole_rows(weight.at[part], places))
        if keep:
            raw_ref[:, part * width : (part + 1) * width] = raw
        scale = lax.rsqrt(two_terms(raw * raw, summing) * (1.0 / head_size) + epsilon)
        scaled = raw * two_terms(scale, spreading) * gain_ref[part : part + 1]
        turned = scaled * cos_ref[...] + partner(scaled, first_half, quarter) * sin_ref[...]
        return turned.astype(bf16)

    queries = prepared(0)
    keys = prepared(1)
    arrived(2)
    values = dot(normed, whole_rows(weight.at[2], places)).astype(bf16)
    if keep:
        value_ref[...] = values
    mixed[...] = jnp.zeros_like(mixed)
    factor = head_size ** (-0.5)
    for head in range(heads):
        start, span = head_window(head, head_size, width)
        mask = head_mask(head, head_size, start, span)
        window = slice(start, start + span)
        scores = dot_right(queries[:, window], keys[:, window] * mask)
        highest = jnp.max(scores, axis=-1, keepdims=True)
        expon = jnp.exp((scores - highest) * factor)
        probs = expon * (1.0 / jnp.sum(expon, axis=-1, keepdims=True))
        mixed[:, window] += dot(probs.astype(bf16), values[:, window] * mask)
    attended = mixed[...].astype(bf16)
    arrived(3)
    branch = dot(attended, whole_rows(weight.at[3], places))
    middle = flow + mod[2:3] * branch
    middle_ref[...] = middle
    normed_two_ref[...] = (middle * inverse_rms(middle) * (1.0 + mod[4:5]) + mod[3:4]).astype(bf16)
    if keep:
        attended_ref[...] = attended
        branch_ref[...] = branch


def attention_forward(x, received, mod, tables, gains, joined, walked, first, count, made=None):
    keep = received is not None
    cos, sin, summing, spreading = tables
    gain, head_size = gains
    images, unused, width = mod.shape
    tokens = x.shape[0]
    patches = tokens // images
    heads = width // head_size
    places = places_of(joined.shape[0], walked)
    row = lambda columns: pl.BlockSpec((patches, columns), lambda image: (first + image, 0))
    fixed = lambda array: pl.BlockSpec(array.shape, lambda image: (0,) * array.ndim)
    shapes = [(width, f32), (width, bf16)]
    if keep:
        shapes = [
            (width, bf16),
            (2 * width, f32),
            (width, bf16),
            (width, bf16),
            (width, f32),
            (width, f32),
            (width, bf16),
            (width, bf16),
        ]
    made = [] if made is None else list(made)
    extra = [received] if keep else []
    inputs = 8 + len(extra)

    def body(*refs):
        rest = refs[inputs + len(made) :]
        received_ref = refs[0] if keep else None
        attention_forward_kernel(
            heads, places, keep, received_ref, *refs[len(extra) : inputs], *rest
        )

    return pl.pallas_call(
        body,
        grid=(count,),
        in_specs=[pl.BlockSpec((patches, width), lambda image: (image, 0))] * len(extra)
        + [
            row(width),
            pl.BlockSpec((1, 6, width), lambda image: (first + image, 0, 0)),
            row(width),
            row(width),
            fixed(gain),
            fixed(summing),
            fixed(spreading),
            pl.BlockSpec(memory_space=pl.ANY),
        ]
        + [pl.BlockSpec(memory_space=pl.ANY)] * len(made),
        out_specs=[row(columns) for columns, kind in shapes],
        out_shape=[jax.ShapeDtypeStruct((tokens, columns), kind) for columns, kind in shapes],
        input_output_aliases={inputs + index: index for index in range(len(made))},
        scratch_shapes=[
            pltpu.VMEM((4, joined.shape[0], joined.shape[1], width), bf16),
            pltpu.VMEM((patches, width), f32),
            pltpu.SemaphoreType.DMA((4,)),
        ],
        compiler_params=params(),
        cost_estimate=cost(
            2 * count * patches * width * (4 * width + 2 * patches),
            8 * width * width + count * patches * width * 20,
        ),
    )(*extra, x, mod, cos, sin, gain, summing, spreading, joined, *made)


def gate_up_kernel(places, keep, normed_ref, gate_ref, up_ref, *outs):
    normed = normed_ref[...]
    gate = dot(normed, whole_rows(gate_ref, places))
    up = dot(normed, whole_rows(up_ref, places))
    outs[0][...] = (gate * (1.0 / (1.0 + jnp.exp(-gate))) * up).astype(bf16)
    if keep:
        outs[1][...] = gate.astype(bf16)
        outs[2][...] = up.astype(bf16)


def gate_up(normed_two, joined, hidden, walked, keep):
    tokens, width = normed_two.shape
    step = 512
    base = 4 * width // step
    count = hidden // step
    parts, rows, unused = joined.shape
    shapes = 3 if keep else 1
    return pl.pallas_call(
        functools.partial(gate_up_kernel, places_of(parts, walked), keep),
        grid=(count,),
        in_specs=[
            pl.BlockSpec((tokens, width), lambda i: (0, 0)),
            pl.BlockSpec((parts, rows, step), lambda i: (0, 0, base + i)),
            pl.BlockSpec((parts, rows, step), lambda i: (0, 0, base + count + i)),
        ],
        out_specs=[pl.BlockSpec((tokens, step), lambda i: (0, i))] * shapes,
        out_shape=[jax.ShapeDtypeStruct((tokens, hidden), bf16)] * shapes,
        compiler_params=params(),
        cost_estimate=cost(4 * tokens * width * hidden, 4 * width * hidden + 2 * shapes * tokens * hidden),
    )(normed_two, joined, joined)


def parts_per_step(rows):
    return max(1, 768 // rows)


def part_specs(down, walked):
    parts, rows, width = down.shape
    each = parts_per_step(rows)

    def spec(which):
        return pl.BlockSpec(
            (1, rows, width), lambda i: (part_place(i * each + which, parts, walked), 0, 0)
        )

    return [spec(which) for which in range(each)]


def joined_parts(refs):
    if len(refs) == 1:
        return refs[0][0]
    return jnp.concatenate([ref[0] for ref in refs], axis=0)


def down_projection(act, down, middle, mod, walked, first, count, keep):
    hidden = act.shape[1]
    images, unused, width = mod.shape
    patches = act.shape[0] // images
    tokens = count * patches
    specs = part_specs(down, walked)
    each, rows = len(specs), down.shape[1]
    outs = [jax.ShapeDtypeStruct((tokens, width), bf16)]
    scratch = [pltpu.VMEM((tokens, width), f32)]
    if keep:
        outs.append(jax.ShapeDtypeStruct((tokens, width), f32))
        scratch = []

    def body(act_ref, middle_ref, mod_ref, *refs):
        step = pl.program_id(0)
        total = refs[each + 1]
        term = dot(act_ref[...], joined_parts(refs[:each]))

        @pl.when(step == 0)
        def _():
            total[...] = term

        @pl.when(step > 0)
        def _():
            total[...] += term

        @pl.when(step == pl.num_programs(0) - 1)
        def _():
            for image in range(count):
                at = slice(image * patches, (image + 1) * patches)
                gate = mod_ref[first + image, 5:6]
                refs[each][at] = (middle_ref[at] + gate * total[at]).astype(bf16)

    return pl.pallas_call(
        body,
        grid=(hidden // (each * rows),),
        in_specs=[
            pl.BlockSpec((tokens, each * rows), lambda i: (first // count, i)),
            pl.BlockSpec((tokens, width), lambda i: (first // count, 0)),
            pl.BlockSpec(mod.shape, lambda i: (0, 0, 0)),
        ]
        + specs,
        out_specs=[pl.BlockSpec((tokens, width), lambda i: (0, 0))] * len(outs),
        out_shape=outs,
        scratch_shapes=scratch,
        compiler_params=params(),
        cost_estimate=cost(2 * tokens * width * hidden, 2 * width * hidden + 8 * tokens * width),
    )(act, middle, mod, *[down] * each)


def incoming(cot_ref, back_refs, image, at):
    value = cot_ref[at].astype(f32)
    return value + back_refs[image][...].astype(f32) if back_refs else value


def mlp_gradient(cot, backs, mod, first, count):
    images, unused, width = mod.shape
    patches = cot.shape[0] // images

    def body(cot_ref, mod_ref, *refs):
        for image in range(count):
            at = slice(image * patches, (image + 1) * patches)
            grads = incoming(cot_ref, refs[: len(backs)], image, at)
            refs[-1][at] = (mod_ref[first + image, 5:6] * grads).astype(bf16)

    return pl.pallas_call(
        body,
        grid=(1,),
        in_specs=[
            pl.BlockSpec((count * patches, width), lambda i: (first // count, 0)),
            pl.BlockSpec(mod.shape, lambda i: (0, 0, 0)),
        ]
        + [pl.BlockSpec((patches, width), lambda i: (0, 0))] * len(backs),
        out_specs=pl.BlockSpec((count * patches, width), lambda i: (0, 0)),
        out_shape=jax.ShapeDtypeStruct((count * patches, width), bf16),
        compiler_params=params(),
        cost_estimate=cost(0, 6 * count * patches * width),
    )(cot, mod, *backs)


def stacked(refs):
    return refs[0][...] if len(refs) == 1 else jnp.concatenate([ref[...] for ref in refs], axis=0)


def whole_specs(arrays):
    return [pl.BlockSpec(array.shape, lambda i: (0, 0)) for array in arrays]


def act_backward(mlp_grads, down, hidden, walked):
    width = mlp_grads[0].shape[1]
    tokens = sum(grad.shape[0] for grad in mlp_grads)
    specs = part_specs(down, walked)
    each, rows = len(specs), down.shape[1]

    def body(*refs):
        grads, refs = refs[: len(mlp_grads)], refs[len(mlp_grads) :]
        refs[each][...] = dot_right(stacked(grads), joined_parts(refs[:each])).astype(bf16)

    return pl.pallas_call(
        body,
        grid=(hidden // (each * rows),),
        in_specs=whole_specs(mlp_grads) + specs,
        out_specs=pl.BlockSpec((tokens, each * rows), lambda i: (0, i)),
        out_shape=jax.ShapeDtypeStruct((tokens, hidden), bf16),
        compiler_params=params(),
        cost_estimate=cost(2 * tokens * width * hidden, 2 * width * hidden + 4 * tokens * width),
    )(*mlp_grads, *[down] * each)


def mlp_backward(cot, backs, mlp, act_grad, gate, up, joined, middle, branch, mod, walked, keep):
    tokens, hidden = gate.shape
    images, unused, width = mod.shape
    patches = tokens // images
    parts, rows, unused = joined.shape
    places = places_of(parts, walked)
    step = 512
    base = 4 * width // step
    count = hidden // step
    whole = pl.BlockSpec((tokens, width), lambda i: (0, 0))
    block = pl.BlockSpec((tokens, step), lambda i: (0, i))
    kept = [mlp, branch] if keep else []

    def body(cot_ref, act_grad_ref, gate_ref, up_ref, gate_weight, up_weight, middle_ref, mod_ref, joined_ref, *refs):
        back_refs, refs = refs[: len(backs)], refs[len(backs) :]
        if keep:
            mlp_ref, branch_ref = refs[:2]
            refs = refs[2:]
        middle_grad_ref, mixed_grad_ref = refs[:2]
        refs = refs[2:]
        if keep:
            gate_grad_ref, up_grad_ref, branch_grad_ref, sums_ref = refs[:4]
            refs = refs[4:]
        total, out_weight, sem = refs
        index = pl.program_id(0)
        fetch = pltpu.make_async_copy(joined_ref.at[:, :, pl.ds(3 * width, width)], out_weight, sem)

        @pl.when(index == 0)
        def _():
            fetch.start()

        gate_val, up_val = gate_ref[...].astype(f32), up_ref[...].astype(f32)
        sigma = 1.0 / (1.0 + jnp.exp(-gate_val))
        slope = act_grad_ref[...].astype(f32) * sigma
        gate_grad = (slope * up_val * (1.0 + gate_val * (1.0 - sigma))).astype(bf16)
        up_grad = (slope * gate_val).astype(bf16)
        if keep:
            gate_grad_ref[...] = gate_grad
            up_grad_ref[...] = up_grad
        term = dot_right(gate_grad, whole_rows(gate_weight, places))
        term = term + dot_right(up_grad, whole_rows(up_weight, places))

        @pl.when(index == 0)
        def _():
            total[...] = term

        @pl.when(index > 0)
        def _():
            total[...] += term

        @pl.when(index == count - 1)
        def _():
            fetch.wait()
            matrix = whole_rows(out_weight, places)
            for image in range(images):
                at = slice(image * patches, (image + 1) * patches)
                mod = mod_ref[image]
                grad, flow = total[at], middle_ref[at]
                inverse = inverse_rms(flow)
                normal = flow * inverse
                scaled = grad * (1.0 + mod[4:5])
                mean = jnp.mean(scaled * normal, axis=-1, keepdims=True)
                out_grad = incoming(cot_ref, back_refs, image, at)
                middle_grad = out_grad + (scaled - normal * mean) * inverse
                middle_grad_ref[at] = middle_grad
                branch_grad = (mod[2:3] * middle_grad).astype(bf16)
                mixed_grad_ref[at] = dot_right(branch_grad, matrix).astype(bf16)
                if keep:
                    branch_grad_ref[at] = branch_grad
                    terms = [middle_grad * branch_ref[at], grad, grad * normal, out_grad * mlp_ref[at]]
                    for place, value in enumerate(terms):
                        sums_ref[image, place : place + 1] = jnp.sum(value, axis=0, keepdims=True)

    out_shapes = [
        jax.ShapeDtypeStruct((tokens, width), f32),
        jax.ShapeDtypeStruct((tokens, width), bf16),
    ]
    out_specs = [whole, whole]
    if keep:
        out_shapes += [jax.ShapeDtypeStruct((tokens, hidden), bf16)] * 2
        out_shapes += [jax.ShapeDtypeStruct((tokens, width), bf16)]
        out_shapes += [jax.ShapeDtypeStruct((images, 4, width), f32)]
        out_specs += [block, block, whole, pl.BlockSpec((images, 4, width), lambda i: (0, 0, 0))]
    return pl.pallas_call(
        body,
        grid=(count,),
        in_specs=[
            whole,
            block,
            block,
            block,
            pl.BlockSpec((parts, rows, step), lambda i: (0, 0, base + i)),
            pl.BlockSpec((parts, rows, step), lambda i: (0, 0, base + count + i)),
            whole,
            pl.BlockSpec(mod.shape, lambda i: (0, 0, 0)),
            pl.BlockSpec(memory_space=pl.ANY),
        ]
        + [pl.BlockSpec((patches, width), lambda i: (0, 0))] * len(backs)
        + [whole] * len(kept),
        out_specs=out_specs,
        out_shape=out_shapes,
        scratch_shapes=[
            pltpu.VMEM((tokens, width), f32),
            pltpu.VMEM((parts, rows, width), bf16),
            pltpu.SemaphoreType.DMA,
        ],
        compiler_params=params(),
        cost_estimate=cost(
            2 * tokens * width * (2 * hidden + width), 4 * width * hidden + 6 * tokens * hidden
        ),
    )(cot, act_grad, gate, up, joined, joined, middle, mod, joined, *backs, *kept)


def attention_backward_kernel(
    heads,
    places,
    keep,
    raw_ref,
    value_ref,
    mixed_grad_ref,
    middle_grad_ref,
    x_ref,
    mod_ref,
    cos_ref,
    sin_ref,
    gain_ref,
    sum_ref,
    spread_ref,
    joined_ref,
    *rest,
):
    if keep:
        flow_grad_ref, qkv_grad_ref, sums_ref = rest[:3]
        rest = rest[3:]
    else:
        back_ref = rest[0]
        rest = rest[1:]
    weight, query_total, key_total, value_total, sems = rest
    width = x_ref.shape[1]
    head_size = width // heads
    quarter = head_size // 4
    factor = head_size ** (-0.5)

    def fetch(part):
        return pltpu.make_async_copy(
            joined_ref.at[:, :, pl.ds(part * width, width)], weight.at[part], sems.at[part]
        )

    @pl.when(pl.program_id(0) == 0)
    def _():
        for part in range(3):
            fetch(part).start()

    summing, spreading = sum_ref[...], spread_ref[...]
    first_half = first_half_mask((1, width), quarter)

    def prepared(part):
        raw = raw_ref[:, part * width : (part + 1) * width]
        scale = lax.rsqrt(two_terms(raw * raw, summing) * (1.0 / head_size) + epsilon)
        scaled = raw * two_terms(scale, spreading) * gain_ref[part : part + 1]
        turned = scaled * cos_ref[...] + partner(scaled, first_half, quarter) * sin_ref[...]
        return turned.astype(bf16)

    queries, keys, values = prepared(0), prepared(1), value_ref[...]
    mixed_grad = mixed_grad_ref[...]
    query_total[...] = jnp.zeros_like(query_total)
    key_total[...] = jnp.zeros_like(key_total)
    value_total[...] = jnp.zeros_like(value_total)
    for head in range(heads):
        start, span = head_window(head, head_size, width)
        mask = head_mask(head, head_size, start, span)
        window = slice(start, start + span)
        key_part, query_part = keys[:, window] * mask, queries[:, window] * mask
        grad_part = mixed_grad[:, window] * mask
        scores = dot_right(key_part, queries[:, window])
        highest = jnp.max(scores, axis=0, keepdims=True)
        expon = jnp.exp((scores - highest) * factor)
        probs = expon * (1.0 / jnp.sum(expon, axis=0, keepdims=True))
        value_total[:, window] += dot(probs.astype(bf16), grad_part)
        probs_grad = dot_right(values[:, window], grad_part)
        middle = jnp.sum(probs * probs_grad, axis=0, keepdims=True)
        scores_grad = (probs * (probs_grad - middle)).astype(bf16)
        key_total[:, window] += dot(scores_grad, query_part)
        query_total[:, window] += dot_left(scores_grad, key_part)

    def raw_grad(part, total):
        turned = total[...] * factor
        weighted = turned * sin_ref[...]
        grad = turned * cos_ref[...] + partner(weighted, first_half, quarter)
        raw = raw_ref[:, part * width : (part + 1) * width]
        scale = lax.rsqrt(two_terms(raw * raw, summing) * (1.0 / head_size) + epsilon)
        scale = two_terms(scale, spreading)
        normal = raw * scale
        if keep:
            sums_ref[0, 2 + part : 3 + part] = jnp.sum(grad * normal, axis=0, keepdims=True)
        grad = grad * gain_ref[part : part + 1]
        mean = two_terms(two_terms(grad * normal, summing) * (1.0 / head_size), spreading)
        return (scale * (grad - normal * mean)).astype(bf16)

    def arrived(part):
        @pl.when(pl.program_id(0) == 0)
        def _():
            fetch(part).wait()

    parts = [raw_grad(0, query_total), raw_grad(1, key_total), value_total[...].astype(bf16)]
    grad = None
    for part in range(3):
        arrived(part)
        if keep:
            qkv_grad_ref[:, part * width : (part + 1) * width] = parts[part]
        term = dot_right(parts[part], whole_rows(weight.at[part], places))
        grad = term if grad is None else grad + term
    mod = mod_ref[0]
    flow = x_ref[...].astype(f32)
    inverse = inverse_rms(flow)
    normal = flow * inverse
    scaled = grad * (1.0 + mod[1:2])
    mean = jnp.mean(scaled * normal, axis=-1, keepdims=True)
    flow_grad = middle_grad_ref[...] + (scaled - normal * mean) * inverse
    if keep:
        flow_grad_ref[...] = flow_grad
        sums_ref[0, 0:1] = jnp.sum(grad, axis=0, keepdims=True)
        sums_ref[0, 1:2] = jnp.sum(grad * normal, axis=0, keepdims=True)
    else:
        back_ref[...] = flow_grad.astype(bf16)


def attention_backward(
    raw, value, mixed_grad, middle_grad, x, mod, tables, gains, joined, walked, first, count, keep
):
    cos, sin, summing, spreading = tables
    gain, head_size = gains
    images, unused, width = mod.shape
    patches = x.shape[0] // images
    tokens = count * patches
    heads = width // head_size
    parts, rows, unused = joined.shape
    row = lambda columns: pl.BlockSpec((patches, columns), lambda image: (first + image, 0))
    token = lambda columns: pl.BlockSpec((patches, columns), lambda image: (image, 0))
    fixed = lambda array: pl.BlockSpec(array.shape, lambda image: (0,) * array.ndim)
    out_shapes = [jax.ShapeDtypeStruct((tokens, width), bf16)]
    out_specs = [token(width)]
    if keep:
        out_shapes = [
            jax.ShapeDtypeStruct((tokens, width), f32),
            jax.ShapeDtypeStruct((tokens, 3 * width), bf16),
            jax.ShapeDtypeStruct((count, 4, width), f32),
        ]
        out_specs = [
            token(width),
            token(3 * width),
            pl.BlockSpec((1, 4, width), lambda image: (image, 0, 0)),
        ]
    return pl.pallas_call(
        functools.partial(attention_backward_kernel, heads, places_of(parts, walked), keep),
        grid=(count,),
        in_specs=[
            row(2 * width),
            row(width),
            row(width),
            row(width),
            row(width),
            pl.BlockSpec((1, 6, width), lambda image: (first + image, 0, 0)),
            row(width),
            row(width),
            fixed(gain),
            fixed(summing),
            fixed(spreading),
            pl.BlockSpec(memory_space=pl.ANY),
        ],
        out_specs=out_specs,
        out_shape=out_shapes,
        scratch_shapes=[
            pltpu.VMEM((3, parts, rows, width), bf16),
            pltpu.VMEM((patches, width), f32),
            pltpu.VMEM((patches, width), f32),
            pltpu.VMEM((patches, width), f32),
            pltpu.SemaphoreType.DMA((3,)),
        ],
        compiler_params=params(),
        cost_estimate=cost(
            2 * tokens * width * (3 * width + 5 * patches),
            6 * width * width + tokens * width * 20,
        ),
    )(raw, value, mixed_grad, middle_grad, x, mod, cos, sin, gain, summing, spreading, joined)


def down_grad(mlp_grads, act, parts, walked):
    tokens, hidden = act.shape
    width = mlp_grads[0].shape[1]
    step = hidden // parts

    def body(act_ref, *refs):
        refs[-1][0] = dot_left(act_ref[...], stacked(refs[:-1])).astype(bf16)

    return pl.pallas_call(
        body,
        grid=(parts,),
        in_specs=[pl.BlockSpec((tokens, step), lambda i: (0, i))] + whole_specs(mlp_grads),
        out_specs=pl.BlockSpec((1, step, width), lambda i: (part_place(i, parts, walked), 0, 0)),
        out_shape=jax.ShapeDtypeStruct((parts, step, width), bf16),
        compiler_params=params(),
        cost_estimate=cost(2 * tokens * width * hidden, 2 * width * hidden),
    )(act, *mlp_grads)


def matrix_grad_kernel(places, counts, *refs):
    pairs = len(counts)
    inputs, grads, out_ref = refs[:pairs], refs[pairs : 2 * pairs], refs[2 * pairs]
    rows = out_ref.shape[1]
    step = pl.program_id(0)
    first = 0
    for index in range(pairs):

        @pl.when(jnp.logical_and(step >= first, step < first + counts[index]))
        def _(index=index):
            product = dot_left(inputs[index][...], grads[index][...]).astype(bf16)
            for part, place in enumerate(places):
                out_ref[place] = product[part * rows : (part + 1) * rows]

        first += counts[index]


def matrix_grad(inputs, grads, step, parts, walked):
    tokens, width = inputs[0].shape
    counts = [grad.shape[1] // step for grad in grads]
    columns = sum(counts) * step
    rows = width // parts
    firsts = [sum(counts[:index]) for index in range(len(counts))]

    def grad_spec(first, count):
        return pl.BlockSpec((tokens, step), lambda i: (0, jnp.clip(i - first, 0, count - 1)))

    return pl.pallas_call(
        functools.partial(matrix_grad_kernel, places_of(parts, walked), counts),
        grid=(sum(counts),),
        in_specs=[pl.BlockSpec((tokens, width), lambda i: (0, 0))] * len(inputs)
        + [grad_spec(first, count) for first, count in zip(firsts, counts)],
        out_specs=pl.BlockSpec((parts, rows, step), lambda i: (0, 0, i)),
        out_shape=jax.ShapeDtypeStruct((parts, rows, columns), bf16),
        compiler_params=params(),
        cost_estimate=cost(2 * tokens * width * columns, 2 * width * columns),
    )(*inputs, *grads)


def walk_of(count):
    chips = count // 2
    order = [chip for chip in range(chips) if chip % 2 == 0]
    order += [chip for chip in reversed(range(chips)) if chip % 2 == 1]
    return [2 * chip + core for chip in order for core in (0, 1)]


def from_walk(rows, count):
    blocks = rows.reshape(count // 2, -1, rows.shape[-1])
    places = places_of(count // 2, True)
    return jnp.concatenate([blocks[place] for place in places], axis=0)


def to_walk(rows, count):
    blocks = rows.reshape(count // 2, -1, rows.shape[-1])
    return jnp.concatenate([blocks[device // 2] for device in walk_of(count)[::2]], axis=0)


def gather_walk(rows, count):
    return lax.all_gather(rows, "dp", axis=0, tiled=True, axis_index_groups=[walk_of(count)])


def scatter_walk(rows, count):
    part = lax.psum_scatter(
        rows, "dp", scatter_dimension=0, tiled=True, axis_index_groups=[walk_of(count)]
    )
    return lax.optimization_barrier(part)


def as_parts(rows, count, unit):
    each = rows.shape[0] // (count // 2)
    if each % unit == 0:
        return rows.reshape(count // 2, each, rows.shape[1]), True
    whole = from_walk(rows, count)
    return whole[None], False


def swapped(block, bit, count):
    return lax.ppermute(block, "dp", [(device, device ^ bit) for device in range(count)])


def gather_small(block, count):
    me = lax.axis_index("dp")
    block = block[None]
    bit = 1
    while bit < count:
        other = swapped(block, bit, count)
        low = (me & bit) == 0
        block = jnp.concatenate(
            [jnp.where(low, block, other), jnp.where(low, other, block)], axis=0
        )
        bit *= 2
    return block


def scatter_small(blocks, count):
    me = lax.axis_index("dp")
    bit = 1
    while bit < count:
        pairs = blocks.reshape(blocks.shape[0] // 2, 2, *blocks.shape[1:])
        mine = jnp.where((me & bit) == 0, 0, 1)
        give = lax.dynamic_index_in_dim(pairs, 1 - mine, 1, keepdims=False)
        keep = lax.dynamic_index_in_dim(pairs, mine, 1, keepdims=False)
        blocks = keep + swapped(give, bit, count)
        bit *= 2
    return blocks[0]


def time_features(timestep_ids, width):
    half_width = width // 2
    frequency = jnp.exp(-math.log(10000.0) * jnp.arange(half_width, dtype=f32) / half_width)
    angle_rows = timestep_ids.astype(f32)[:, None] * frequency[None, :]
    return jnp.concatenate([jnp.cos(angle_rows), jnp.sin(angle_rows)], axis=-1)


def rotation_tables(positions, width, head_size):
    heads = width // head_size
    quarter = head_size // 4
    frequency = jnp.exp(-math.log(10000.0) * jnp.arange(quarter, dtype=f32) / quarter)
    places = positions.reshape(-1, 1)
    row_angle = (places // GRID).astype(f32) * frequency
    col_angle = (places % GRID).astype(f32) * frequency
    row_cos, row_sin = jnp.cos(row_angle), jnp.sin(row_angle)
    col_cos, col_sin = jnp.cos(col_angle), jnp.sin(col_angle)
    cos = jnp.concatenate([row_cos, row_cos, col_cos, col_cos], axis=1)
    sin = jnp.concatenate([-row_sin, row_sin, -col_sin, col_sin], axis=1)
    head = jnp.arange(width) // head_size
    summing = (head[:, None] == jnp.arange(LANES)[None, :]).astype(bf16)
    return jnp.tile(cos, (1, heads)), jnp.tile(sin, (1, heads)), summing, summing.T


def per_device(
    tokens,
    cotangent,
    labels,
    timesteps,
    positions,
    label_table,
    ada_weight,
    qkv_weight,
    out_weight,
    gate_weight,
    up_weight,
    down_weight,
    q_gain,
    k_gain,
):
    first_section = lax.axis_index("section") == 0
    count = lax.axis_size("dp")
    me = lax.axis_index("dp")
    images, patches, width = tokens.shape
    hidden = gate_weight.shape[2]
    head_size = q_gain.shape[1]
    heads = width // head_size
    rows = ada_weight.shape[1]
    classes = label_table.shape[0]

    joined = gather_walk(
        jnp.concatenate([qkv_weight[0], out_weight[0], gate_weight[0], up_weight[0]], axis=1),
        count,
    )

    ids = gather_small(jnp.stack([labels, timesteps]), count)
    all_labels = ids[:, 0].reshape(-1)
    all_times = ids[:, 1].reshape(-1)
    label_hot = all_labels[:, None] == jnp.arange(classes, dtype=jnp.int32)[None, :]
    condition = dot(label_hot.astype(bf16), label_table) + time_features(all_times, width)
    sigma_cond = jax.nn.sigmoid(condition)
    silu_cond = (condition * sigma_cond).astype(bf16)
    silu_rows = lax.dynamic_slice_in_dim(silu_cond, me * rows, rows, 1)
    mod_part = dot(silu_rows, ada_weight[0])
    mod = scatter_small(mod_part.reshape(count, images, -1), count).reshape(images, 6, width)
    tables = rotation_tables(positions, width, head_size)
    flat = tokens.reshape(images * patches, width)
    own = jnp.where(first_section, flat, jnp.zeros_like(flat))

    down, joined, mod, own, tables = lax.optimization_barrier(
        (down_weight[0], joined, mod, own, tables)
    )
    down = gather_walk(down, count)
    joined, walked = as_parts(joined, count, 16)
    down, down_walked = as_parts(down, count, LANES)
    if not down_walked:
        down = down.reshape(hidden // 384, 384, width)
    gains = (jnp.tile(jnp.concatenate([q_gain, k_gain]), (1, heads)), head_size)

    cot = cotangent[0].reshape(images * patches, width)
    middle, normed_two = attention_forward(
        flat, None, mod, tables, gains, joined, walked, 0, images
    )
    (act,) = gate_up(normed_two, joined, hidden, walked, False)
    received = []
    for image in range(images):
        (early,) = down_projection(act, down, middle, mod, down_walked, image, 1, False)
        received.append(lax.ppermute(early, "section", [(0, 1)]))
    late_cot, unused = lax.optimization_barrier((cot, early))
    mlp_grads = [mlp_gradient(late_cot, [], mod, 0, images)]
    act_grad = act_backward(mlp_grads, down, hidden, down_walked)
    kept = None
    for image in range(images):
        kept = attention_forward(
            own, received[image], mod, tables, gains, joined, walked, image, 1, kept
        )
    normed, raw, values, attended, branch, middle, normed_two, layer_in = kept
    act, gate, up = gate_up(normed_two, joined, hidden, walked, True)

    middle_grad, mixed_grad = mlp_backward(
        cot, [], None, act_grad, gate, up, joined, middle, None, mod, walked, False
    )
    backs = []
    for image in range(images):
        (early,) = attention_backward(
            raw,
            values,
            mixed_grad,
            middle_grad,
            layer_in,
            mod,
            tables,
            gains,
            joined,
            walked,
            image,
            1,
            False,
        )
        backs.append(lax.ppermute(early, "section", [(1, 0)]))
    late_act, unused = lax.optimization_barrier((act, early))
    result, mlp = down_projection(late_act, down, middle, mod, down_walked, 0, images, True)

    late_cot, unused = lax.optimization_barrier((cot, mlp))
    mlp_grads = [
        mlp_gradient(late_cot, [back], mod, image, 1) for image, back in enumerate(backs)
    ]
    down_term = down_grad(mlp_grads, act, down.shape[0], down_walked)
    down_term, mlp_grads = lax.optimization_barrier((down_term, mlp_grads))
    down_term = down_term.reshape(hidden, width)
    down_part = scatter_walk(down_term if down_walked else to_walk(down_term, count), count)
    act_grad = act_backward(mlp_grads, down, hidden, down_walked)
    middle_grad, mixed_grad, gate_grad, up_grad, branch_grad, mlp_sums = mlp_backward(
        cot, backs, mlp, act_grad, gate, up, joined, middle, branch, mod, walked, True
    )

    def matrix_part(inputs, grads, step, before):
        term = matrix_grad(inputs, grads, step, joined.shape[0], walked).reshape(width, -1)
        term = term if walked else to_walk(term, count)
        term, before = lax.optimization_barrier((term, before))
        return scatter_walk(term, count), before

    gate_up_part, down_part = matrix_part(
        [normed_two, normed_two], [gate_grad, up_grad], hidden // 2, down_part
    )
    flow_grad, qkv_grad, attention_sums = attention_backward(
        raw,
        values,
        mixed_grad,
        middle_grad,
        layer_in,
        mod,
        tables,
        gains,
        joined,
        walked,
        0,
        images,
        True,
    )
    rest_part, gate_up_part = matrix_part(
        [normed, attended], [qkv_grad, branch_grad], width, gate_up_part
    )
    flow_grad = flow_grad.reshape(images, patches, width)
    input_grads = jnp.where(first_section, flow_grad, flow_grad.astype(bf16).astype(f32))

    mod_grad = jnp.concatenate([attention_sums[:, :2], mlp_sums], axis=1).reshape(images, -1)
    head_sums = jnp.sum(attention_sums[:, 2:], axis=0).reshape(2, heads, head_size)
    mod_all = gather_small(mod_grad.astype(bf16), count).reshape(-1, mod_grad.shape[1])
    ada_part = dot_left(silu_rows, mod_all)
    silu_grad = dot_right(mod_all, ada_weight[0])
    silu_grad = silu_grad + lax.ppermute(silu_grad, "section", [(0, 1), (1, 0)])
    silu_all = gather_small(silu_grad, count)
    gain_all = jnp.sum(gather_small(jnp.sum(head_sums, axis=1), count), axis=0)
    silu_all = jnp.swapaxes(silu_all, 0, 1).reshape(condition.shape)
    cond_grad = silu_all * sigma_cond * (1.0 + condition * (1.0 - sigma_cond))
    table_grad = lax.dot_general(
        label_hot.astype(f32),
        cond_grad,
        (((0,), (0,)), ((), ())),
        precision=lax.Precision.HIGHEST,
        preferred_element_type=f32,
    )
    return (
        result.reshape(1, images, patches, width),
        input_grads[None],
        table_grad,
        ada_part[None],
        rest_part[None, :, : 3 * width].astype(f32),
        rest_part[None, :, 3 * width :].astype(f32),
        gate_up_part[None, :, :hidden].astype(f32),
        gate_up_part[None, :, hidden:].astype(f32),
        down_part[None].astype(f32),
        gain_all[None, 0],
        gain_all[None, 1],
    )


def solution(mesh):
    placed = (
        P("dp", None, None),
        P("section", "dp", None, None),
        P("dp"),
        P("dp"),
        P("dp", None),
        P(),
        P("section", "dp", None),
        P("section", "dp", None),
        P("section", "dp", None),
        P("section", "dp", None),
        P("section", "dp", None),
        P("section", "dp", None),
        P("section", None),
        P("section", None),
    )
    return jax.shard_map(
        per_device,
        mesh=mesh,
        in_specs=placed,
        out_specs=(
            P("section", "dp", None, None),
            P("section", "dp", None, None),
            P(),
            P("section", "dp", None),
            P("section", "dp", None),
            P("section", "dp", None),
            P("section", "dp", None),
            P("section", "dp", None),
            P("section", "dp", None),
            P("section", None),
            P("section", None),
        ),
        check_vma=False,
    )
```

```python
import functools
import math

import jax
import jax.numpy as jnp
from jax import lax
from jax.experimental import pallas as pl
from jax.experimental.pallas import tpu as pltpu
from jax.sharding import PartitionSpec as P

GRID = 16
epsilon = 1e-06
f32 = jnp.float32
bf16 = jnp.bfloat16
LANES = 128
VMEM_BYTES = 56 * 1024 * 1024


def params():
    return pltpu.CompilerParams(vmem_limit_bytes=VMEM_BYTES)


def cost(flops, moved):
    return pl.CostEstimate(flops=int(flops), bytes_accessed=int(moved), transcendentals=0)


def dot(left, right):
    return jnp.dot(left, right, preferred_element_type=f32)


def dot_right(left, right):
    return lax.dot_general(left, right, (((1,), (1,)), ((), ())), preferred_element_type=f32)


def dot_left(left, right):
    return lax.dot_general(left, right, (((0,), (0,)), ((), ())), preferred_element_type=f32)


def whole_rows(ref, places):
    if len(places) == 1:
        return ref[places[0]]
    return jnp.concatenate([ref[place] for place in places], axis=0)


def part_place(index, parts, walked):
    if not walked:
        return index
    return index // 2 + (index % 2) * (parts - 1 - 2 * (index // 2))


def places_of(parts, walked):
    return [part_place(index, parts, walked) for index in range(parts)]


def two_terms(values):
    high = values.astype(bf16)
    low = (values - high.astype(f32)).astype(bf16)
    return jnp.concatenate([high, low], axis=1)


def inverse_rms(values):
    return lax.rsqrt(jnp.mean(values * values, axis=-1, keepdims=True) + epsilon)


def partner(values, first_half, quarter):
    width = values.shape[1]
    return jnp.where(
        first_half, pltpu.roll(values, width - quarter, 1), pltpu.roll(values, quarter, 1)
    )


def first_half_mask(shape, quarter):
    lane = lax.broadcasted_iota(jnp.int32, shape, 1)
    return lane % (2 * quarter) < quarter


def head_groups(heads, head_size):
    width = heads * head_size
    span = min(2 * LANES, width)
    groups = []
    for head in range(heads):
        low, high = head * head_size, (head + 1) * head_size
        if groups and high <= groups[-1][0] + span:
            groups[-1][2].append(head)
        else:
            groups.append((min(low // LANES * LANES, width - span), span, [head]))
    return groups


def head_mask(head, head_size, start, span):
    lane = lax.broadcasted_iota(jnp.int32, (1, span), 1) + start
    inside = jnp.logical_and(lane >= head * head_size, lane < (head + 1) * head_size)
    return inside.astype(f32).astype(bf16)


def side_by_side(parts):
    return parts[0] if len(parts) == 1 else jnp.concatenate(parts, axis=1)


def one_above_other(parts):
    return parts[0] if len(parts) == 1 else jnp.concatenate(parts, axis=0)


def rotated(raw, part, tables, keep_scale=None):
    cos_ref, sin_ref, gain_ref, sum_ref, spread_ref, repeat_ref, head_size = tables
    quarter = head_size // 4
    squares = dot((raw * raw).astype(bf16), sum_ref[...])
    scale = lax.rsqrt(squares * (1.0 / head_size) + epsilon)
    scale = dot(two_terms(scale), spread_ref[...])
    if keep_scale is not None:
        keep_scale[part] = scale
    scaled = raw * scale * gain_ref[part : part + 1]
    first_half = first_half_mask((1, raw.shape[1]), quarter)
    cos, sin = dot(cos_ref[...], repeat_ref[...]), dot(sin_ref[...], repeat_ref[...])
    return (scaled * cos + partner(scaled, first_half, quarter) * sin).astype(bf16)


def attention_forward_kernel(heads, places, first, keep, refs):
    if keep:
        received_ref, refs = refs[0], refs[1:]
    x_ref, mod_ref, cos_ref, sin_ref, gain_ref, sum_ref, spread_ref, repeat_ref = refs[:8]
    query_weight, joined_ref = refs[8:10]
    refs = refs[10:]
    patches, width = x_ref.shape
    if keep:
        outs, refs = refs[:8], refs[8:]
        weight, mixed, sems = refs[:3]
        held, out_sems = refs[3:11], refs[11]
    else:
        middle_ref, normed_two_ref, weight, mixed, sems = refs
    head_size = width // heads
    tables = (cos_ref, sin_ref, gain_ref, sum_ref, spread_ref, repeat_ref, head_size)

    def fetch(part):
        return pltpu.make_async_copy(
            joined_ref.at[:, :, pl.ds((part + 1) * width, width)], weight.at[part], sems.at[part]
        )

    @pl.when(pl.program_id(0) == 0)
    def _():
        for part in range(3):
            fetch(part).start()

    def arrived(part):
        @pl.when(pl.program_id(0) == 0)
        def _():
            fetch(part).wait()

        return whole_rows(weight.at[part], places)

    def put(which):
        rows = pl.ds(first * patches, patches)
        return pltpu.make_async_copy(held[which], outs[which].at[rows], out_sems.at[which])

    flow = x_ref[...].astype(f32)
    if keep:
        flow = flow + received_ref[...].astype(f32)
    mod = mod_ref[0]
    normed = (flow * inverse_rms(flow) * (1.0 + mod[1:2]) + mod[0:1]).astype(bf16)
    raw = dot(normed, whole_rows(query_weight, places))
    if keep:
        held[7][...] = flow.astype(bf16)
        held[0][...] = normed
        held[1][:, :width] = raw
        put(7).start()
        put(0).start()
    queries = rotated(raw, 0, tables)
    raw = dot(normed, arrived(0))
    if keep:
        held[1][:, width:] = raw
        put(1).start()
    keys = rotated(raw, 1, tables)
    values = dot(normed, arrived(1)).astype(bf16)
    if keep:
        held[2][...] = values
        put(2).start()
    mixed[...] = jnp.zeros_like(mixed)
    factor = head_size ** (-0.5) * math.log2(math.e)
    for start, span, members in head_groups(heads, head_size):
        window = slice(start, start + span)
        probs, parts = [], []
        for head in members:
            mask = head_mask(head, head_size, start, span)
            expon = jnp.exp2(dot_right(queries[:, window], keys[:, window] * mask) * factor)
            total = jnp.sum(expon, axis=-1, keepdims=True)
            probs.append((expon * (1.0 / total)).astype(bf16))
            parts.append(values[:, window] * mask)
        mixed[:, window] += dot(side_by_side(probs), one_above_other(parts))
    attended = mixed[...].astype(bf16)
    if keep:
        held[3][...] = attended
        put(3).start()
    branch = dot(attended, arrived(2))
    middle = flow + mod[2:3] * branch
    normed_two = (middle * inverse_rms(middle) * (1.0 + mod[4:5]) + mod[3:4]).astype(bf16)
    if keep:
        for which, value in ((4, branch), (5, middle), (6, normed_two)):
            held[which][...] = value
            put(which).start()
        for which in range(8):
            put(which).wait()
    else:
        middle_ref[...] = middle
        normed_two_ref[...] = normed_two


def attention_forward(x, received, mod, tables, gain, joined, walked, first, count, made=None):
    keep = received is not None
    images, unused, width = mod.shape
    tokens = x.shape[0]
    patches = tokens // images
    heads = width // tables[-1]
    arrays = tables[:-1]
    parts, rows, unused = joined.shape
    row = lambda columns: pl.BlockSpec((patches, columns), lambda image: (first + image, 0))
    fixed = lambda array: pl.BlockSpec(array.shape, lambda image: (0,) * array.ndim)
    anywhere = pl.BlockSpec(memory_space=pl.ANY)
    shapes = [(width, f32), (width, bf16)]
    if keep:
        shapes = [
            (width, bf16),
            (2 * width, f32),
            (width, bf16),
            (width, bf16),
            (width, f32),
            (width, f32),
            (width, bf16),
            (width, bf16),
        ]
    made = [] if made is None else list(made)
    extra = [received] if keep else []
    inputs = 10 + len(extra)
    scratch = [
        pltpu.VMEM((3, parts, rows, width), bf16),
        pltpu.VMEM((patches, width), f32),
        pltpu.SemaphoreType.DMA((3,)),
    ]
    if keep:
        scratch += [pltpu.VMEM((patches, columns), kind) for columns, kind in shapes]
        scratch += [pltpu.SemaphoreType.DMA((len(shapes),))]

    def body(*refs):
        refs = refs[:inputs] + refs[inputs + len(made) :]
        attention_forward_kernel(heads, places_of(parts, walked), first, keep, refs)

    return pl.pallas_call(
        body,
        grid=(count,),
        in_specs=[pl.BlockSpec((patches, width), lambda image: (image, 0))] * len(extra)
        + [
            row(width),
            pl.BlockSpec((1, 6, width), lambda image: (first + image, 0, 0)),
            row(arrays[0].shape[1]),
            row(arrays[1].shape[1]),
            fixed(gain),
            fixed(arrays[2]),
            fixed(arrays[3]),
            fixed(arrays[4]),
            pl.BlockSpec((parts, rows, width), lambda image: (0, 0, 0)),
            anywhere,
        ]
        + [anywhere] * len(made),
        out_specs=[anywhere if keep else row(columns) for columns, kind in shapes],
        out_shape=[jax.ShapeDtypeStruct((tokens, columns), kind) for columns, kind in shapes],
        input_output_aliases={inputs + index: index for index in range(len(made))},
        scratch_shapes=scratch,
        compiler_params=params(),
        cost_estimate=cost(
            2 * count * patches * width * (4 * width + 2 * patches),
            8 * width * width + count * patches * width * 20,
        ),
    )(*extra, x, mod, arrays[0], arrays[1], gain, *arrays[2:], joined, joined, *made)


def pack_columns(matrices, pieces):
    rows = matrices[0].shape[0]
    total = sum(columns for unused, first, columns in pieces)

    def body(*refs):
        at = 0
        for which, first, columns in pieces:
            refs[-1][:, at : at + columns] = refs[which][:, first : first + columns]
            at += columns

    if any(columns % LANES or first % LANES for unused, first, columns in pieces):
        return jnp.concatenate(
            [matrices[which][:, first : first + columns] for which, first, columns in pieces], axis=1
        )
    return pl.pallas_call(
        body,
        grid=(1,),
        in_specs=whole_specs(matrices),
        out_specs=pl.BlockSpec((rows, total), lambda i: (0, 0)),
        out_shape=jax.ShapeDtypeStruct((rows, total), matrices[0].dtype),
        compiler_params=params(),
        cost_estimate=cost(0, 4 * rows * total),
    )(*matrices)


def gate_up_kernel(places, keep, normed_ref, gate_ref, up_ref, *outs):
    normed = normed_ref[...]
    gate = dot(normed, whole_rows(gate_ref, places))
    up = dot(normed, whole_rows(up_ref, places))
    outs[0][...] = (gate * (1.0 / (1.0 + jnp.exp(-gate))) * up).astype(bf16)
    if keep:
        outs[1][...] = gate.astype(bf16)
        outs[2][...] = up.astype(bf16)


def gate_up(normed_two, joined, hidden, walked, keep):
    tokens, width = normed_two.shape
    step = 512
    base = 4 * width // step
    count = hidden // step
    parts, rows, unused = joined.shape
    shapes = 3 if keep else 1
    return pl.pallas_call(
        functools.partial(gate_up_kernel, places_of(parts, walked), keep),
        grid=(count,),
        in_specs=[
            pl.BlockSpec((tokens, width), lambda i: (0, 0)),
            pl.BlockSpec((parts, rows, step), lambda i: (0, 0, base + i)),
            pl.BlockSpec((parts, rows, step), lambda i: (0, 0, base + count + i)),
        ],
        out_specs=[pl.BlockSpec((tokens, step), lambda i: (0, i))] * shapes,
        out_shape=[jax.ShapeDtypeStruct((tokens, hidden), bf16)] * shapes,
        compiler_params=params(),
        cost_estimate=cost(4 * tokens * width * hidden, 4 * width * hidden + 2 * shapes * tokens * hidden),
    )(normed_two, joined, joined)


def down_projection(active, act, down, middle, mod, first, count, keep, step):
    hidden = act.shape[1]
    images, unused, width = mod.shape
    patches = act.shape[0] // images
    tokens = count * patches
    outs = [jax.ShapeDtypeStruct((tokens, width), bf16)]
    scratch = [pltpu.VMEM((tokens, width), f32)]
    if keep:
        outs.append(jax.ShapeDtypeStruct((tokens, width), f32))
        scratch = []

    def body(active_ref, act_ref, middle_ref, mod_ref, down_ref, result_ref, total):
        index = pl.program_id(0)

        @pl.when(active_ref[0] == 0)
        def _():
            result_ref[...] = jnp.zeros_like(result_ref)

        @pl.when(active_ref[0] != 0)
        def _():
            term = dot(act_ref[...], down_ref[...])

            @pl.when(index == 0)
            def _():
                total[...] = term

            @pl.when(index > 0)
            def _():
                total[...] += term

            @pl.when(index == hidden // step - 1)
            def _():
                for image in range(count):
                    at = slice(image * patches, (image + 1) * patches)
                    gate = mod_ref[first + image, 5:6]
                    result_ref[at] = (middle_ref[at] + gate * total[at]).astype(bf16)

    return pl.pallas_call(
        body,
        grid_spec=pltpu.PrefetchScalarGridSpec(
            num_scalar_prefetch=1,
            grid=(hidden // step,),
            in_specs=[
                pl.BlockSpec((tokens, step), lambda i, active: (first // count, i * active[0])),
                pl.BlockSpec((tokens, width), lambda i, active: (first // count, 0)),
                pl.BlockSpec(mod.shape, lambda i, active: (0, 0, 0)),
                pl.BlockSpec((step, width), lambda i, active: (i * active[0], 0)),
            ],
            out_specs=[pl.BlockSpec((tokens, width), lambda i, active: (0, 0))] * len(outs),
            scratch_shapes=scratch,
        ),
        out_shape=outs,
        compiler_params=params(),
        cost_estimate=cost(2 * tokens * width * hidden, 2 * width * hidden + 8 * tokens * width),
    )(active, act, middle, mod, down)


def incoming(cot_ref, back_refs, image, at):
    value = cot_ref[at].astype(f32)
    return value + back_refs[image][...].astype(f32) if back_refs else value


def mlp_gradient(cot, backs, mod, first, count):
    images, unused, width = mod.shape
    patches = cot.shape[0] // images

    def body(cot_ref, mod_ref, *refs):
        for image in range(count):
            at = slice(image * patches, (image + 1) * patches)
            grads = incoming(cot_ref, refs[: len(backs)], image, at)
            refs[-1][at] = (mod_ref[first + image, 5:6] * grads).astype(bf16)

    return pl.pallas_call(
        body,
        grid=(1,),
        in_specs=[
            pl.BlockSpec((count * patches, width), lambda i: (first // count, 0)),
            pl.BlockSpec(mod.shape, lambda i: (0, 0, 0)),
        ]
        + [pl.BlockSpec((patches, width), lambda i: (0, 0))] * len(backs),
        out_specs=pl.BlockSpec((count * patches, width), lambda i: (0, 0)),
        out_shape=jax.ShapeDtypeStruct((count * patches, width), bf16),
        compiler_params=params(),
        cost_estimate=cost(0, 6 * count * patches * width),
    )(cot, mod, *backs)


def stacked(refs):
    return refs[0][...] if len(refs) == 1 else jnp.concatenate([ref[...] for ref in refs], axis=0)


def whole_specs(arrays):
    return [pl.BlockSpec(array.shape, lambda i: (0, 0)) for array in arrays]


def act_backward(mlp_grads, down, step):
    hidden, width = down.shape
    tokens = sum(grad.shape[0] for grad in mlp_grads)

    def body(*refs):
        refs[-1][...] = dot_right(stacked(refs[:-2]), refs[-2][...]).astype(bf16)

    return pl.pallas_call(
        body,
        grid=(hidden // step,),
        in_specs=whole_specs(mlp_grads) + [pl.BlockSpec((step, width), lambda i: (i, 0))],
        out_specs=pl.BlockSpec((tokens, step), lambda i: (0, i)),
        out_shape=jax.ShapeDtypeStruct((tokens, hidden), bf16),
        compiler_params=params(),
        cost_estimate=cost(2 * tokens * width * hidden, 2 * width * hidden + 4 * tokens * width),
    )(*mlp_grads, down)


def mlp_backward(cot, backs, mlp, act_grad, gate, up, joined, middle, branch, mod, walked, keep):
    tokens, hidden = gate.shape
    images, unused, width = mod.shape
    patches = tokens // images
    parts, rows, unused = joined.shape
    places = places_of(parts, walked)
    step = 512
    base = 4 * width // step
    count = hidden // step
    whole = pl.BlockSpec((tokens, width), lambda i: (0, 0))
    block = pl.BlockSpec((tokens, step), lambda i: (0, i))
    anywhere = pl.BlockSpec(memory_space=pl.ANY)
    late = [cot, middle] + ([mlp, branch] if keep else [])

    def body(act_grad_ref, gate_ref, up_ref, gate_weight, up_weight, mod_ref, joined_ref, *refs):
        back_refs, refs = refs[: len(backs)], refs[len(backs) :]
        sources, refs = refs[: len(late)], refs[len(late) :]
        sems, refs = refs[-1], refs[:-1]
        copies, refs = refs[-len(late) :], refs[: -len(late)]
        cot_ref, middle_ref = copies[:2]
        if keep:
            mlp_ref, branch_ref = copies[2:]
        middle_grad_ref, mixed_grad_ref = refs[:2]
        refs = refs[2:]
        if keep:
            gate_grad_ref, up_grad_ref, branch_grad_ref, sums_ref = refs[:4]
            refs = refs[4:]
        total, out_weight, sem = refs
        index = pl.program_id(0)
        fetches = [
            pltpu.make_async_copy(joined_ref.at[:, :, pl.ds(3 * width, width)], out_weight, sem)
        ] + [
            pltpu.make_async_copy(source, copies[which], sems.at[which])
            for which, source in enumerate(sources)
        ]

        @pl.when(index == 0)
        def _():
            for fetch in fetches:
                fetch.start()

        gate_val, up_val = gate_ref[...].astype(f32), up_ref[...].astype(f32)
        sigma = 1.0 / (1.0 + jnp.exp(-gate_val))
        slope = act_grad_ref[...].astype(f32) * sigma
        gate_grad = (slope * up_val * (1.0 + gate_val * (1.0 - sigma))).astype(bf16)
        up_grad = (slope * gate_val).astype(bf16)
        if keep:
            gate_grad_ref[...] = gate_grad
            up_grad_ref[...] = up_grad
        term = dot_right(gate_grad, whole_rows(gate_weight, places))
        term = term + dot_right(up_grad, whole_rows(up_weight, places))

        @pl.when(index == 0)
        def _():
            total[...] = term

        @pl.when(index > 0)
        def _():
            total[...] += term

        @pl.when(index == count - 1)
        def _():
            for fetch in fetches:
                fetch.wait()
            matrix = whole_rows(out_weight, places)
            for image in range(images):
                at = slice(image * patches, (image + 1) * patches)
                mod = mod_ref[image]
                grad, flow = total[at], middle_ref[at]
                inverse = inverse_rms(flow)
                normal = flow * inverse
                scaled = grad * (1.0 + mod[4:5])
                mean = jnp.mean(scaled * normal, axis=-1, keepdims=True)
                out_grad = incoming(cot_ref, back_refs, image, at)
                middle_grad = out_grad + (scaled - normal * mean) * inverse
                middle_grad_ref[at] = middle_grad
                branch_grad = (mod[2:3] * middle_grad).astype(bf16)
                mixed_grad_ref[at] = dot_right(branch_grad, matrix).astype(bf16)
                if keep:
                    branch_grad_ref[at] = branch_grad
                    terms = [middle_grad * branch_ref[at], grad, grad * normal, out_grad * mlp_ref[at]]
                    for place, value in enumerate(terms):
                        sums_ref[image, place : place + 1] = jnp.sum(value, axis=0, keepdims=True)

    out_shapes = [
        jax.ShapeDtypeStruct((tokens, width), f32),
        jax.ShapeDtypeStruct((tokens, width), bf16),
    ]
    out_specs = [whole, whole]
    if keep:
        out_shapes += [jax.ShapeDtypeStruct((tokens, hidden), bf16)] * 2
        out_shapes += [jax.ShapeDtypeStruct((tokens, width), bf16)]
        out_shapes += [jax.ShapeDtypeStruct((images, 4, width), f32)]
        out_specs += [block, block, whole, pl.BlockSpec((images, 4, width), lambda i: (0, 0, 0))]
    return pl.pallas_call(
        body,
        grid=(count,),
        in_specs=[
            block,
            block,
            block,
            pl.BlockSpec((parts, rows, step), lambda i: (0, 0, base + i)),
            pl.BlockSpec((parts, rows, step), lambda i: (0, 0, base + count + i)),
            pl.BlockSpec(mod.shape, lambda i: (0, 0, 0)),
            anywhere,
        ]
        + [pl.BlockSpec((patches, width), lambda i: (0, 0))] * len(backs)
        + [anywhere] * len(late),
        out_specs=out_specs,
        out_shape=out_shapes,
        scratch_shapes=[
            pltpu.VMEM((tokens, width), f32),
            pltpu.VMEM((parts, rows, width), bf16),
            pltpu.SemaphoreType.DMA,
        ]
        + [pltpu.VMEM(array.shape, array.dtype) for array in late]
        + [pltpu.SemaphoreType.DMA((len(late),))],
        compiler_params=params(),
        cost_estimate=cost(
            2 * tokens * width * (2 * hidden + width), 4 * width * hidden + 6 * tokens * hidden
        ),
    )(act_grad, gate, up, joined, joined, mod, joined, *backs, *late)


def attention_backward_kernel(heads, places, first, keep, refs):
    raw_ref, value_ref, mixed_grad_ref, middle_grad_hbm, x_hbm, mod_ref = refs[:6]
    cos_ref, sin_ref, gain_ref, sum_ref, spread_ref, repeat_ref, joined_ref = refs[6:13]
    refs = refs[13:]
    if keep:
        flow_grad_ref, qkv_grad_ref, sums_ref = refs[:3]
        refs = refs[3:]
    else:
        back_ref = refs[0]
        refs = refs[1:]
    weight, scales, query_total, key_total, value_total, middle_grad_ref, x_ref, sems = refs
    patches, width = x_ref.shape
    head_size = width // heads
    quarter = head_size // 4
    factor = head_size ** (-0.5)
    image = pl.program_id(0)
    tables = (cos_ref, sin_ref, gain_ref, sum_ref, spread_ref, repeat_ref, head_size)
    rows = pl.ds((first + image) * patches, patches)
    late = [
        pltpu.make_async_copy(x_hbm.at[rows], x_ref, sems.at[3]),
        pltpu.make_async_copy(middle_grad_hbm.at[rows], middle_grad_ref, sems.at[4]),
    ]

    def fetch(part):
        return pltpu.make_async_copy(
            joined_ref.at[:, :, pl.ds(part * width, width)], weight.at[part], sems.at[part]
        )

    @pl.when(image == 0)
    def _():
        for part in range(3):
            fetch(part).start()

    for copy in late:
        copy.start()
    first_half = first_half_mask((1, width), quarter)
    raws = [raw_ref[:, part * width : (part + 1) * width] for part in range(2)]
    queries = rotated(raws[0], 0, tables, scales)
    keys = rotated(raws[1], 1, tables, scales)
    values, mixed_grad = value_ref[...], mixed_grad_ref[...]
    query_total[...] = jnp.zeros_like(query_total)
    key_total[...] = jnp.zeros_like(key_total)
    value_total[...] = jnp.zeros_like(value_total)
    for start, span, members in head_groups(heads, head_size):
        window = slice(start, start + span)
        probs, slopes, key_parts, query_parts, grad_parts = [], [], [], [], []
        for head in members:
            mask = head_mask(head, head_size, start, span)
            key_part, query_part = keys[:, window] * mask, queries[:, window] * mask
            grad_part = mixed_grad[:, window] * mask
            scores = dot_right(key_part, queries[:, window])
            expon = jnp.exp2(scores * (factor * math.log2(math.e)))
            prob = expon * (1.0 / jnp.sum(expon, axis=0, keepdims=True))
            prob_grad = dot_right(values[:, window], grad_part)
            middle = jnp.sum(prob * prob_grad, axis=0, keepdims=True)
            probs.append(prob.astype(bf16))
            slopes.append((prob * (prob_grad - middle)).astype(bf16))
            key_parts.append(key_part)
            query_parts.append(query_part)
            grad_parts.append(grad_part)
        value_total[:, window] += dot(side_by_side(probs), one_above_other(grad_parts))
        key_total[:, window] += dot(side_by_side(slopes), one_above_other(query_parts))
        query_total[:, window] += dot_left(one_above_other(slopes), one_above_other(key_parts))

    def raw_grad(part, total):
        turned = total[...] * factor
        cos, sin = dot(cos_ref[...], repeat_ref[...]), dot(sin_ref[...], repeat_ref[...])
        grad = turned * cos + partner(turned * sin, first_half, quarter)
        scale = scales[part]
        normal = raw_ref[:, part * width : (part + 1) * width] * scale
        if keep:
            sums_ref[0, 2 + part : 3 + part] = jnp.sum(grad * normal, axis=0, keepdims=True)
        grad = grad * gain_ref[part : part + 1]
        mean = dot((grad * normal).astype(bf16), sum_ref[...]) * (1.0 / head_size)
        mean = dot(two_terms(mean), spread_ref[...])
        return (scale * (grad - normal * mean)).astype(bf16)

    def arrived(part):
        @pl.when(image == 0)
        def _():
            fetch(part).wait()

        return whole_rows(weight.at[part], places)

    parts = [raw_grad(0, query_total), raw_grad(1, key_total), value_total[...].astype(bf16)]
    grad = None
    for part in range(3):
        if keep:
            qkv_grad_ref[:, part * width : (part + 1) * width] = parts[part]
        term = dot_right(parts[part], arrived(part))
        grad = term if grad is None else grad + term
    for copy in late:
        copy.wait()
    mod = mod_ref[0]
    flow = x_ref[...].astype(f32)
    inverse = inverse_rms(flow)
    normal = flow * inverse
    scaled = grad * (1.0 + mod[1:2])
    mean = jnp.mean(scaled * normal, axis=-1, keepdims=True)
    flow_grad = middle_grad_ref[...] + (scaled - normal * mean) * inverse
    if keep:
        flow_grad_ref[...] = flow_grad
        sums_ref[0, 0:1] = jnp.sum(grad, axis=0, keepdims=True)
        sums_ref[0, 1:2] = jnp.sum(grad * normal, axis=0, keepdims=True)
    else:
        back_ref[...] = flow_grad.astype(bf16)


def attention_backward(
    raw, value, mixed_grad, middle_grad, x, mod, tables, gain, joined, walked, first, count, keep
):
    images, unused, width = mod.shape
    patches = x.shape[0] // images
    tokens = count * patches
    heads = width // tables[-1]
    arrays = tables[:-1]
    parts, rows, unused = joined.shape
    row = lambda columns: pl.BlockSpec((patches, columns), lambda image: (first + image, 0))
    token = lambda columns: pl.BlockSpec((patches, columns), lambda image: (image, 0))
    fixed = lambda array: pl.BlockSpec(array.shape, lambda image: (0,) * array.ndim)
    anywhere = pl.BlockSpec(memory_space=pl.ANY)
    out_shapes = [jax.ShapeDtypeStruct((tokens, width), bf16)]
    out_specs = [token(width)]
    if keep:
        out_shapes = [
            jax.ShapeDtypeStruct((tokens, width), f32),
            jax.ShapeDtypeStruct((tokens, 3 * width), bf16),
            jax.ShapeDtypeStruct((count, 4, width), f32),
        ]
        out_specs = [
            token(width),
            token(3 * width),
            pl.BlockSpec((1, 4, width), lambda image: (image, 0, 0)),
        ]

    def body(*refs):
        attention_backward_kernel(heads, places_of(parts, walked), first, keep, refs)

    return pl.pallas_call(
        body,
        grid=(count,),
        in_specs=[
            row(2 * width),
            row(width),
            row(width),
            anywhere,
            anywhere,
            pl.BlockSpec((1, 6, width), lambda image: (first + image, 0, 0)),
            row(arrays[0].shape[1]),
            row(arrays[1].shape[1]),
            fixed(gain),
            fixed(arrays[2]),
            fixed(arrays[3]),
            fixed(arrays[4]),
            anywhere,
        ],
        out_specs=out_specs,
        out_shape=out_shapes,
        scratch_shapes=[
            pltpu.VMEM((3, parts, rows, width), bf16),
            pltpu.VMEM((2, patches, width), f32),
            pltpu.VMEM((patches, width), f32),
            pltpu.VMEM((patches, width), f32),
            pltpu.VMEM((patches, width), f32),
            pltpu.VMEM((patches, width), f32),
            pltpu.VMEM((patches, width), bf16),
            pltpu.SemaphoreType.DMA((5,)),
        ],
        compiler_params=params(),
        cost_estimate=cost(
            2 * tokens * width * (3 * width + 5 * patches),
            6 * width * width + tokens * width * 20,
        ),
    )(raw, value, mixed_grad, middle_grad, x, mod, arrays[0], arrays[1], gain, *arrays[2:], joined)


def down_grad(mlp_grads, act, step):
    tokens, hidden = act.shape
    width = mlp_grads[0].shape[1]

    def body(act_ref, *refs):
        refs[-1][...] = dot_left(act_ref[...], stacked(refs[:-1])).astype(bf16)

    return pl.pallas_call(
        body,
        grid=(hidden // step,),
        in_specs=[pl.BlockSpec((tokens, step), lambda i: (0, i))] + whole_specs(mlp_grads),
        out_specs=pl.BlockSpec((step, width), lambda i: (i, 0)),
        out_shape=jax.ShapeDtypeStruct((hidden, width), bf16),
        compiler_params=params(),
        cost_estimate=cost(2 * tokens * width * hidden, 2 * width * hidden),
    )(act, *mlp_grads)


def matrix_grad_kernel(places, counts, *refs):
    pairs = len(counts)
    inputs, grads, out_ref = refs[:pairs], refs[pairs : 2 * pairs], refs[2 * pairs]
    rows = out_ref.shape[1]
    step = pl.program_id(0)
    first = 0
    for index in range(pairs):

        @pl.when(jnp.logical_and(step >= first, step < first + counts[index]))
        def _(index=index):
            product = dot_left(inputs[index][...], grads[index][...]).astype(bf16)
            for part, place in enumerate(places):
                out_ref[place] = product[part * rows : (part + 1) * rows]

        first += counts[index]


def matrix_grad(inputs, grads, step, parts, walked):
    tokens, width = inputs[0].shape
    counts = [grad.shape[1] // step for grad in grads]
    columns = sum(counts) * step
    rows = width // parts
    firsts = [sum(counts[:index]) for index in range(len(counts))]

    def grad_spec(first, count):
        return pl.BlockSpec((tokens, step), lambda i: (0, jnp.clip(i - first, 0, count - 1)))

    return pl.pallas_call(
        functools.partial(matrix_grad_kernel, places_of(parts, walked), counts),
        grid=(sum(counts),),
        in_specs=[pl.BlockSpec((tokens, width), lambda i: (0, 0))] * len(inputs)
        + [grad_spec(first, count) for first, count in zip(firsts, counts)],
        out_specs=pl.BlockSpec((parts, rows, step), lambda i: (0, 0, i)),
        out_shape=jax.ShapeDtypeStruct((parts, rows, columns), bf16),
        compiler_params=params(),
        cost_estimate=cost(2 * tokens * width * columns, 2 * width * columns),
    )(*inputs, *grads)


def walk_of(count):
    chips = count // 2
    order = [chip for chip in range(chips) if chip % 2 == 0]
    order += [chip for chip in reversed(range(chips)) if chip % 2 == 1]
    return [2 * chip + core for chip in order for core in (0, 1)]


def from_walk(rows, count):
    blocks = rows.reshape(count // 2, -1, rows.shape[-1])
    places = places_of(count // 2, True)
    return jnp.concatenate([blocks[place] for place in places], axis=0)


def walk_columns(which, columns, count):
    each = columns // (count // 2)
    return [(which, device // 2 * each, each) for device in walk_of(count)[::2]]


def columns_from_walk(matrix, count):
    each = matrix.shape[1] // (count // 2)
    places = places_of(count // 2, True)
    return jnp.concatenate(
        [matrix[:, place * each : (place + 1) * each] for place in places], axis=1
    )


def to_walk(rows, count):
    blocks = rows.reshape(count // 2, -1, rows.shape[-1])
    return jnp.concatenate([blocks[device // 2] for device in walk_of(count)[::2]], axis=0)


def gather_walk(rows, count):
    return lax.all_gather(rows, "dp", axis=0, tiled=True, axis_index_groups=[walk_of(count)])


def scatter_walk(rows, count):
    part = lax.psum_scatter(
        rows, "dp", scatter_dimension=0, tiled=True, axis_index_groups=[walk_of(count)]
    )
    return lax.optimization_barrier(part)


def as_parts(rows, count):
    each = rows.shape[0] // (count // 2)
    if each % 16 == 0:
        return rows.reshape(count // 2, each, rows.shape[1]), True
    whole = from_walk(rows, count)
    return whole[None], False


def swapped(block, bit, count):
    return lax.ppermute(block, "dp", [(device, device ^ bit) for device in range(count)])


def gather_small(block, count):
    me = lax.axis_index("dp")
    block = block[None]
    bit = count // 2
    while bit:
        other = swapped(block, bit, count)
        low = (me & bit) == 0
        pair = [jnp.where(low, block, other), jnp.where(low, other, block)]
        block = jnp.stack(pair, axis=1).reshape(2 * block.shape[0], *block.shape[1:])
        bit //= 2
    return block


def scatter_small(blocks, count):
    me = lax.axis_index("dp")
    bit = 1
    while bit < count:
        pairs = blocks.reshape(blocks.shape[0] // 2, 2, *blocks.shape[1:])
        mine = jnp.where((me & bit) == 0, 0, 1)
        give = lax.dynamic_index_in_dim(pairs, 1 - mine, 1, keepdims=False)
        keep = lax.dynamic_index_in_dim(pairs, mine, 1, keepdims=False)
        blocks = keep + swapped(give, bit, count)
        bit *= 2
    return blocks[0]


def time_features(timestep_ids, width):
    half_width = width // 2
    frequency = jnp.exp(-math.log(10000.0) * jnp.arange(half_width, dtype=f32) / half_width)
    angle_rows = timestep_ids.astype(f32)[:, None] * frequency[None, :]
    return jnp.concatenate([jnp.cos(angle_rows), jnp.sin(angle_rows)], axis=-1)


def rotation_tables(positions, width, head_size):
    quarter = head_size // 4
    frequency = jnp.exp(-math.log(10000.0) * jnp.arange(quarter, dtype=f32) / quarter)
    places = positions.reshape(-1, 1)
    row_angle = (places // GRID).astype(f32) * frequency
    col_angle = (places % GRID).astype(f32) * frequency
    row_cos, row_sin = jnp.cos(row_angle), jnp.sin(row_angle)
    col_cos, col_sin = jnp.cos(col_angle), jnp.sin(col_angle)
    cos = jnp.concatenate([row_cos, row_cos, col_cos, col_cos], axis=1)
    sin = jnp.concatenate([-row_sin, row_sin, -col_sin, col_sin], axis=1)
    padding = ((0, 0), (0, LANES - head_size))
    number = jnp.arange(LANES)
    column = jnp.arange(width)
    summing = (column[:, None] // head_size == number[None, :]).astype(bf16)
    spreading = (column[None, :] // head_size == number[:, None]).astype(bf16)
    repeating = (column[None, :] % head_size == number[:, None]).astype(bf16)
    return (
        two_terms(jnp.pad(cos, padding)),
        two_terms(jnp.pad(sin, padding)),
        summing,
        jnp.concatenate([spreading, spreading]),
        jnp.concatenate([repeating, repeating]),
    )


def per_device(
    tokens,
    cotangent,
    labels,
    timesteps,
    positions,
    label_table,
    ada_weight,
    qkv_weight,
    out_weight,
    gate_weight,
    up_weight,
    down_weight,
    q_gain,
    k_gain,
):
    first_section = lax.axis_index("section") == 0
    first_only = first_section.astype(jnp.int32).reshape(1)
    always = jnp.ones((1,), jnp.int32)
    count = lax.axis_size("dp")
    me = lax.axis_index("dp")
    images, patches, width = tokens.shape
    hidden = gate_weight.shape[2]
    head_size = q_gain.shape[1]
    heads = width // head_size
    rows = ada_weight.shape[1]
    classes = label_table.shape[0]

    pieces = [(0, 0, 3 * width), (1, 0, width)]
    pieces += walk_columns(2, hidden, count) + walk_columns(3, hidden, count)
    joined = gather_walk(
        pack_columns([qkv_weight[0], out_weight[0], gate_weight[0], up_weight[0]], pieces), count
    )

    ids = gather_small(jnp.stack([labels, timesteps]), count)
    all_labels = ids[:, 0].reshape(-1)
    all_times = ids[:, 1].reshape(-1)
    label_hot = all_labels[:, None] == jnp.arange(classes, dtype=jnp.int32)[None, :]
    condition = dot(label_hot.astype(bf16), label_table) + time_features(all_times, width)
    sigma_cond = jax.nn.sigmoid(condition)
    silu_cond = (condition * sigma_cond).astype(bf16)
    silu_rows = lax.dynamic_slice_in_dim(silu_cond, me * rows, rows, 1)
    mod_part = dot(silu_rows, ada_weight[0])
    mod = scatter_small(mod_part.reshape(count, images, -1), count).reshape(images, 6, width)
    tables = rotation_tables(positions, width, head_size)
    flat = tokens.reshape(images * patches, width)
    own = jnp.where(first_section, flat, jnp.zeros_like(flat))

    down, joined, mod, own, tables = lax.optimization_barrier(
        (down_weight[0], joined, mod, own, tables)
    )
    down = gather_walk(down, count)
    joined, walked = as_parts(joined, count)
    tables = (*tables, head_size)
    gain = jnp.tile(jnp.concatenate([q_gain, k_gain]), (1, heads))

    cot = cotangent[0].reshape(images * patches, width)
    middle, normed_two = attention_forward(
        flat, None, mod, tables, gain, joined, walked, 0, images
    )
    (act,) = gate_up(normed_two, joined, hidden, walked, False)
    received = []
    for image in range(images):
        (early,) = down_projection(
            first_only, act, down, middle, mod, image, 1, False, hidden // 2
        )
        received.append(lax.ppermute(early, "section", [(0, 1)]))
    mlp_grad, unused = lax.optimization_barrier((mlp_gradient(cot, [], mod, 0, images), early))
    mlp_grads = [mlp_grad]
    act_grad = act_backward(mlp_grads, down, hidden // 2)
    kept = None
    for image in range(images):
        kept = attention_forward(
            own, received[image], mod, tables, gain, joined, walked, image, 1, kept
        )
    normed, raw, values, attended, branch, middle, normed_two, layer_in = kept
    act, gate, up = gate_up(normed_two, joined, hidden, walked, True)

    middle_grad, mixed_grad = mlp_backward(
        cot, [], None, act_grad, gate, up, joined, middle, None, mod, walked, False
    )
    backs = []
    for image in range(images):
        (early,) = attention_backward(
            raw,
            values,
            mixed_grad,
            middle_grad,
            layer_in,
            mod,
            tables,
            gain,
            joined,
            walked,
            image,
            1,
            False,
        )
        backs.append(lax.ppermute(early, "section", [(1, 0)]))
    late_act, unused = lax.optimization_barrier((act, early))
    result, mlp = down_projection(
        always, late_act, down, middle, mod, 0, images, True, hidden // 2
    )

    late_cot, unused = lax.optimization_barrier((cot, mlp))
    mlp_grads = [
        mlp_gradient(late_cot, [back], mod, image, 1) for image, back in enumerate(backs)
    ]
    down_term = down_grad(mlp_grads, act, hidden // 4)
    down_term, mlp_grads = lax.optimization_barrier((down_term, mlp_grads))
    down_part = scatter_walk(down_term, count)
    act_grad = act_backward(mlp_grads, down, hidden // 2)
    middle_grad, mixed_grad, gate_grad, up_grad, branch_grad, mlp_sums = mlp_backward(
        cot, backs, mlp, act_grad, gate, up, joined, middle, branch, mod, walked, True
    )

    def matrix_part(inputs, grads, step, before):
        term = matrix_grad(inputs, grads, step, joined.shape[0], walked).reshape(width, -1)
        term = term if walked else to_walk(term, count)
        term, *before = lax.optimization_barrier((term, *before))
        return scatter_walk(term, count), *before

    gate_up_part, down_part = matrix_part(
        [normed_two, normed_two], [gate_grad, up_grad], hidden // 2, [down_part]
    )
    flow_grad, qkv_grad, attention_sums = attention_backward(
        raw,
        values,
        mixed_grad,
        middle_grad,
        layer_in,
        mod,
        tables,
        gain,
        joined,
        walked,
        0,
        images,
        True,
    )
    mod_grad = jnp.concatenate([attention_sums[:, :2], mlp_sums], axis=1).reshape(images, -1)
    mod_all = gather_small(mod_grad.astype(bf16), count).reshape(-1, mod_grad.shape[1])
    rest_part, gate_up_part, mod_all = matrix_part(
        [normed, attended], [qkv_grad, branch_grad], width, [gate_up_part, mod_all]
    )
    flow_grad = flow_grad.reshape(images, patches, width)
    input_grads = jnp.where(first_section, flow_grad, flow_grad.astype(bf16).astype(f32))

    head_sums = jnp.sum(attention_sums[:, 2:], axis=0).reshape(2, heads, head_size)
    ada_part = dot_left(silu_rows, mod_all)
    silu_grad = dot_right(mod_all, ada_weight[0])
    silu_grad = silu_grad + lax.ppermute(silu_grad, "section", [(0, 1), (1, 0)])
    silu_all = gather_small(silu_grad, count)
    gain_all = jnp.sum(gather_small(jnp.sum(head_sums, axis=1), count), axis=0)
    silu_all = jnp.swapaxes(silu_all, 0, 1).reshape(condition.shape)
    cond_grad = silu_all * sigma_cond * (1.0 + condition * (1.0 - sigma_cond))
    table_grad = lax.dot_general(
        label_hot.astype(f32),
        cond_grad,
        (((0,), (0,)), ((), ())),
        precision=lax.Precision.HIGHEST,
        preferred_element_type=f32,
    )
    return (
        result.reshape(1, images, patches, width),
        input_grads[None],
        table_grad,
        ada_part[None],
        rest_part[None, :, : 3 * width].astype(f32),
        rest_part[None, :, 3 * width :].astype(f32),
        columns_from_walk(gate_up_part[:, :hidden], count)[None].astype(f32),
        columns_from_walk(gate_up_part[:, hidden:], count)[None].astype(f32),
        down_part[None].astype(f32),
        gain_all[None, 0],
        gain_all[None, 1],
    )


def solution(mesh):
    placed = (
        P("dp", None, None),
        P("section", "dp", None, None),
        P("dp"),
        P("dp"),
        P("dp", None),
        P(),
        P("section", "dp", None),
        P("section", "dp", None),
        P("section", "dp", None),
        P("section", "dp", None),
        P("section", "dp", None),
        P("section", "dp", None),
        P("section", None),
        P("section", None),
    )
    return jax.shard_map(
        per_device,
        mesh=mesh,
        in_specs=placed,
        out_specs=(
            P("section", "dp", None, None),
            P("section", "dp", None, None),
            P(),
            P("section", "dp", None),
            P("section", "dp", None),
            P("section", "dp", None),
            P("section", "dp", None),
            P("section", "dp", None),
            P("section", "dp", None),
            P("section", None),
            P("section", None),
        ),
        check_vma=False,
    )
```

```python
import functools
import math

import jax
import jax.numpy as jnp
from jax import lax
from jax.experimental import pallas as pl
from jax.experimental.pallas import tpu as pltpu
from jax.sharding import PartitionSpec as P

GRID = 16
epsilon = 1e-06
f32 = jnp.float32
bf16 = jnp.bfloat16
LANES = 128
VMEM_BYTES = 56 * 1024 * 1024


def params():
    return pltpu.CompilerParams(vmem_limit_bytes=VMEM_BYTES)


def cost(flops, moved):
    return pl.CostEstimate(flops=int(flops), bytes_accessed=int(moved), transcendentals=0)


def dot(left, right):
    return jnp.dot(left, right, preferred_element_type=f32)


def dot_right(left, right):
    return lax.dot_general(left, right, (((1,), (1,)), ((), ())), preferred_element_type=f32)


def dot_left(left, right):
    return lax.dot_general(left, right, (((0,), (0,)), ((), ())), preferred_element_type=f32)


def whole_rows(ref, places):
    if len(places) == 1:
        return ref[places[0]]
    return jnp.concatenate([ref[place] for place in places], axis=0)


def part_place(index, parts, walked):
    if not walked:
        return index
    return index // 2 + (index % 2) * (parts - 1 - 2 * (index // 2))


def places_of(parts, walked):
    return [part_place(index, parts, walked) for index in range(parts)]


def two_terms(values):
    high = values.astype(bf16)
    low = (values - high.astype(f32)).astype(bf16)
    return jnp.concatenate([high, low], axis=1)


def inverse_rms(values):
    return lax.rsqrt(jnp.mean(values * values, axis=-1, keepdims=True) + epsilon)


def partner(values, first_half, quarter):
    width = values.shape[1]
    return jnp.where(
        first_half, pltpu.roll(values, width - quarter, 1), pltpu.roll(values, quarter, 1)
    )


def first_half_mask(shape, quarter):
    lane = lax.broadcasted_iota(jnp.int32, shape, 1)
    return lane % (2 * quarter) < quarter


def head_groups(heads, head_size):
    width = heads * head_size
    span = min(2 * LANES, width)
    groups = []
    for head in range(heads):
        low, high = head * head_size, (head + 1) * head_size
        if groups and high <= groups[-1][0] + span:
            groups[-1][2].append(head)
        else:
            groups.append((min(low // LANES * LANES, width - span), span, [head]))
    return groups


def head_mask(head, head_size, start, span):
    lane = lax.broadcasted_iota(jnp.int32, (1, span), 1) + start
    inside = jnp.logical_and(lane >= head * head_size, lane < (head + 1) * head_size)
    return inside.astype(f32).astype(bf16)


def side_by_side(parts):
    return parts[0] if len(parts) == 1 else jnp.concatenate(parts, axis=1)


def one_above_other(parts):
    return parts[0] if len(parts) == 1 else jnp.concatenate(parts, axis=0)


def rotated(raw, part, tables, keep_scale=None):
    cos, sin, gain_ref, summing, spreading, head_size = tables
    quarter = head_size // 4
    squares = dot((raw * raw).astype(bf16), summing)
    scale = lax.rsqrt(squares * (1.0 / head_size) + epsilon)
    scale = dot(two_terms(scale), spreading)
    if keep_scale is not None:
        keep_scale[part] = scale
    scaled = raw * scale * gain_ref[part : part + 1]
    first_half = first_half_mask((1, raw.shape[1]), quarter)
    return (scaled * cos + partner(scaled, first_half, quarter) * sin).astype(bf16)


def attention_forward_kernel(heads, places, first, keep, refs):
    if keep:
        received_ref, refs = refs[0], refs[1:]
    x_ref, mod_ref, cos_ref, sin_ref, gain_ref, sum_ref, spread_ref, repeat_ref = refs[:8]
    query_weight, joined_ref = refs[8:10]
    refs = refs[10:]
    patches, width = x_ref.shape
    if keep:
        outs, refs = refs[:8], refs[8:]
        weight, mixed, sems = refs[:3]
        held, out_sems = refs[3:11], refs[11]
    else:
        middle_ref, normed_two_ref, weight, mixed, sems = refs
    head_size = width // heads

    def fetch(part):
        return pltpu.make_async_copy(
            joined_ref.at[:, :, pl.ds((part + 1) * width, width)], weight.at[part], sems.at[part]
        )

    @pl.when(pl.program_id(0) == 0)
    def _():
        for part in range(3):
            fetch(part).start()

    def arrived(part):
        @pl.when(pl.program_id(0) == 0)
        def _():
            fetch(part).wait()

        return whole_rows(weight.at[part], places)

    def put(which):
        rows = pl.ds(first * patches, patches)
        return pltpu.make_async_copy(held[which], outs[which].at[rows], out_sems.at[which])

    flow = x_ref[...].astype(f32)
    if keep:
        flow = flow + received_ref[...].astype(f32)
    mod = mod_ref[0]
    normed = (flow * inverse_rms(flow) * (1.0 + mod[1:2]) + mod[0:1]).astype(bf16)
    cos, sin = dot(cos_ref[...], repeat_ref[...]), dot(sin_ref[...], repeat_ref[...])
    tables = (cos, sin, gain_ref, sum_ref[...], spread_ref[...], head_size)
    raw = dot(normed, whole_rows(query_weight, places))
    if keep:
        held[7][...] = flow.astype(bf16)
        held[0][...] = normed
        held[1][:, :width] = raw
        put(7).start()
        put(0).start()
    queries = rotated(raw, 0, tables)
    raw = dot(normed, arrived(0))
    if keep:
        held[1][:, width:] = raw
        put(1).start()
    keys = rotated(raw, 1, tables)
    values = dot(normed, arrived(1)).astype(bf16)
    if keep:
        held[2][...] = values
        put(2).start()
    mixed[...] = jnp.zeros_like(mixed)
    factor = head_size ** (-0.5) * math.log2(math.e)
    for start, span, members in head_groups(heads, head_size):
        window = slice(start, start + span)
        probs, parts = [], []
        for head in members:
            mask = head_mask(head, head_size, start, span)
            expon = jnp.exp2(dot_right(queries[:, window], keys[:, window] * mask) * factor)
            total = jnp.sum(expon, axis=-1, keepdims=True)
            probs.append((expon * (1.0 / total)).astype(bf16))
            parts.append(values[:, window] * mask)
        mixed[:, window] += dot(side_by_side(probs), one_above_other(parts))
    attended = mixed[...].astype(bf16)
    if keep:
        held[3][...] = attended
        put(3).start()
    branch = dot(attended, arrived(2))
    middle = flow + mod[2:3] * branch
    normed_two = (middle * inverse_rms(middle) * (1.0 + mod[4:5]) + mod[3:4]).astype(bf16)
    if keep:
        for which, value in ((4, branch), (5, middle), (6, normed_two)):
            held[which][...] = value
            put(which).start()
        for which in range(8):
            put(which).wait()
    else:
        middle_ref[...] = middle
        normed_two_ref[...] = normed_two


def attention_forward(x, received, mod, tables, gain, joined, walked, first, count, made=None):
    keep = received is not None
    images, unused, width = mod.shape
    tokens = x.shape[0]
    patches = tokens // images
    heads = width // tables[-1]
    cos, sin, *matrices, unused = tables
    parts, rows, unused = joined.shape
    row = lambda columns: pl.BlockSpec((patches, columns), lambda image: (first + image, 0))
    fixed = lambda array: pl.BlockSpec(array.shape, lambda image: (0,) * array.ndim)
    anywhere = pl.BlockSpec(memory_space=pl.ANY)
    shapes = [(width, f32), (width, bf16)]
    if keep:
        shapes = [
            (width, bf16),
            (2 * width, f32),
            (width, bf16),
            (width, bf16),
            (width, f32),
            (width, f32),
            (width, bf16),
            (width, bf16),
        ]
    made = [] if made is None else list(made)
    extra = [received] if keep else []
    inputs = 10 + len(extra)
    scratch = [
        pltpu.VMEM((3, parts, rows, width), bf16),
        pltpu.VMEM((patches, width), f32),
        pltpu.SemaphoreType.DMA((3,)),
    ]
    if keep:
        scratch += [pltpu.VMEM((patches, columns), kind) for columns, kind in shapes]
        scratch += [pltpu.SemaphoreType.DMA((len(shapes),))]

    def body(*refs):
        refs = refs[:inputs] + refs[inputs + len(made) :]
        attention_forward_kernel(heads, places_of(parts, walked), first, keep, refs)

    return pl.pallas_call(
        body,
        grid=(count,),
        in_specs=[pl.BlockSpec((patches, width), lambda image: (image, 0))] * len(extra)
        + [
            row(width),
            pl.BlockSpec((1, 6, width), lambda image: (first + image, 0, 0)),
            row(cos.shape[1]),
            row(sin.shape[1]),
            fixed(gain),
        ]
        + [fixed(matrix) for matrix in matrices]
        + [pl.BlockSpec((parts, rows, width), lambda image: (0, 0, 0))]
        + [anywhere] * (1 + len(made)),
        out_specs=[anywhere if keep else row(columns) for columns, kind in shapes],
        out_shape=[jax.ShapeDtypeStruct((tokens, columns), kind) for columns, kind in shapes],
        input_output_aliases={inputs + index: index for index in range(len(made))},
        scratch_shapes=scratch,
        compiler_params=params(),
        cost_estimate=cost(
            2 * count * patches * width * (4 * width + 2 * patches),
            8 * width * width + count * patches * width * 20,
        ),
    )(*extra, x, mod, cos, sin, gain, *matrices, joined, joined, *made)


def pack_columns(matrices, pieces):
    rows = matrices[0].shape[0]
    total = sum(columns for unused, first, columns in pieces)

    def body(*refs):
        at = 0
        for which, first, columns in pieces:
            refs[-1][:, at : at + columns] = refs[which][:, first : first + columns]
            at += columns

    if any(columns % LANES or first % LANES for unused, first, columns in pieces):
        return jnp.concatenate(
            [matrices[which][:, first : first + columns] for which, first, columns in pieces], axis=1
        )
    return pl.pallas_call(
        body,
        grid=(1,),
        in_specs=whole_specs(matrices),
        out_specs=pl.BlockSpec((rows, total), lambda i: (0, 0)),
        out_shape=jax.ShapeDtypeStruct((rows, total), matrices[0].dtype),
        compiler_params=params(),
        cost_estimate=cost(0, 4 * rows * total),
    )(*matrices)


def gate_up(normed_two, joined, hidden, walked):
    tokens, width = normed_two.shape
    step = 512
    base = 4 * width // step
    count = hidden // step
    parts, rows, unused = joined.shape
    places = places_of(parts, walked)

    def body(normed_ref, gate_ref, up_ref, act_ref):
        normed = normed_ref[...]
        gate = dot(normed, whole_rows(gate_ref, places))
        up = dot(normed, whole_rows(up_ref, places))
        act_ref[...] = (gate * (1.0 / (1.0 + jnp.exp(-gate))) * up).astype(bf16)

    return pl.pallas_call(
        body,
        grid=(count,),
        in_specs=[
            pl.BlockSpec((tokens, width), lambda i: (0, 0)),
            pl.BlockSpec((parts, rows, step), lambda i: (0, 0, base + i)),
            pl.BlockSpec((parts, rows, step), lambda i: (0, 0, base + count + i)),
        ],
        out_specs=pl.BlockSpec((tokens, step), lambda i: (0, i)),
        out_shape=jax.ShapeDtypeStruct((tokens, hidden), bf16),
        compiler_params=params(),
        cost_estimate=cost(4 * tokens * width * hidden, 4 * width * hidden + 2 * tokens * hidden),
    )(normed_two, joined, joined)


def down_projection(active, act, down, middle, mod, first, count, keep, step):
    hidden = act.shape[1]
    images, unused, width = mod.shape
    patches = act.shape[0] // images
    tokens = count * patches
    outs = [jax.ShapeDtypeStruct((tokens, width), bf16)]
    scratch = [pltpu.VMEM((tokens, width), f32)]
    if keep:
        outs.append(jax.ShapeDtypeStruct((tokens, width), f32))
        scratch = []

    def body(active_ref, act_ref, middle_ref, mod_ref, down_ref, result_ref, total):
        index = pl.program_id(0)

        @pl.when(active_ref[0] == 0)
        def _():
            result_ref[...] = jnp.zeros_like(result_ref)

        @pl.when(active_ref[0] != 0)
        def _():
            term = dot(act_ref[...], down_ref[...])

            @pl.when(index == 0)
            def _():
                total[...] = term

            @pl.when(index > 0)
            def _():
                total[...] += term

            @pl.when(index == hidden // step - 1)
            def _():
                for image in range(count):
                    at = slice(image * patches, (image + 1) * patches)
                    gate = mod_ref[first + image, 5:6]
                    result_ref[at] = (middle_ref[at] + gate * total[at]).astype(bf16)

    return pl.pallas_call(
        body,
        grid_spec=pltpu.PrefetchScalarGridSpec(
            num_scalar_prefetch=1,
            grid=(hidden // step,),
            in_specs=[
                pl.BlockSpec((tokens, step), lambda i, active: (first // count, i * active[0])),
                pl.BlockSpec((tokens, width), lambda i, active: (first // count, 0)),
                pl.BlockSpec(mod.shape, lambda i, active: (0, 0, 0)),
                pl.BlockSpec((step, width), lambda i, active: (i * active[0], 0)),
            ],
            out_specs=[pl.BlockSpec((tokens, width), lambda i, active: (0, 0))] * len(outs),
            scratch_shapes=scratch,
        ),
        out_shape=outs,
        compiler_params=params(),
        cost_estimate=cost(2 * tokens * width * hidden, 2 * width * hidden + 8 * tokens * width),
    )(active, act, middle, mod, down)


def incoming(cot_ref, back_refs, image, at):
    value = cot_ref[at].astype(f32)
    return value + back_refs[image][...].astype(f32) if back_refs else value


def mlp_gradient(cot, backs, mod, first, count):
    images, unused, width = mod.shape
    patches = cot.shape[0] // images

    def body(cot_ref, mod_ref, *refs):
        for image in range(count):
            at = slice(image * patches, (image + 1) * patches)
            grads = incoming(cot_ref, refs[: len(backs)], image, at)
            refs[-1][at] = (mod_ref[first + image, 5:6] * grads).astype(bf16)

    return pl.pallas_call(
        body,
        grid=(1,),
        in_specs=[
            pl.BlockSpec((count * patches, width), lambda i: (first // count, 0)),
            pl.BlockSpec(mod.shape, lambda i: (0, 0, 0)),
        ]
        + [pl.BlockSpec((patches, width), lambda i: (0, 0))] * len(backs),
        out_specs=pl.BlockSpec((count * patches, width), lambda i: (0, 0)),
        out_shape=jax.ShapeDtypeStruct((count * patches, width), bf16),
        compiler_params=params(),
        cost_estimate=cost(0, 6 * count * patches * width),
    )(cot, mod, *backs)


def stacked(refs):
    return refs[0][...] if len(refs) == 1 else jnp.concatenate([ref[...] for ref in refs], axis=0)


def whole_specs(arrays):
    return [pl.BlockSpec(array.shape, lambda i: (0, 0)) for array in arrays]


def act_backward(mlp_grads, down, step):
    hidden, width = down.shape
    tokens = sum(grad.shape[0] for grad in mlp_grads)

    def body(*refs):
        refs[-1][...] = dot_right(stacked(refs[:-2]), refs[-2][...]).astype(bf16)

    return pl.pallas_call(
        body,
        grid=(hidden // step,),
        in_specs=whole_specs(mlp_grads) + [pl.BlockSpec((step, width), lambda i: (i, 0))],
        out_specs=pl.BlockSpec((tokens, step), lambda i: (0, i)),
        out_shape=jax.ShapeDtypeStruct((tokens, hidden), bf16),
        compiler_params=params(),
        cost_estimate=cost(2 * tokens * width * hidden, 2 * width * hidden + 4 * tokens * width),
    )(*mlp_grads, down)


def mlp_backward(cot, backs, act_grad, forward, joined, middle, mod, walked, sums_of):
    tokens, hidden = act_grad.shape
    images, unused, width = mod.shape
    patches = tokens // images
    parts, rows, unused = joined.shape
    places = places_of(parts, walked)
    step = 512
    base = 4 * width // step
    count = hidden // step
    fresh, keep = len(forward) == 1, sums_of is not None
    whole = pl.BlockSpec((tokens, width), lambda i: (0, 0))
    block = pl.BlockSpec((tokens, step), lambda i: (0, i))
    anywhere = pl.BlockSpec(memory_space=pl.ANY)
    late = [cot, middle] + (list(sums_of) if keep else [])

    def body(act_grad_ref, gate_weight_ref, up_weight_ref, mod_ref, joined_ref, *refs):
        refs = list(refs)

        def taken(number):
            first = refs[:number]
            del refs[:number]
            return first

        forward_refs, back_refs, sources = taken(len(forward)), taken(len(backs)), taken(len(late))
        middle_grad_ref, mixed_grad_ref = taken(2)
        fresh_refs = taken(3 if fresh else 0)
        kept_refs = taken(4 if keep else 0)
        total, out_weight, sem = taken(3)
        copies, (sems,) = taken(len(late)), refs
        cot_ref, middle_ref = copies[:2]
        index = pl.program_id(0)
        fetches = [
            pltpu.make_async_copy(joined_ref.at[:, :, pl.ds(3 * width, width)], out_weight, sem)
        ] + [
            pltpu.make_async_copy(source, copies[which], sems.at[which])
            for which, source in enumerate(sources)
        ]

        @pl.when(index == 0)
        def _():
            for fetch in fetches:
                fetch.start()

        gate_weight = whole_rows(gate_weight_ref, places)
        up_weight = whole_rows(up_weight_ref, places)
        if fresh:
            normed = forward_refs[0][...]
            gate, up = dot(normed, gate_weight), dot(normed, up_weight)
        else:
            gate, up = (ref[...].astype(f32) for ref in forward_refs)
        sigma = 1.0 / (1.0 + jnp.exp(-gate))
        slope = act_grad_ref[...].astype(f32) * sigma
        gate_grad = (slope * up * (1.0 + gate * (1.0 - sigma))).astype(bf16)
        up_grad = (slope * gate).astype(bf16)
        if fresh:
            fresh_refs[0][...] = (gate * sigma * up).astype(bf16)
            fresh_refs[1][...] = gate.astype(bf16)
            fresh_refs[2][...] = up.astype(bf16)
        if keep:
            kept_refs[0][...] = gate_grad
            kept_refs[1][...] = up_grad
        term = dot_right(gate_grad, gate_weight) + dot_right(up_grad, up_weight)

        @pl.when(index == 0)
        def _():
            total[...] = term

        @pl.when(index > 0)
        def _():
            total[...] += term

        @pl.when(index == count - 1)
        def _():
            for fetch in fetches:
                fetch.wait()
            matrix = whole_rows(out_weight, places)
            for image in range(images):
                at = slice(image * patches, (image + 1) * patches)
                mod = mod_ref[image]
                grad, flow = total[at], middle_ref[at]
                inverse = inverse_rms(flow)
                normal = flow * inverse
                scaled = grad * (1.0 + mod[4:5])
                mean = jnp.mean(scaled * normal, axis=-1, keepdims=True)
                out_grad = incoming(cot_ref, back_refs, image, at)
                middle_grad = out_grad + (scaled - normal * mean) * inverse
                middle_grad_ref[at] = middle_grad
                branch_grad = (mod[2:3] * middle_grad).astype(bf16)
                mixed_grad_ref[at] = dot_right(branch_grad, matrix).astype(bf16)
                if keep:
                    mlp_ref, branch_ref = copies[2:]
                    kept_refs[2][at] = branch_grad
                    terms = [middle_grad * branch_ref[at], grad, grad * normal, out_grad * mlp_ref[at]]
                    for place, value in enumerate(terms):
                        kept_refs[3][image, place : place + 1] = jnp.sum(value, axis=0, keepdims=True)

    out_shapes = [
        jax.ShapeDtypeStruct((tokens, width), f32),
        jax.ShapeDtypeStruct((tokens, width), bf16),
    ]
    out_specs = [whole, whole]
    if fresh:
        out_shapes += [jax.ShapeDtypeStruct((tokens, hidden), bf16)] * 3
        out_specs += [block] * 3
    if keep:
        out_shapes += [jax.ShapeDtypeStruct((tokens, hidden), bf16)] * 2
        out_shapes += [jax.ShapeDtypeStruct((tokens, width), bf16)]
        out_shapes += [jax.ShapeDtypeStruct((images, 4, width), f32)]
        out_specs += [block, block, whole, pl.BlockSpec((images, 4, width), lambda i: (0, 0, 0))]
    return pl.pallas_call(
        body,
        grid=(count,),
        in_specs=[
            block,
            pl.BlockSpec((parts, rows, step), lambda i: (0, 0, base + i)),
            pl.BlockSpec((parts, rows, step), lambda i: (0, 0, base + count + i)),
            pl.BlockSpec(mod.shape, lambda i: (0, 0, 0)),
            anywhere,
        ]
        + [whole if fresh else block] * len(forward)
        + [pl.BlockSpec((patches, width), lambda i: (0, 0))] * len(backs)
        + [anywhere] * len(late),
        out_specs=out_specs,
        out_shape=out_shapes,
        scratch_shapes=[
            pltpu.VMEM((tokens, width), f32),
            pltpu.VMEM((parts, rows, width), bf16),
            pltpu.SemaphoreType.DMA,
        ]
        + [pltpu.VMEM(array.shape, array.dtype) for array in late]
        + [pltpu.SemaphoreType.DMA((len(late),))],
        compiler_params=params(),
        cost_estimate=cost(
            2 * tokens * width * (4 * hidden + width), 4 * width * hidden + 6 * tokens * hidden
        ),
    )(act_grad, joined, joined, mod, joined, *forward, *backs, *late)


def attention_backward_kernel(heads, places, first, keep, refs):
    raw_hbm, value_hbm, mixed_grad_hbm, middle_grad_hbm, x_hbm = refs[:5]
    mod_ref, cos_ref, sin_ref, gain_ref, sum_ref, spread_ref, repeat_ref, joined_ref = refs[5:13]
    refs = refs[13:]
    if keep:
        flow_grad_ref, qkv_grad_ref, sums_ref = refs[:3]
        refs = refs[3:]
    else:
        back_ref = refs[0]
        refs = refs[1:]
    weight, scales, query_total, key_total, value_total = refs[:5]
    raw_ref, value_ref, mixed_grad_ref, middle_grad_ref, x_ref, sems = refs[5:]
    patches, width = x_ref.shape
    head_size = width // heads
    quarter = head_size // 4
    factor = head_size ** (-0.5)
    image = pl.program_id(0)
    rows = pl.ds((first + image) * patches, patches)
    sources = [
        raw_hbm.at[rows, pl.ds(0, width)],
        raw_hbm.at[rows, pl.ds(width, width)],
        value_hbm.at[rows],
        mixed_grad_hbm.at[rows],
        middle_grad_hbm.at[rows],
        x_hbm.at[rows],
    ]
    targets = [raw_ref.at[0], raw_ref.at[1], value_ref, mixed_grad_ref, middle_grad_ref, x_ref]
    copies = [
        pltpu.make_async_copy(source, target, sems.at[3 + which])
        for which, (source, target) in enumerate(zip(sources, targets))
    ]
    for copy in copies[:4]:
        copy.start()

    def fetch(part):
        return pltpu.make_async_copy(
            joined_ref.at[:, :, pl.ds(part * width, width)], weight.at[part], sems.at[part]
        )

    @pl.when(image == 0)
    def _():
        for part in range(3):
            fetch(part).start()

    for copy in copies[4:]:
        copy.start()
    first_half = first_half_mask((1, width), quarter)
    cos, sin = dot(cos_ref[...], repeat_ref[...]), dot(sin_ref[...], repeat_ref[...])
    summing, spreading = sum_ref[...], spread_ref[...]
    tables = (cos, sin, gain_ref, summing, spreading, head_size)
    copies[0].wait()
    queries = rotated(raw_ref[0], 0, tables, scales)
    copies[1].wait()
    keys = rotated(raw_ref[1], 1, tables, scales)
    for copy in copies[2:4]:
        copy.wait()
    values, mixed_grad = value_ref[...], mixed_grad_ref[...]
    query_total[...] = jnp.zeros_like(query_total)
    key_total[...] = jnp.zeros_like(key_total)
    value_total[...] = jnp.zeros_like(value_total)
    for start, span, members in head_groups(heads, head_size):
        window = slice(start, start + span)
        probs, slopes, key_parts, query_parts, grad_parts = [], [], [], [], []
        for head in members:
            mask = head_mask(head, head_size, start, span)
            key_part, query_part = keys[:, window] * mask, queries[:, window] * mask
            grad_part = mixed_grad[:, window] * mask
            scores = dot_right(key_part, queries[:, window])
            expon = jnp.exp2(scores * (factor * math.log2(math.e)))
            prob = expon * (1.0 / jnp.sum(expon, axis=0, keepdims=True))
            prob_grad = dot_right(values[:, window], grad_part)
            middle = jnp.sum(prob * prob_grad, axis=0, keepdims=True)
            probs.append(prob.astype(bf16))
            slopes.append((prob * (prob_grad - middle)).astype(bf16))
            key_parts.append(key_part)
            query_parts.append(query_part)
            grad_parts.append(grad_part)
        value_total[:, window] += dot(side_by_side(probs), one_above_other(grad_parts))
        key_total[:, window] += dot(side_by_side(slopes), one_above_other(query_parts))
        query_total[:, window] += dot_left(one_above_other(slopes), one_above_other(key_parts))

    def raw_grad(part, total):
        turned = total[...] * factor
        grad = turned * cos + partner(turned * sin, first_half, quarter)
        scale = scales[part]
        normal = raw_ref[part] * scale
        if keep:
            sums_ref[0, 2 + part : 3 + part] = jnp.sum(grad * normal, axis=0, keepdims=True)
        grad = grad * gain_ref[part : part + 1]
        mean = dot((grad * normal).astype(bf16), summing) * (1.0 / head_size)
        mean = dot(two_terms(mean), spreading)
        return (scale * (grad - normal * mean)).astype(bf16)

    def arrived(part):
        @pl.when(image == 0)
        def _():
            fetch(part).wait()

        return whole_rows(weight.at[part], places)

    parts = [raw_grad(0, query_total), raw_grad(1, key_total), value_total[...].astype(bf16)]
    grad = None
    for part in range(3):
        if keep:
            qkv_grad_ref[:, part * width : (part + 1) * width] = parts[part]
        term = dot_right(parts[part], arrived(part))
        grad = term if grad is None else grad + term
    for copy in copies[4:]:
        copy.wait()
    mod = mod_ref[0]
    flow = x_ref[...].astype(f32)
    inverse = inverse_rms(flow)
    normal = flow * inverse
    scaled = grad * (1.0 + mod[1:2])
    mean = jnp.mean(scaled * normal, axis=-1, keepdims=True)
    flow_grad = middle_grad_ref[...] + (scaled - normal * mean) * inverse
    if keep:
        flow_grad_ref[...] = flow_grad
        sums_ref[0, 0:1] = jnp.sum(grad, axis=0, keepdims=True)
        sums_ref[0, 1:2] = jnp.sum(grad * normal, axis=0, keepdims=True)
    else:
        back_ref[...] = flow_grad.astype(bf16)


def attention_backward(
    raw, value, mixed_grad, middle_grad, x, mod, tables, gain, joined, walked, first, count, keep
):
    images, unused, width = mod.shape
    patches = x.shape[0] // images
    tokens = count * patches
    heads = width // tables[-1]
    cos, sin, *matrices, unused = tables
    parts, rows, unused = joined.shape
    row = lambda columns: pl.BlockSpec((patches, columns), lambda image: (first + image, 0))
    token = lambda columns: pl.BlockSpec((patches, columns), lambda image: (image, 0))
    fixed = lambda array: pl.BlockSpec(array.shape, lambda image: (0,) * array.ndim)
    anywhere = pl.BlockSpec(memory_space=pl.ANY)
    out_shapes = [jax.ShapeDtypeStruct((tokens, width), bf16)]
    out_specs = [token(width)]
    if keep:
        out_shapes = [
            jax.ShapeDtypeStruct((tokens, width), f32),
            jax.ShapeDtypeStruct((tokens, 3 * width), bf16),
            jax.ShapeDtypeStruct((count, 4, width), f32),
        ]
        out_specs = [
            token(width),
            token(3 * width),
            pl.BlockSpec((1, 4, width), lambda image: (image, 0, 0)),
        ]

    def body(*refs):
        attention_backward_kernel(heads, places_of(parts, walked), first, keep, refs)

    return pl.pallas_call(
        body,
        grid=(count,),
        in_specs=[anywhere] * 5
        + [
            pl.BlockSpec((1, 6, width), lambda image: (first + image, 0, 0)),
            row(cos.shape[1]),
            row(sin.shape[1]),
            fixed(gain),
        ]
        + [fixed(matrix) for matrix in matrices]
        + [anywhere],
        out_specs=out_specs,
        out_shape=out_shapes,
        scratch_shapes=[
            pltpu.VMEM((3, parts, rows, width), bf16),
            pltpu.VMEM((2, patches, width), f32),
            pltpu.VMEM((patches, width), f32),
            pltpu.VMEM((patches, width), f32),
            pltpu.VMEM((patches, width), f32),
            pltpu.VMEM((2, patches, width), f32),
            pltpu.VMEM((patches, width), bf16),
            pltpu.VMEM((patches, width), bf16),
            pltpu.VMEM((patches, width), f32),
            pltpu.VMEM((patches, width), bf16),
            pltpu.SemaphoreType.DMA((9,)),
        ],
        compiler_params=params(),
        cost_estimate=cost(
            2 * tokens * width * (3 * width + 5 * patches),
            6 * width * width + tokens * width * 20,
        ),
    )(raw, value, mixed_grad, middle_grad, x, mod, cos, sin, gain, *matrices, joined)


def down_grad(mlp_grads, cot, back, act, mod, step):
    tokens, hidden = act.shape
    images, unused, width = mod.shape
    patches = tokens // images
    last = images - 1

    def body(act_ref, cot_ref, back_ref, mod_ref, *refs):
        given, (out_ref, last_ref, mlp_grad) = refs[:last], refs[last:]

        @pl.when(pl.program_id(0) == 0)
        def _():
            grads = incoming(cot_ref, [back_ref], 0, slice(0, patches))
            value = (mod_ref[last, 5:6] * grads).astype(bf16)
            last_ref[...] = value
            for image in range(last):
                mlp_grad[image * patches : (image + 1) * patches] = given[image][...]
            mlp_grad[last * patches :] = value

        out_ref[...] = dot_left(act_ref[...], mlp_grad[...]).astype(bf16)

    return pl.pallas_call(
        body,
        grid=(hidden // step,),
        in_specs=[
            pl.BlockSpec((tokens, step), lambda i: (0, i)),
            pl.BlockSpec((patches, width), lambda i: (last, 0)),
            pl.BlockSpec((patches, width), lambda i: (0, 0)),
            pl.BlockSpec(mod.shape, lambda i: (0, 0, 0)),
        ]
        + whole_specs(mlp_grads),
        out_specs=[
            pl.BlockSpec((step, width), lambda i: (i, 0)),
            pl.BlockSpec((patches, width), lambda i: (0, 0)),
        ],
        out_shape=[
            jax.ShapeDtypeStruct((hidden, width), bf16),
            jax.ShapeDtypeStruct((patches, width), bf16),
        ],
        scratch_shapes=[pltpu.VMEM((tokens, width), bf16)],
        compiler_params=params(),
        cost_estimate=cost(2 * tokens * width * hidden, 2 * width * hidden),
    )(act, cot, back, mod, *mlp_grads)


def matrix_grad_kernel(places, counts, *refs):
    pairs = len(counts)
    inputs, grads, out_ref = refs[:pairs], refs[pairs : 2 * pairs], refs[2 * pairs]
    rows = out_ref.shape[1]
    step = pl.program_id(0)
    first = 0
    for index in range(pairs):

        @pl.when(jnp.logical_and(step >= first, step < first + counts[index]))
        def _(index=index):
            product = dot_left(inputs[index][...], grads[index][...]).astype(bf16)
            for part, place in enumerate(places):
                out_ref[place] = product[part * rows : (part + 1) * rows]

        first += counts[index]


def matrix_grad(inputs, grads, step, parts, walked):
    tokens, width = inputs[0].shape
    counts = [grad.shape[1] // step for grad in grads]
    columns = sum(counts) * step
    rows = width // parts
    firsts = [sum(counts[:index]) for index in range(len(counts))]

    def grad_spec(first, count):
        return pl.BlockSpec((tokens, step), lambda i: (0, jnp.clip(i - first, 0, count - 1)))

    return pl.pallas_call(
        functools.partial(matrix_grad_kernel, places_of(parts, walked), counts),
        grid=(sum(counts),),
        in_specs=[pl.BlockSpec((tokens, width), lambda i: (0, 0))] * len(inputs)
        + [grad_spec(first, count) for first, count in zip(firsts, counts)],
        out_specs=pl.BlockSpec((parts, rows, step), lambda i: (0, 0, i)),
        out_shape=jax.ShapeDtypeStruct((parts, rows, columns), bf16),
        compiler_params=params(),
        cost_estimate=cost(2 * tokens * width * columns, 2 * width * columns),
    )(*inputs, *grads)


def walk_of(count):
    chips = count // 2
    order = [chip for chip in range(chips) if chip % 2 == 0]
    order += [chip for chip in reversed(range(chips)) if chip % 2 == 1]
    return [2 * chip + core for chip in order for core in (0, 1)]


def from_walk(rows, count):
    blocks = rows.reshape(count // 2, -1, rows.shape[-1])
    places = places_of(count // 2, True)
    return jnp.concatenate([blocks[place] for place in places], axis=0)


def walk_columns(which, columns, count):
    each = columns // (count // 2)
    return [(which, device // 2 * each, each) for device in walk_of(count)[::2]]


def columns_from_walk(matrix, count):
    each = matrix.shape[1] // (count // 2)
    places = places_of(count // 2, True)
    return jnp.concatenate(
        [matrix[:, place * each : (place + 1) * each] for place in places], axis=1
    )


def to_walk(rows, count):
    blocks = rows.reshape(count // 2, -1, rows.shape[-1])
    return jnp.concatenate([blocks[device // 2] for device in walk_of(count)[::2]], axis=0)


def gather_walk(rows, count):
    return lax.all_gather(rows, "dp", axis=0, tiled=True, axis_index_groups=[walk_of(count)])


def scatter_walk(rows, count):
    part = lax.psum_scatter(
        rows, "dp", scatter_dimension=0, tiled=True, axis_index_groups=[walk_of(count)]
    )
    return lax.optimization_barrier(part)


def as_parts(rows, count):
    each = rows.shape[0] // (count // 2)
    if each % 16 == 0:
        return rows.reshape(count // 2, each, rows.shape[1]), True
    whole = from_walk(rows, count)
    return whole[None], False


def swapped(block, bit, count):
    return lax.ppermute(block, "dp", [(device, device ^ bit) for device in range(count)])


def gather_small(block, count):
    me = lax.axis_index("dp")
    block = block[None]
    bit = count // 2
    while bit:
        other = swapped(block, bit, count)
        low = (me & bit) == 0
        pair = [jnp.where(low, block, other), jnp.where(low, other, block)]
        block = jnp.stack(pair, axis=1).reshape(2 * block.shape[0], *block.shape[1:])
        bit //= 2
    return block


def scatter_small(blocks, count):
    me = lax.axis_index("dp")
    bit = 1
    while bit < count:
        pairs = blocks.reshape(blocks.shape[0] // 2, 2, *blocks.shape[1:])
        mine = jnp.where((me & bit) == 0, 0, 1)
        give = lax.dynamic_index_in_dim(pairs, 1 - mine, 1, keepdims=False)
        keep = lax.dynamic_index_in_dim(pairs, mine, 1, keepdims=False)
        blocks = keep + swapped(give, bit, count)
        bit *= 2
    return blocks[0]


def time_features(timestep_ids, width):
    half_width = width // 2
    frequency = jnp.exp(-math.log(10000.0) * jnp.arange(half_width, dtype=f32) / half_width)
    angle_rows = timestep_ids.astype(f32)[:, None] * frequency[None, :]
    return jnp.concatenate([jnp.cos(angle_rows), jnp.sin(angle_rows)], axis=-1)


def rotation_tables(positions, width, head_size):
    quarter = head_size // 4
    frequency = jnp.exp(-math.log(10000.0) * jnp.arange(quarter, dtype=f32) / quarter)
    places = positions.reshape(-1, 1)
    row_angle = (places // GRID).astype(f32) * frequency
    col_angle = (places % GRID).astype(f32) * frequency
    row_cos, row_sin = jnp.cos(row_angle), jnp.sin(row_angle)
    col_cos, col_sin = jnp.cos(col_angle), jnp.sin(col_angle)
    cos = jnp.concatenate([row_cos, row_cos, col_cos, col_cos], axis=1)
    sin = jnp.concatenate([-row_sin, row_sin, -col_sin, col_sin], axis=1)
    padding = ((0, 0), (0, LANES - head_size))
    number = jnp.arange(LANES)
    column = jnp.arange(width)
    summing = (column[:, None] // head_size == number[None, :]).astype(bf16)
    spreading = (column[None, :] // head_size == number[:, None]).astype(bf16)
    repeating = (column[None, :] % head_size == number[:, None]).astype(bf16)
    return (
        two_terms(jnp.pad(cos, padding)),
        two_terms(jnp.pad(sin, padding)),
        summing,
        jnp.concatenate([spreading, spreading]),
        jnp.concatenate([repeating, repeating]),
    )


def per_device(
    tokens,
    cotangent,
    labels,
    timesteps,
    positions,
    label_table,
    ada_weight,
    qkv_weight,
    out_weight,
    gate_weight,
    up_weight,
    down_weight,
    q_gain,
    k_gain,
):
    first_section = lax.axis_index("section") == 0
    first_only = first_section.astype(jnp.int32).reshape(1)
    always = jnp.ones((1,), jnp.int32)
    count = lax.axis_size("dp")
    me = lax.axis_index("dp")
    images, patches, width = tokens.shape
    hidden = gate_weight.shape[2]
    head_size = q_gain.shape[1]
    heads = width // head_size
    rows = ada_weight.shape[1]
    classes = label_table.shape[0]

    pieces = [(0, 0, 3 * width), (1, 0, width)]
    pieces += walk_columns(2, hidden, count) + walk_columns(3, hidden, count)
    joined = gather_walk(
        pack_columns([qkv_weight[0], out_weight[0], gate_weight[0], up_weight[0]], pieces), count
    )

    ids = gather_small(jnp.stack([labels, timesteps]), count)
    all_labels = ids[:, 0].reshape(-1)
    all_times = ids[:, 1].reshape(-1)
    label_hot = all_labels[:, None] == jnp.arange(classes, dtype=jnp.int32)[None, :]
    condition = dot(label_hot.astype(bf16), label_table) + time_features(all_times, width)
    sigma_cond = jax.nn.sigmoid(condition)
    silu_cond = (condition * sigma_cond).astype(bf16)
    silu_rows = lax.dynamic_slice_in_dim(silu_cond, me * rows, rows, 1)
    mod_part = dot(silu_rows, ada_weight[0])
    mod = scatter_small(mod_part.reshape(count, images, -1), count).reshape(images, 6, width)
    tables = rotation_tables(positions, width, head_size)
    flat = tokens.reshape(images * patches, width)
    own = jnp.where(first_section, flat, jnp.zeros_like(flat))

    down, joined, mod, own, tables = lax.optimization_barrier(
        (down_weight[0], joined, mod, own, tables)
    )
    down = gather_walk(down, count)
    joined, walked = as_parts(joined, count)
    tables = (*tables, head_size)
    gain = jnp.tile(jnp.concatenate([q_gain, k_gain]), (1, heads))

    cot = cotangent[0].reshape(images * patches, width)
    middle, normed_two = attention_forward(
        flat, None, mod, tables, gain, joined, walked, 0, images
    )
    act = gate_up(normed_two, joined, hidden, walked)
    received = []
    for image in range(images):
        (early,) = down_projection(
            first_only, act, down, middle, mod, image, 1, False, hidden // 2
        )
        received.append(lax.ppermute(early, "section", [(0, 1)]))
    mlp_grad, unused = lax.optimization_barrier((mlp_gradient(cot, [], mod, 0, images), early))
    mlp_grads = [mlp_grad]
    act_grad = act_backward(mlp_grads, down, hidden // 2)
    kept = None
    for image in range(images):
        kept = attention_forward(
            own, received[image], mod, tables, gain, joined, walked, image, 1, kept
        )
    normed, raw, values, attended, branch, middle, normed_two, layer_in = kept

    middle_grad, mixed_grad, act, gate, up = mlp_backward(
        cot, [], act_grad, [normed_two], joined, middle, mod, walked, None
    )
    backs = []
    for image in range(images):
        (early,) = attention_backward(
            raw,
            values,
            mixed_grad,
            middle_grad,
            layer_in,
            mod,
            tables,
            gain,
            joined,
            walked,
            image,
            1,
            False,
        )
        backs.append(lax.ppermute(early, "section", [(1, 0)]))
    late_act, unused = lax.optimization_barrier((act, early))
    result, mlp = down_projection(
        always, late_act, down, middle, mod, 0, images, True, hidden // 2
    )

    late_cot, unused = lax.optimization_barrier((cot, mlp))
    mlp_grads = [
        mlp_gradient(late_cot, [back], mod, image, 1) for image, back in enumerate(backs[:-1])
    ]
    down_term, mlp_grad = down_grad(mlp_grads, late_cot, backs[-1], act, mod, hidden // 4)
    mlp_grads = [*mlp_grads, mlp_grad]
    down_term, mlp_grads = lax.optimization_barrier((down_term, mlp_grads))
    down_part = scatter_walk(down_term, count)
    act_grad = act_backward(mlp_grads, down, hidden // 2)
    middle_grad, mixed_grad, gate_grad, up_grad, branch_grad, mlp_sums = mlp_backward(
        cot, backs, act_grad, [gate, up], joined, middle, mod, walked, [mlp, branch]
    )

    def matrix_part(inputs, grads, step, before):
        term = matrix_grad(inputs, grads, step, joined.shape[0], walked).reshape(width, -1)
        term = term if walked else to_walk(term, count)
        term, *before = lax.optimization_barrier((term, *before))
        return scatter_walk(term, count), *before

    gate_up_part, down_part = matrix_part(
        [normed_two, normed_two], [gate_grad, up_grad], hidden // 2, [down_part]
    )
    flow_grad, qkv_grad, attention_sums = attention_backward(
        raw,
        values,
        mixed_grad,
        middle_grad,
        layer_in,
        mod,
        tables,
        gain,
        joined,
        walked,
        0,
        images,
        True,
    )
    mod_grad = jnp.concatenate([attention_sums[:, :2], mlp_sums], axis=1).reshape(images, -1)
    mod_all = gather_small(mod_grad.astype(bf16), count).reshape(-1, mod_grad.shape[1])
    rest_part, gate_up_part, mod_all = matrix_part(
        [normed, attended], [qkv_grad, branch_grad], width, [gate_up_part, mod_all]
    )
    flow_grad = flow_grad.reshape(images, patches, width)
    input_grads = jnp.where(first_section, flow_grad, flow_grad.astype(bf16).astype(f32))

    head_sums = jnp.sum(attention_sums[:, 2:], axis=0).reshape(2, heads, head_size)
    ada_part = dot_left(silu_rows, mod_all)
    silu_grad = dot_right(mod_all, ada_weight[0])
    silu_grad = silu_grad + lax.ppermute(silu_grad, "section", [(0, 1), (1, 0)])
    silu_all = gather_small(silu_grad, count)
    gain_all = jnp.sum(gather_small(jnp.sum(head_sums, axis=1), count), axis=0)
    silu_all = jnp.swapaxes(silu_all, 0, 1).reshape(condition.shape)
    cond_grad = silu_all * sigma_cond * (1.0 + condition * (1.0 - sigma_cond))
    table_grad = lax.dot_general(
        label_hot.astype(f32),
        cond_grad,
        (((0,), (0,)), ((), ())),
        precision=lax.Precision.HIGHEST,
        preferred_element_type=f32,
    )
    return (
        result.reshape(1, images, patches, width),
        input_grads[None],
        table_grad,
        ada_part[None],
        rest_part[None, :, : 3 * width].astype(f32),
        rest_part[None, :, 3 * width :].astype(f32),
        columns_from_walk(gate_up_part[:, :hidden], count)[None].astype(f32),
        columns_from_walk(gate_up_part[:, hidden:], count)[None].astype(f32),
        down_part[None].astype(f32),
        gain_all[None, 0],
        gain_all[None, 1],
    )


def solution(mesh):
    placed = (
        P("dp", None, None),
        P("section", "dp", None, None),
        P("dp"),
        P("dp"),
        P("dp", None),
        P(),
        P("section", "dp", None),
        P("section", "dp", None),
        P("section", "dp", None),
        P("section", "dp", None),
        P("section", "dp", None),
        P("section", "dp", None),
        P("section", None),
        P("section", None),
    )
    return jax.shard_map(
        per_device,
        mesh=mesh,
        in_specs=placed,
        out_specs=(
            P("section", "dp", None, None),
            P("section", "dp", None, None),
            P(),
            P("section", "dp", None),
            P("section", "dp", None),
            P("section", "dp", None),
            P("section", "dp", None),
            P("section", "dp", None),
            P("section", "dp", None),
            P("section", None),
            P("section", None),
        ),
        check_vma=False,
    )
```

```python
import functools
import math

import jax
import jax.numpy as jnp
from jax import lax
from jax.experimental import pallas as pl
from jax.experimental.pallas import tpu as pltpu
from jax.sharding import PartitionSpec as P

GRID = 16
epsilon = 1e-06
f32 = jnp.float32
bf16 = jnp.bfloat16
LANES = 128
VMEM_BYTES = 56 * 1024 * 1024


def params():
    return pltpu.CompilerParams(vmem_limit_bytes=VMEM_BYTES)


def cost(flops, moved):
    return pl.CostEstimate(flops=int(flops), bytes_accessed=int(moved), transcendentals=0)


def dot(left, right):
    return jnp.dot(left, right, preferred_element_type=f32)


def dot_right(left, right):
    return lax.dot_general(left, right, (((1,), (1,)), ((), ())), preferred_element_type=f32)


def dot_left(left, right):
    return lax.dot_general(left, right, (((0,), (0,)), ((), ())), preferred_element_type=f32)


def whole_rows(ref, places):
    if len(places) == 1:
        return ref[places[0]]
    return jnp.concatenate([ref[place] for place in places], axis=0)


def part_place(index, parts, walked):
    if not walked:
        return index
    return index // 2 + (index % 2) * (parts - 1 - 2 * (index // 2))


def places_of(parts, walked):
    return [part_place(index, parts, walked) for index in range(parts)]


def two_terms(values):
    high = values.astype(bf16)
    low = (values - high.astype(f32)).astype(bf16)
    return jnp.concatenate([high, low], axis=1)


def inverse_rms(values):
    return lax.rsqrt(jnp.mean(values * values, axis=-1, keepdims=True) + epsilon)


def partner(values, first_half, quarter):
    width = values.shape[1]
    return jnp.where(
        first_half, pltpu.roll(values, width - quarter, 1), pltpu.roll(values, quarter, 1)
    )


def first_half_mask(shape, quarter):
    lane = lax.broadcasted_iota(jnp.int32, shape, 1)
    return lane % (2 * quarter) < quarter


def head_groups(heads, head_size):
    width = heads * head_size
    span = min(2 * LANES, width)
    groups = []
    for head in range(heads):
        low, high = head * head_size, (head + 1) * head_size
        if groups and high <= groups[-1][0] + span:
            groups[-1][2].append(head)
        else:
            groups.append((min(low // LANES * LANES, width - span), span, [head]))
    return groups


def head_mask(head, head_size, start, span):
    lane = lax.broadcasted_iota(jnp.int32, (1, span), 1) + start
    inside = jnp.logical_and(lane >= head * head_size, lane < (head + 1) * head_size)
    return inside.astype(f32).astype(bf16)


def side_by_side(parts):
    return parts[0] if len(parts) == 1 else jnp.concatenate(parts, axis=1)


def one_above_other(parts):
    return parts[0] if len(parts) == 1 else jnp.concatenate(parts, axis=0)


def rotated(raw, part, tables, keep_scale=None):
    cos, sin, gain_ref, summing, spreading, head_size = tables
    quarter = head_size // 4
    squares = dot((raw * raw).astype(bf16), summing)
    scale = lax.rsqrt(squares * (1.0 / head_size) + epsilon)
    scale = dot(two_terms(scale), spreading)
    if keep_scale is not None:
        keep_scale[part] = scale
    scaled = raw * scale * gain_ref[part : part + 1]
    first_half = first_half_mask((1, raw.shape[1]), quarter)
    return (scaled * cos + partner(scaled, first_half, quarter) * sin).astype(bf16)


def attention_forward_kernel(heads, places, first, keep, refs):
    if keep:
        received_ref, refs = refs[0], refs[1:]
    x_ref, mod_ref, cos_ref, sin_ref, gain_ref, sum_ref, spread_ref, repeat_ref = refs[:8]
    query_weight, joined_ref = refs[8:10]
    refs = refs[10:]
    patches, width = x_ref.shape
    if keep:
        outs, refs = refs[:8], refs[8:]
        weight, mixed, sems = refs[:3]
        held, out_sems = refs[3:11], refs[11]
    else:
        middle_ref, normed_two_ref, weight, mixed, sems = refs
    head_size = width // heads

    def fetch(part):
        return pltpu.make_async_copy(
            joined_ref.at[:, :, pl.ds((part + 1) * width, width)], weight.at[part], sems.at[part]
        )

    @pl.when(pl.program_id(0) == 0)
    def _():
        for part in range(3):
            fetch(part).start()

    def arrived(part):
        @pl.when(pl.program_id(0) == 0)
        def _():
            fetch(part).wait()

        return whole_rows(weight.at[part], places)

    def put(which):
        rows = pl.ds(first * patches, patches)
        return pltpu.make_async_copy(held[which], outs[which].at[rows], out_sems.at[which])

    flow = x_ref[...].astype(f32)
    if keep:
        flow = flow + received_ref[...].astype(f32)
    mod = mod_ref[0]
    normed = (flow * inverse_rms(flow) * (1.0 + mod[1:2]) + mod[0:1]).astype(bf16)
    cos, sin = dot(cos_ref[...], repeat_ref[...]), dot(sin_ref[...], repeat_ref[...])
    tables = (cos, sin, gain_ref, sum_ref[...], spread_ref[...], head_size)
    raw = dot(normed, whole_rows(query_weight, places))
    if keep:
        held[7][...] = flow.astype(bf16)
        held[0][...] = normed
        held[1][:, :width] = raw
        put(7).start()
        put(0).start()
    queries = rotated(raw, 0, tables)
    raw = dot(normed, arrived(0))
    if keep:
        held[1][:, width:] = raw
        put(1).start()
    keys = rotated(raw, 1, tables)
    values = dot(normed, arrived(1)).astype(bf16)
    if keep:
        held[2][...] = values
        put(2).start()
    mixed[...] = jnp.zeros_like(mixed)
    factor = head_size ** (-0.5) * math.log2(math.e)
    for start, span, members in head_groups(heads, head_size):
        window = slice(start, start + span)
        probs, parts = [], []
        for head in members:
            mask = head_mask(head, head_size, start, span)
            expon = jnp.exp2(dot_right(queries[:, window], keys[:, window] * mask) * factor)
            total = jnp.sum(expon, axis=-1, keepdims=True)
            probs.append((expon * (1.0 / total)).astype(bf16))
            parts.append(values[:, window] * mask)
        mixed[:, window] += dot(side_by_side(probs), one_above_other(parts))
    attended = mixed[...].astype(bf16)
    if keep:
        held[3][...] = attended
        put(3).start()
    branch = dot(attended, arrived(2))
    middle = flow + mod[2:3] * branch
    normed_two = (middle * inverse_rms(middle) * (1.0 + mod[4:5]) + mod[3:4]).astype(bf16)
    if keep:
        for which, value in ((4, branch), (5, middle), (6, normed_two)):
            held[which][...] = value
            put(which).start()
        for which in range(8):
            put(which).wait()
    else:
        middle_ref[...] = middle
        normed_two_ref[...] = normed_two


def attention_forward(x, received, mod, tables, gain, joined, walked, first, count, made=None):
    keep = received is not None
    images, unused, width = mod.shape
    tokens = x.shape[0]
    patches = tokens // images
    heads = width // tables[-1]
    cos, sin, *matrices, unused = tables
    parts, rows, unused = joined.shape
    row = lambda columns: pl.BlockSpec((patches, columns), lambda image: (first + image, 0))
    fixed = lambda array: pl.BlockSpec(array.shape, lambda image: (0,) * array.ndim)
    anywhere = pl.BlockSpec(memory_space=pl.ANY)
    shapes = [(width, f32), (width, bf16)]
    if keep:
        shapes = [
            (width, bf16),
            (2 * width, f32),
            (width, bf16),
            (width, bf16),
            (width, f32),
            (width, f32),
            (width, bf16),
            (width, bf16),
        ]
    made = [] if made is None else list(made)
    extra = [received] if keep else []
    inputs = 10 + len(extra)
    scratch = [
        pltpu.VMEM((3, parts, rows, width), bf16),
        pltpu.VMEM((patches, width), f32),
        pltpu.SemaphoreType.DMA((3,)),
    ]
    if keep:
        scratch += [pltpu.VMEM((patches, columns), kind) for columns, kind in shapes]
        scratch += [pltpu.SemaphoreType.DMA((len(shapes),))]

    def body(*refs):
        refs = refs[:inputs] + refs[inputs + len(made) :]
        attention_forward_kernel(heads, places_of(parts, walked), first, keep, refs)

    return pl.pallas_call(
        body,
        grid=(count,),
        in_specs=[pl.BlockSpec((patches, width), lambda image: (image, 0))] * len(extra)
        + [
            row(width),
            pl.BlockSpec((1, 8, width), lambda image: (first + image, 0, 0)),
            row(cos.shape[1]),
            row(sin.shape[1]),
            fixed(gain),
        ]
        + [fixed(matrix) for matrix in matrices]
        + [pl.BlockSpec((parts, rows, width), lambda image: (0, 0, 0))]
        + [anywhere] * (1 + len(made)),
        out_specs=[anywhere if keep else row(columns) for columns, kind in shapes],
        out_shape=[jax.ShapeDtypeStruct((tokens, columns), kind) for columns, kind in shapes],
        input_output_aliases={inputs + index: index for index in range(len(made))},
        scratch_shapes=scratch,
        compiler_params=params(),
        cost_estimate=cost(
            2 * count * patches * width * (4 * width + 2 * patches),
            8 * width * width + count * patches * width * 20,
        ),
    )(*extra, x, mod, cos, sin, gain, *matrices, joined, joined, *made)


def walk_chip(place, chips):
    return jnp.where(place < chips // 2, 2 * place, 2 * (chips - 1 - place) + 1)


def column_specs(joined, first, hidden, chips, step):
    parts, rows, unused = joined.shape
    if not chips:
        return [pl.BlockSpec((parts, rows, step), lambda i: (0, 0, first // step + i))]
    each = hidden // chips
    number = step // each

    def spec(which):
        return pl.BlockSpec(
            (parts, rows, each),
            lambda i: (0, 0, first // each + walk_chip(i * number + which, chips)),
        )

    return [spec(which) for which in range(number)]


def step_matrix(refs, places):
    return side_by_side([whole_rows(ref, places) for ref in refs])


def gate_up(normed_two, joined, hidden, walked, chips):
    tokens, width = normed_two.shape
    step = 768
    places = places_of(joined.shape[0], walked)
    gate_specs = column_specs(joined, 4 * width, hidden, chips, step)
    up_specs = column_specs(joined, 4 * width + hidden, hidden, chips, step)
    number = len(gate_specs)

    def body(normed_ref, *refs):
        normed = normed_ref[...]
        gate = dot(normed, step_matrix(refs[:number], places))
        up = dot(normed, step_matrix(refs[number : 2 * number], places))
        refs[-1][...] = (gate * (1.0 / (1.0 + jnp.exp(-gate))) * up).astype(bf16)

    return pl.pallas_call(
        body,
        grid=(hidden // step,),
        in_specs=[pl.BlockSpec((tokens, width), lambda i: (0, 0))] + gate_specs + up_specs,
        out_specs=pl.BlockSpec((tokens, step), lambda i: (0, i)),
        out_shape=jax.ShapeDtypeStruct((tokens, hidden), bf16),
        compiler_params=params(),
        cost_estimate=cost(4 * tokens * width * hidden, 4 * width * hidden + 2 * tokens * hidden),
    )(normed_two, *[joined] * (2 * number))


def down_projection(active, act, down, middle, mod, first, count, keep, step):
    hidden = act.shape[1]
    images, unused, width = mod.shape
    patches = act.shape[0] // images
    tokens = count * patches
    outs = [jax.ShapeDtypeStruct((tokens, width), bf16)]
    scratch = [pltpu.VMEM((tokens, width), f32)]
    if keep:
        outs.append(jax.ShapeDtypeStruct((tokens, width), f32))
        scratch = []

    def body(active_ref, act_ref, middle_ref, mod_ref, down_ref, result_ref, total):
        index = pl.program_id(0)

        @pl.when(active_ref[0] == 0)
        def _():
            result_ref[...] = jnp.zeros_like(result_ref)

        @pl.when(active_ref[0] != 0)
        def _():
            term = dot(act_ref[...], down_ref[...])

            @pl.when(index == 0)
            def _():
                total[...] = term

            @pl.when(index > 0)
            def _():
                total[...] += term

            @pl.when(index == hidden // step - 1)
            def _():
                for image in range(count):
                    at = slice(image * patches, (image + 1) * patches)
                    gate = mod_ref[first + image, 5:6]
                    result_ref[at] = (middle_ref[at] + gate * total[at]).astype(bf16)

    return pl.pallas_call(
        body,
        grid_spec=pltpu.PrefetchScalarGridSpec(
            num_scalar_prefetch=1,
            grid=(hidden // step,),
            in_specs=[
                pl.BlockSpec((tokens, step), lambda i, active: (first // count, i * active[0])),
                pl.BlockSpec((tokens, width), lambda i, active: (first // count, 0)),
                pl.BlockSpec(mod.shape, lambda i, active: (0, 0, 0)),
                pl.BlockSpec((step, width), lambda i, active: (i * active[0], 0)),
            ],
            out_specs=[pl.BlockSpec((tokens, width), lambda i, active: (0, 0))] * len(outs),
            scratch_shapes=scratch,
        ),
        out_shape=outs,
        compiler_params=params(),
        cost_estimate=cost(2 * tokens * width * hidden, 2 * width * hidden + 8 * tokens * width),
    )(active, act, middle, mod, down)


def incoming(cot_ref, back_refs, image, at):
    value = cot_ref[at].astype(f32)
    return value + back_refs[image][...].astype(f32) if back_refs else value


def mlp_gradient(cot, backs, mod, first, count):
    images, unused, width = mod.shape
    patches = cot.shape[0] // images

    def body(cot_ref, mod_ref, *refs):
        for image in range(count):
            at = slice(image * patches, (image + 1) * patches)
            grads = incoming(cot_ref, refs[: len(backs)], image, at)
            refs[-1][at] = (mod_ref[first + image, 5:6] * grads).astype(bf16)

    return pl.pallas_call(
        body,
        grid=(1,),
        in_specs=[
            pl.BlockSpec((count * patches, width), lambda i: (first // count, 0)),
            pl.BlockSpec(mod.shape, lambda i: (0, 0, 0)),
        ]
        + [pl.BlockSpec((patches, width), lambda i: (0, 0))] * len(backs),
        out_specs=pl.BlockSpec((count * patches, width), lambda i: (0, 0)),
        out_shape=jax.ShapeDtypeStruct((count * patches, width), bf16),
        compiler_params=params(),
        cost_estimate=cost(0, 6 * count * patches * width),
    )(cot, mod, *backs)


def stacked(refs):
    return refs[0][...] if len(refs) == 1 else jnp.concatenate([ref[...] for ref in refs], axis=0)


def whole_specs(arrays):
    return [pl.BlockSpec(array.shape, lambda i: (0, 0)) for array in arrays]


def act_backward(mlp_grads, down, step):
    hidden, width = down.shape
    tokens = sum(grad.shape[0] for grad in mlp_grads)

    def body(*refs):
        refs[-1][...] = dot_right(stacked(refs[:-2]), refs[-2][...]).astype(bf16)

    return pl.pallas_call(
        body,
        grid=(hidden // step,),
        in_specs=whole_specs(mlp_grads) + [pl.BlockSpec((step, width), lambda i: (i, 0))],
        out_specs=pl.BlockSpec((tokens, step), lambda i: (0, i)),
        out_shape=jax.ShapeDtypeStruct((tokens, hidden), bf16),
        compiler_params=params(),
        cost_estimate=cost(2 * tokens * width * hidden, 2 * width * hidden + 4 * tokens * width),
    )(*mlp_grads, down)


def mlp_backward(
    cot, backs, act_grad, forward, joined, middle, mod, walked, chips, sums_of
):
    tokens, hidden = act_grad.shape
    images, unused, width = mod.shape
    patches = tokens // images
    parts, rows, unused = joined.shape
    places = places_of(parts, walked)
    step = 768
    count = hidden // step
    gate_specs = column_specs(joined, 4 * width, hidden, chips, step)
    up_specs = column_specs(joined, 4 * width + hidden, hidden, chips, step)
    number = len(gate_specs)
    fresh, keep = len(forward) == 1, sums_of is not None
    whole = pl.BlockSpec((tokens, width), lambda i: (0, 0))
    block = pl.BlockSpec((tokens, step), lambda i: (0, i))
    anywhere = pl.BlockSpec(memory_space=pl.ANY)
    late = [cot, middle] + (list(sums_of) if keep else [])

    def body(act_grad_ref, mod_ref, joined_ref, *refs):
        refs = list(refs)

        def taken(size):
            first = refs[:size]
            del refs[:size]
            return first

        gate_refs, up_refs = taken(number), taken(number)

        forward_refs, back_refs, sources = taken(len(forward)), taken(len(backs)), taken(len(late))
        middle_grad_ref, mixed_grad_ref = taken(2)
        fresh_refs = taken(3 if fresh else 0)
        kept_refs = taken(4 if keep else 0)
        total, out_weight, sem = taken(3)
        copies, (sems,) = taken(len(late)), refs
        cot_ref, middle_ref = copies[:2]
        index = pl.program_id(0)
        fetches = [
            pltpu.make_async_copy(joined_ref.at[:, :, pl.ds(3 * width, width)], out_weight, sem)
        ] + [
            pltpu.make_async_copy(source, copies[which], sems.at[which])
            for which, source in enumerate(sources)
        ]

        @pl.when(index == 0)
        def _():
            for fetch in fetches:
                fetch.start()

        gate_weight = step_matrix(gate_refs, places)
        up_weight = step_matrix(up_refs, places)
        if fresh:
            normed = forward_refs[0][...]
            gate, up = dot(normed, gate_weight), dot(normed, up_weight)
        else:
            gate, up = (ref[...].astype(f32) for ref in forward_refs)
        sigma = 1.0 / (1.0 + jnp.exp(-gate))
        slope = act_grad_ref[...].astype(f32) * sigma
        gate_grad = (slope * up * (1.0 + gate * (1.0 - sigma))).astype(bf16)
        up_grad = (slope * gate).astype(bf16)
        if fresh:
            fresh_refs[0][...] = (gate * sigma * up).astype(bf16)
            fresh_refs[1][...] = gate.astype(bf16)
            fresh_refs[2][...] = up.astype(bf16)
        if keep:
            kept_refs[0][...] = gate_grad
            kept_refs[1][...] = up_grad
        term = dot_right(gate_grad, gate_weight) + dot_right(up_grad, up_weight)

        @pl.when(index == 0)
        def _():
            total[...] = term

        @pl.when(index > 0)
        def _():
            total[...] += term

        @pl.when(index == count - 1)
        def _():
            for fetch in fetches:
                fetch.wait()
            matrix = whole_rows(out_weight, places)
            for image in range(images):
                at = slice(image * patches, (image + 1) * patches)
                mod = mod_ref[image]
                grad, flow = total[at], middle_ref[at]
                inverse = inverse_rms(flow)
                normal = flow * inverse
                scaled = grad * (1.0 + mod[4:5])
                mean = jnp.mean(scaled * normal, axis=-1, keepdims=True)
                out_grad = incoming(cot_ref, back_refs, image, at)
                middle_grad = out_grad + (scaled - normal * mean) * inverse
                middle_grad_ref[at] = middle_grad
                branch_grad = (mod[2:3] * middle_grad).astype(bf16)
                mixed_grad_ref[at] = dot_right(branch_grad, matrix).astype(bf16)
                if keep:
                    mlp_ref, branch_ref = copies[2:]
                    kept_refs[2][at] = branch_grad
                    terms = [middle_grad * branch_ref[at], grad, grad * normal, out_grad * mlp_ref[at]]
                    for place, value in enumerate(terms):
                        kept_refs[3][image, place : place + 1] = jnp.sum(value, axis=0, keepdims=True)

    out_shapes = [
        jax.ShapeDtypeStruct((tokens, width), f32),
        jax.ShapeDtypeStruct((tokens, width), bf16),
    ]
    out_specs = [whole, whole]
    if fresh:
        out_shapes += [jax.ShapeDtypeStruct((tokens, hidden), bf16)] * 3
        out_specs += [block] * 3
    if keep:
        out_shapes += [jax.ShapeDtypeStruct((tokens, hidden), bf16)] * 2
        out_shapes += [jax.ShapeDtypeStruct((tokens, width), bf16)]
        out_shapes += [jax.ShapeDtypeStruct((images, 8, width), f32)]
        out_specs += [block, block, whole, pl.BlockSpec((images, 8, width), lambda i: (0, 0, 0))]
    return pl.pallas_call(
        body,
        grid=(count,),
        in_specs=[block, pl.BlockSpec(mod.shape, lambda i: (0, 0, 0)), anywhere]
        + gate_specs
        + up_specs
        + [whole if fresh else block] * len(forward)
        + [pl.BlockSpec((patches, width), lambda i: (0, 0))] * len(backs)
        + [anywhere] * len(late),
        out_specs=out_specs,
        out_shape=out_shapes,
        scratch_shapes=[
            pltpu.VMEM((tokens, width), f32),
            pltpu.VMEM((parts, rows, width), bf16),
            pltpu.SemaphoreType.DMA,
        ]
        + [pltpu.VMEM(array.shape, array.dtype) for array in late]
        + [pltpu.SemaphoreType.DMA((len(late),))],
        compiler_params=params(),
        cost_estimate=cost(
            2 * tokens * width * (4 * hidden + width), 4 * width * hidden + 6 * tokens * hidden
        ),
    )(act_grad, mod, joined, *[joined] * (2 * number), *forward, *backs, *late)


def attention_backward_kernel(heads, places, first, keep, refs):
    raw_hbm, value_hbm, mixed_grad_hbm, middle_grad_hbm, x_hbm = refs[:5]
    mod_ref, cos_ref, sin_ref, gain_ref, sum_ref, spread_ref, repeat_ref, joined_ref = refs[5:13]
    refs = refs[13:]
    if keep:
        flow_grad_ref, qkv_grad_ref, sums_ref = refs[:3]
        refs = refs[3:]
    else:
        back_ref = refs[0]
        refs = refs[1:]
    weight, scales, query_total, key_total, value_total = refs[:5]
    raw_ref, value_ref, mixed_grad_ref, middle_grad_ref, x_ref, sems = refs[5:]
    patches, width = x_ref.shape
    head_size = width // heads
    quarter = head_size // 4
    factor = head_size ** (-0.5)
    image = pl.program_id(0)
    rows = pl.ds((first + image) * patches, patches)
    sources = [
        raw_hbm.at[rows, pl.ds(0, width)],
        raw_hbm.at[rows, pl.ds(width, width)],
        value_hbm.at[rows],
        mixed_grad_hbm.at[rows],
        middle_grad_hbm.at[rows],
        x_hbm.at[rows],
    ]
    targets = [raw_ref.at[0], raw_ref.at[1], value_ref, mixed_grad_ref, middle_grad_ref, x_ref]
    copies = [
        pltpu.make_async_copy(source, target, sems.at[3 + which])
        for which, (source, target) in enumerate(zip(sources, targets))
    ]
    for copy in copies[:4]:
        copy.start()

    def fetch(part):
        return pltpu.make_async_copy(
            joined_ref.at[:, :, pl.ds(part * width, width)], weight.at[part], sems.at[part]
        )

    @pl.when(image == 0)
    def _():
        for part in range(3):
            fetch(part).start()

    for copy in copies[4:]:
        copy.start()
    first_half = first_half_mask((1, width), quarter)
    cos, sin = dot(cos_ref[...], repeat_ref[...]), dot(sin_ref[...], repeat_ref[...])
    summing, spreading = sum_ref[...], spread_ref[...]
    tables = (cos, sin, gain_ref, summing, spreading, head_size)
    copies[0].wait()
    queries = rotated(raw_ref[0], 0, tables, scales)
    copies[1].wait()
    keys = rotated(raw_ref[1], 1, tables, scales)
    for copy in copies[2:4]:
        copy.wait()
    values, mixed_grad = value_ref[...], mixed_grad_ref[...]
    query_total[...] = jnp.zeros_like(query_total)
    key_total[...] = jnp.zeros_like(key_total)
    value_total[...] = jnp.zeros_like(value_total)
    for start, span, members in head_groups(heads, head_size):
        window = slice(start, start + span)
        probs, slopes, key_parts, query_parts, grad_parts = [], [], [], [], []
        for head in members:
            mask = head_mask(head, head_size, start, span)
            key_part, query_part = keys[:, window] * mask, queries[:, window] * mask
            grad_part = mixed_grad[:, window] * mask
            scores = dot_right(key_part, queries[:, window])
            expon = jnp.exp2(scores * (factor * math.log2(math.e)))
            prob = expon * (1.0 / jnp.sum(expon, axis=0, keepdims=True))
            prob_grad = dot_right(values[:, window], grad_part)
            middle = jnp.sum(prob * prob_grad, axis=0, keepdims=True)
            probs.append(prob.astype(bf16))
            slopes.append((prob * (prob_grad - middle)).astype(bf16))
            key_parts.append(key_part)
            query_parts.append(query_part)
            grad_parts.append(grad_part)
        value_total[:, window] += dot(side_by_side(probs), one_above_other(grad_parts))
        key_total[:, window] += dot(side_by_side(slopes), one_above_other(query_parts))
        query_total[:, window] += dot_left(one_above_other(slopes), one_above_other(key_parts))

    def raw_grad(part, total):
        turned = total[...] * factor
        grad = turned * cos + partner(turned * sin, first_half, quarter)
        scale = scales[part]
        normal = raw_ref[part] * scale
        if keep:
            sums_ref[0, 2 + part : 3 + part] = jnp.sum(grad * normal, axis=0, keepdims=True)
        grad = grad * gain_ref[part : part + 1]
        mean = dot((grad * normal).astype(bf16), summing) * (1.0 / head_size)
        mean = dot(two_terms(mean), spreading)
        return (scale * (grad - normal * mean)).astype(bf16)

    def arrived(part):
        @pl.when(image == 0)
        def _():
            fetch(part).wait()

        return whole_rows(weight.at[part], places)

    parts = [raw_grad(0, query_total), raw_grad(1, key_total), value_total[...].astype(bf16)]
    grad = None
    for part in range(3):
        if keep:
            qkv_grad_ref[:, part * width : (part + 1) * width] = parts[part]
        term = dot_right(parts[part], arrived(part))
        grad = term if grad is None else grad + term
    for copy in copies[4:]:
        copy.wait()
    mod = mod_ref[0]
    flow = x_ref[...].astype(f32)
    inverse = inverse_rms(flow)
    normal = flow * inverse
    scaled = grad * (1.0 + mod[1:2])
    mean = jnp.mean(scaled * normal, axis=-1, keepdims=True)
    flow_grad = middle_grad_ref[...] + (scaled - normal * mean) * inverse
    if keep:
        flow_grad_ref[...] = flow_grad
        sums_ref[0, 0:1] = jnp.sum(grad, axis=0, keepdims=True)
        sums_ref[0, 1:2] = jnp.sum(grad * normal, axis=0, keepdims=True)
    else:
        back_ref[...] = flow_grad.astype(bf16)


def attention_backward(
    raw, value, mixed_grad, middle_grad, x, mod, tables, gain, joined, walked, first, count, keep
):
    images, unused, width = mod.shape
    patches = x.shape[0] // images
    tokens = count * patches
    heads = width // tables[-1]
    cos, sin, *matrices, unused = tables
    parts, rows, unused = joined.shape
    row = lambda columns: pl.BlockSpec((patches, columns), lambda image: (first + image, 0))
    token = lambda columns: pl.BlockSpec((patches, columns), lambda image: (image, 0))
    fixed = lambda array: pl.BlockSpec(array.shape, lambda image: (0,) * array.ndim)
    anywhere = pl.BlockSpec(memory_space=pl.ANY)
    out_shapes = [jax.ShapeDtypeStruct((tokens, width), bf16)]
    out_specs = [token(width)]
    if keep:
        out_shapes = [
            jax.ShapeDtypeStruct((tokens, width), f32),
            jax.ShapeDtypeStruct((tokens, 3 * width), bf16),
            jax.ShapeDtypeStruct((count, 8, width), f32),
        ]
        out_specs = [
            token(width),
            token(3 * width),
            pl.BlockSpec((1, 8, width), lambda image: (image, 0, 0)),
        ]

    def body(*refs):
        attention_backward_kernel(heads, places_of(parts, walked), first, keep, refs)

    return pl.pallas_call(
        body,
        grid=(count,),
        in_specs=[anywhere] * 5
        + [
            pl.BlockSpec((1, 8, width), lambda image: (first + image, 0, 0)),
            row(cos.shape[1]),
            row(sin.shape[1]),
            fixed(gain),
        ]
        + [fixed(matrix) for matrix in matrices]
        + [anywhere],
        out_specs=out_specs,
        out_shape=out_shapes,
        scratch_shapes=[
            pltpu.VMEM((3, parts, rows, width), bf16),
            pltpu.VMEM((2, patches, width), f32),
            pltpu.VMEM((patches, width), f32),
            pltpu.VMEM((patches, width), f32),
            pltpu.VMEM((patches, width), f32),
            pltpu.VMEM((2, patches, width), f32),
            pltpu.VMEM((patches, width), bf16),
            pltpu.VMEM((patches, width), bf16),
            pltpu.VMEM((patches, width), f32),
            pltpu.VMEM((patches, width), bf16),
            pltpu.SemaphoreType.DMA((9,)),
        ],
        compiler_params=params(),
        cost_estimate=cost(
            2 * tokens * width * (3 * width + 5 * patches),
            6 * width * width + tokens * width * 20,
        ),
    )(raw, value, mixed_grad, middle_grad, x, mod, cos, sin, gain, *matrices, joined)


def down_grad(mlp_grads, cot, back, act, mod, step):
    tokens, hidden = act.shape
    images, unused, width = mod.shape
    patches = tokens // images
    last = images - 1

    def body(act_ref, cot_ref, back_ref, mod_ref, *refs):
        given, (out_ref, last_ref, mlp_grad) = refs[:last], refs[last:]

        @pl.when(pl.program_id(0) == 0)
        def _():
            grads = incoming(cot_ref, [back_ref], 0, slice(0, patches))
            value = (mod_ref[last, 5:6] * grads).astype(bf16)
            last_ref[...] = value
            for image in range(last):
                mlp_grad[image * patches : (image + 1) * patches] = given[image][...]
            mlp_grad[last * patches :] = value

        out_ref[...] = dot_left(act_ref[...], mlp_grad[...]).astype(bf16)

    return pl.pallas_call(
        body,
        grid=(hidden // step,),
        in_specs=[
            pl.BlockSpec((tokens, step), lambda i: (0, i)),
            pl.BlockSpec((patches, width), lambda i: (last, 0)),
            pl.BlockSpec((patches, width), lambda i: (0, 0)),
            pl.BlockSpec(mod.shape, lambda i: (0, 0, 0)),
        ]
        + whole_specs(mlp_grads),
        out_specs=[
            pl.BlockSpec((step, width), lambda i: (i, 0)),
            pl.BlockSpec((patches, width), lambda i: (0, 0)),
        ],
        out_shape=[
            jax.ShapeDtypeStruct((hidden, width), bf16),
            jax.ShapeDtypeStruct((patches, width), bf16),
        ],
        scratch_shapes=[pltpu.VMEM((tokens, width), bf16)],
        compiler_params=params(),
        cost_estimate=cost(2 * tokens * width * hidden, 2 * width * hidden),
    )(act, cot, back, mod, *mlp_grads)


def matrix_grad_kernel(places, counts, *refs):
    pairs = len(counts)
    inputs, grads, out_ref = refs[:pairs], refs[pairs : 2 * pairs], refs[2 * pairs]
    rows = out_ref.shape[1]
    step = pl.program_id(0)
    first = 0
    for index in range(pairs):

        @pl.when(jnp.logical_and(step >= first, step < first + counts[index]))
        def _(index=index):
            product = dot_left(inputs[index][...], grads[index][...]).astype(bf16)
            for part, place in enumerate(places):
                out_ref[place] = product[part * rows : (part + 1) * rows]

        first += counts[index]


def matrix_grad(inputs, grads, step, parts, walked):
    tokens, width = inputs[0].shape
    counts = [grad.shape[1] // step for grad in grads]
    columns = sum(counts) * step
    rows = width // parts
    firsts = [sum(counts[:index]) for index in range(len(counts))]

    def grad_spec(first, count):
        return pl.BlockSpec((tokens, step), lambda i: (0, jnp.clip(i - first, 0, count - 1)))

    return pl.pallas_call(
        functools.partial(matrix_grad_kernel, places_of(parts, walked), counts),
        grid=(sum(counts),),
        in_specs=[pl.BlockSpec((tokens, width), lambda i: (0, 0))] * len(inputs)
        + [grad_spec(first, count) for first, count in zip(firsts, counts)],
        out_specs=pl.BlockSpec((parts, rows, step), lambda i: (0, 0, i)),
        out_shape=jax.ShapeDtypeStruct((parts, rows, columns), bf16),
        compiler_params=params(),
        cost_estimate=cost(2 * tokens * width * columns, 2 * width * columns),
    )(*inputs, *grads)


def walk_of(count):
    chips = count // 2
    order = [chip for chip in range(chips) if chip % 2 == 0]
    order += [chip for chip in reversed(range(chips)) if chip % 2 == 1]
    return [2 * chip + core for chip in order for core in (0, 1)]


def from_walk(rows, count):
    blocks = rows.reshape(count // 2, -1, rows.shape[-1])
    places = places_of(count // 2, True)
    return jnp.concatenate([blocks[place] for place in places], axis=0)


def columns_to_walk(matrix, count):
    each = matrix.shape[1] // (count // 2)
    chips = [device // 2 for device in walk_of(count)[::2]]
    return jnp.concatenate([matrix[:, chip * each : (chip + 1) * each] for chip in chips], axis=1)


def columns_from_walk(matrix, count):
    each = matrix.shape[1] // (count // 2)
    places = places_of(count // 2, True)
    return jnp.concatenate(
        [matrix[:, place * each : (place + 1) * each] for place in places], axis=1
    )


def to_walk(rows, count):
    blocks = rows.reshape(count // 2, -1, rows.shape[-1])
    return jnp.concatenate([blocks[device // 2] for device in walk_of(count)[::2]], axis=0)


def gather_walk(rows, count):
    return lax.all_gather(rows, "dp", axis=0, tiled=True, axis_index_groups=[walk_of(count)])


def scatter_walk(rows, groups):
    part = lax.psum_scatter(
        rows, "dp", scatter_dimension=0, tiled=True, axis_index_groups=groups
    )
    return lax.optimization_barrier(part)


def scatter_cores(rows, count):
    me = lax.axis_index("dp")
    width = rows.shape[-1]
    pairs = rows.reshape(count // 2, 2, -1, width)
    give = lax.dynamic_index_in_dim(pairs, 1 - me % 2, 1, keepdims=False)
    keep = lax.dynamic_index_in_dim(pairs, me % 2, 1, keepdims=False)
    both = keep.astype(f32) + swapped(give, 1, count).astype(f32)
    both = both.astype(bf16).reshape(-1, width)
    walk = walk_of(count)
    return both, [walk[0::2], walk[1::2]]


def as_parts(rows, count):
    each = rows.shape[0] // (count // 2)
    if each % 16 == 0:
        return rows.reshape(count // 2, each, rows.shape[1]), True
    whole = from_walk(rows, count)
    return whole[None], False


def swapped(block, bit, count):
    return lax.ppermute(block, "dp", [(device, device ^ bit) for device in range(count)])


def gather_small(block, count):
    me = lax.axis_index("dp")
    block = block[None]
    bit = count // 2
    while bit:
        other = swapped(block, bit, count)
        low = (me & bit) == 0
        pair = [jnp.where(low, block, other), jnp.where(low, other, block)]
        block = jnp.stack(pair, axis=1).reshape(2 * block.shape[0], *block.shape[1:])
        bit //= 2
    return block


def scatter_small(blocks, count):
    me = lax.axis_index("dp")
    bit = 1
    while bit < count:
        pairs = blocks.reshape(blocks.shape[0] // 2, 2, *blocks.shape[1:])
        mine = jnp.where((me & bit) == 0, 0, 1)
        give = lax.dynamic_index_in_dim(pairs, 1 - mine, 1, keepdims=False)
        keep = lax.dynamic_index_in_dim(pairs, mine, 1, keepdims=False)
        blocks = keep + swapped(give, bit, count)
        bit *= 2
    return blocks[0]


def time_features(timestep_ids, width):
    half_width = width // 2
    frequency = jnp.exp(-math.log(10000.0) * jnp.arange(half_width, dtype=f32) / half_width)
    angle_rows = timestep_ids.astype(f32)[:, None] * frequency[None, :]
    return jnp.concatenate([jnp.cos(angle_rows), jnp.sin(angle_rows)], axis=-1)


def rotation_tables(positions, width, head_size):
    quarter = head_size // 4
    frequency = jnp.exp(-math.log(10000.0) * jnp.arange(quarter, dtype=f32) / quarter)
    places = positions.reshape(-1, 1)
    row_angle = (places // GRID).astype(f32) * frequency
    col_angle = (places % GRID).astype(f32) * frequency
    row_cos, row_sin = jnp.cos(row_angle), jnp.sin(row_angle)
    col_cos, col_sin = jnp.cos(col_angle), jnp.sin(col_angle)
    cos = jnp.concatenate([row_cos, row_cos, col_cos, col_cos], axis=1)
    sin = jnp.concatenate([-row_sin, row_sin, -col_sin, col_sin], axis=1)
    padding = ((0, 0), (0, LANES - head_size))
    number = jnp.arange(LANES)
    column = jnp.arange(width)
    summing = (column[:, None] // head_size == number[None, :]).astype(bf16)
    spreading = (column[None, :] // head_size == number[:, None]).astype(bf16)
    repeating = (column[None, :] % head_size == number[:, None]).astype(bf16)
    return (
        two_terms(jnp.pad(cos, padding)),
        two_terms(jnp.pad(sin, padding)),
        summing,
        jnp.concatenate([spreading, spreading]),
        jnp.concatenate([repeating, repeating]),
    )


def per_device(
    tokens,
    cotangent,
    labels,
    timesteps,
    positions,
    label_table,
    ada_weight,
    qkv_weight,
    out_weight,
    gate_weight,
    up_weight,
    down_weight,
    q_gain,
    k_gain,
):
    first_section = lax.axis_index("section") == 0
    first_only = first_section.astype(jnp.int32).reshape(1)
    always = jnp.ones((1,), jnp.int32)
    count = lax.axis_size("dp")
    me = lax.axis_index("dp")
    images, patches, width = tokens.shape
    hidden = gate_weight.shape[2]
    head_size = q_gain.shape[1]
    heads = width // head_size
    rows = ada_weight.shape[1]
    classes = label_table.shape[0]

    gate_matrix, up_matrix, chips = gate_weight[0], up_weight[0], count // 2
    if hidden // chips % LANES:
        gate_matrix, up_matrix = columns_to_walk(gate_matrix, count), columns_to_walk(up_matrix, count)
        chips = 0
    joined = gather_walk(
        jnp.concatenate([qkv_weight[0], out_weight[0], gate_matrix, up_matrix], axis=1), count
    )

    ids = gather_small(jnp.stack([labels, timesteps]), count)
    all_labels = ids[:, 0].reshape(-1)
    all_times = ids[:, 1].reshape(-1)
    label_hot = all_labels[:, None] == jnp.arange(classes, dtype=jnp.int32)[None, :]
    condition = dot(label_hot.astype(bf16), label_table) + time_features(all_times, width)
    sigma_cond = jax.nn.sigmoid(condition)
    silu_cond = (condition * sigma_cond).astype(bf16)
    silu_rows = lax.dynamic_slice_in_dim(silu_cond, me * rows, rows, 1)
    mod_part = dot(silu_rows, ada_weight[0])
    mod = scatter_small(mod_part.reshape(count, images, -1), count).reshape(images, 6, width)
    mod = jnp.pad(mod, ((0, 0), (0, 2), (0, 0)))
    tables = rotation_tables(positions, width, head_size)
    flat = tokens.reshape(images * patches, width)
    own = jnp.where(first_section, flat, jnp.zeros_like(flat))

    down, joined, mod, own, tables = lax.optimization_barrier(
        (down_weight[0], joined, mod, own, tables)
    )
    down = gather_walk(down, count)
    joined, walked = as_parts(joined, count)
    tables = (*tables, head_size)
    gain = jnp.pad(jnp.tile(jnp.concatenate([q_gain, k_gain]), (1, heads)), ((0, 6), (0, 0)))

    cot = cotangent[0].reshape(images * patches, width)
    middle, normed_two = attention_forward(
        flat, None, mod, tables, gain, joined, walked, 0, images
    )
    act = gate_up(normed_two, joined, hidden, walked, chips)
    received = []
    for image in range(images):
        (early,) = down_projection(
            first_only, act, down, middle, mod, image, 1, False, hidden // 2
        )
        received.append(lax.ppermute(early, "section", [(0, 1)]))
    mlp_grad, unused = lax.optimization_barrier((mlp_gradient(cot, [], mod, 0, images), early))
    mlp_grads = [mlp_grad]
    act_grad = act_backward(mlp_grads, down, hidden // 2)
    kept = None
    for image in range(images):
        kept = attention_forward(
            own, received[image], mod, tables, gain, joined, walked, image, 1, kept
        )
    normed, raw, values, attended, branch, middle, normed_two, layer_in = kept

    middle_grad, mixed_grad, act, gate, up = mlp_backward(
        cot, [], act_grad, [normed_two], joined, middle, mod, walked, chips, None
    )
    backs = []
    for image in range(images):
        (early,) = attention_backward(
            raw,
            values,
            mixed_grad,
            middle_grad,
            layer_in,
            mod,
            tables,
            gain,
            joined,
            walked,
            image,
            1,
            False,
        )
        backs.append(lax.ppermute(early, "section", [(1, 0)]))
    late_act, unused = lax.optimization_barrier((act, early))
    result, mlp = down_projection(
        always, late_act, down, middle, mod, 0, images, True, hidden // 2
    )

    late_cot, unused = lax.optimization_barrier((cot, mlp))
    mlp_grads = [
        mlp_gradient(late_cot, [back], mod, image, 1) for image, back in enumerate(backs[:-1])
    ]
    down_term, mlp_grad = down_grad(mlp_grads, late_cot, backs[-1], act, mod, hidden // 4)
    mlp_grads = [*mlp_grads, mlp_grad]
    down_term, mlp_grads = lax.optimization_barrier((down_term, mlp_grads))
    down_part = scatter_walk(down_term, [walk_of(count)])
    act_grad = act_backward(mlp_grads, down, hidden // 2)
    middle_grad, mixed_grad, gate_grad, up_grad, branch_grad, mlp_sums = mlp_backward(
        cot, backs, act_grad, [gate, up], joined, middle, mod, walked, chips, [mlp, branch]
    )

    def matrix_term(inputs, grads, step):
        term = matrix_grad(inputs, grads, step, joined.shape[0], walked).reshape(width, -1)
        return term if walked else to_walk(term, count)

    gate_up_term = matrix_term([normed_two, normed_two], [gate_grad, up_grad], hidden // 2)
    gate_up_term, down_part = lax.optimization_barrier((gate_up_term, down_part))
    gate_up_part = scatter_walk(gate_up_term, [walk_of(count)])
    flow_grad, qkv_grad, attention_sums = attention_backward(
        raw,
        values,
        mixed_grad,
        middle_grad,
        layer_in,
        mod,
        tables,
        gain,
        joined,
        walked,
        0,
        images,
        True,
    )
    rest_term = matrix_term([normed, attended], [qkv_grad, branch_grad], width)
    rest_term, attention_sums = lax.optimization_barrier((rest_term, attention_sums))
    rest_term, groups = scatter_cores(rest_term, count)
    mod_grad = jnp.concatenate([attention_sums[:, :2], mlp_sums[:, :4]], axis=1)
    mod_grad = mod_grad.reshape(images, -1).astype(bf16)
    mod_all = gather_small(mod_grad, count).reshape(-1, mod_grad.shape[1])
    rest_term, gate_up_part, mod_all = lax.optimization_barrier((rest_term, gate_up_part, mod_all))
    rest_part = scatter_walk(rest_term, groups)
    flow_grad = flow_grad.reshape(images, patches, width)
    input_grads = jnp.where(first_section, flow_grad, flow_grad.astype(bf16).astype(f32))

    head_sums = jnp.sum(attention_sums[:, 2:4], axis=0).reshape(2, heads, head_size)
    ada_part = dot_left(silu_rows, mod_all)
    silu_grad = dot_right(mod_all, ada_weight[0])
    silu_grad = silu_grad + lax.ppermute(silu_grad, "section", [(0, 1), (1, 0)])
    silu_all = gather_small(silu_grad, count)
    gain_all = jnp.sum(gather_small(jnp.sum(head_sums, axis=1), count), axis=0)
    silu_all = jnp.swapaxes(silu_all, 0, 1).reshape(condition.shape)
    cond_grad = silu_all * sigma_cond * (1.0 + condition * (1.0 - sigma_cond))
    table_grad = lax.dot_general(
        label_hot.astype(f32),
        cond_grad,
        (((0,), (0,)), ((), ())),
        precision=lax.Precision.HIGHEST,
        preferred_element_type=f32,
    )
    return (
        result.reshape(1, images, patches, width),
        input_grads[None],
        table_grad,
        ada_part[None],
        rest_part[None, :, : 3 * width].astype(f32),
        rest_part[None, :, 3 * width :].astype(f32),
        columns_from_walk(gate_up_part[:, :hidden], count)[None].astype(f32),
        columns_from_walk(gate_up_part[:, hidden:], count)[None].astype(f32),
        down_part[None].astype(f32),
        gain_all[None, 0],
        gain_all[None, 1],
    )


def solution(mesh):
    placed = (
        P("dp", None, None),
        P("section", "dp", None, None),
        P("dp"),
        P("dp"),
        P("dp", None),
        P(),
        P("section", "dp", None),
        P("section", "dp", None),
        P("section", "dp", None),
        P("section", "dp", None),
        P("section", "dp", None),
        P("section", "dp", None),
        P("section", None),
        P("section", None),
    )
    return jax.shard_map(
        per_device,
        mesh=mesh,
        in_specs=placed,
        out_specs=(
            P("section", "dp", None, None),
            P("section", "dp", None, None),
            P(),
            P("section", "dp", None),
            P("section", "dp", None),
            P("section", "dp", None),
            P("section", "dp", None),
            P("section", "dp", None),
            P("section", "dp", None),
            P("section", None),
            P("section", None),
        ),
        check_vma=False,
    )
```

```python
import functools
import math

import jax
import jax.numpy as jnp
from jax import lax
from jax.experimental import pallas as pl
from jax.experimental.pallas import tpu as pltpu
from jax.sharding import PartitionSpec as P

GRID = 16
epsilon = 1e-06
f32 = jnp.float32
bf16 = jnp.bfloat16
LANES = 128
VMEM_BYTES = 56 * 1024 * 1024


def params():
    return pltpu.CompilerParams(vmem_limit_bytes=VMEM_BYTES)


def cost(flops, moved):
    return pl.CostEstimate(flops=int(flops), bytes_accessed=int(moved), transcendentals=0)


def dot(left, right):
    return jnp.dot(left, right, preferred_element_type=f32)


def dot_right(left, right):
    return lax.dot_general(left, right, (((1,), (1,)), ((), ())), preferred_element_type=f32)


def dot_left(left, right):
    return lax.dot_general(left, right, (((0,), (0,)), ((), ())), preferred_element_type=f32)


def whole_rows(ref, places):
    if len(places) == 1:
        return ref[places[0]]
    return jnp.concatenate([ref[place] for place in places], axis=0)


def part_place(index, parts, walked):
    if not walked:
        return index
    return index // 2 + (index % 2) * (parts - 1 - 2 * (index // 2))


def places_of(parts, walked):
    return [part_place(index, parts, walked) for index in range(parts)]


def two_terms(values):
    high = values.astype(bf16)
    low = (values - high.astype(f32)).astype(bf16)
    return jnp.concatenate([high, low], axis=1)


def inverse_rms(values):
    return lax.rsqrt(jnp.mean(values * values, axis=-1, keepdims=True) + epsilon)


def partner(values, first_half, quarter):
    width = values.shape[1]
    return jnp.where(
        first_half, pltpu.roll(values, width - quarter, 1), pltpu.roll(values, quarter, 1)
    )


def first_half_mask(shape, quarter):
    lane = lax.broadcasted_iota(jnp.int32, shape, 1)
    return lane % (2 * quarter) < quarter


def head_groups(heads, head_size):
    width = heads * head_size
    span = min(2 * LANES, width)
    groups = []
    for head in range(heads):
        low, high = head * head_size, (head + 1) * head_size
        if groups and high <= groups[-1][0] + span:
            groups[-1][2].append(head)
        else:
            groups.append((min(low // LANES * LANES, width - span), span, [head]))
    return groups


def head_mask(head, head_size, start, span):
    lane = lax.broadcasted_iota(jnp.int32, (1, span), 1) + start
    inside = jnp.logical_and(lane >= head * head_size, lane < (head + 1) * head_size)
    return inside.astype(f32).astype(bf16)


def side_by_side(parts):
    return parts[0] if len(parts) == 1 else jnp.concatenate(parts, axis=1)


def one_above_other(parts):
    return parts[0] if len(parts) == 1 else jnp.concatenate(parts, axis=0)


def rotated(raw, part, tables, keep_scale=None):
    cos, sin, gain_ref, summing, spreading, head_size = tables
    quarter = head_size // 4
    squares = dot((raw * raw).astype(bf16), summing)
    scale = lax.rsqrt(squares * (1.0 / head_size) + epsilon)
    scale = dot(two_terms(scale), spreading)
    if keep_scale is not None:
        keep_scale[part] = scale
    scaled = raw * scale * gain_ref[part : part + 1]
    first_half = first_half_mask((1, raw.shape[1]), quarter)
    return (scaled * cos + partner(scaled, first_half, quarter) * sin).astype(bf16)


def attention_forward_kernel(heads, places, first, keep, refs):
    if keep:
        received_ref, refs = refs[0], refs[1:]
    x_ref, mod_ref, cos_ref, sin_ref, gain_ref, sum_ref, spread_ref, repeat_ref = refs[:8]
    query_weight, joined_ref = refs[8:10]
    refs = refs[10:]
    patches, width = x_ref.shape
    if keep:
        outs, refs = refs[:8], refs[8:]
        weight, mixed, sems = refs[:3]
        held, out_sems = refs[3:11], refs[11]
    else:
        middle_ref, normed_two_ref, weight, mixed, sems = refs
    head_size = width // heads

    def fetch(part):
        return pltpu.make_async_copy(
            joined_ref.at[:, :, pl.ds((part + 1) * width, width)], weight.at[part], sems.at[part]
        )

    @pl.when(pl.program_id(0) == 0)
    def _():
        for part in range(3):
            fetch(part).start()

    def arrived(part):
        @pl.when(pl.program_id(0) == 0)
        def _():
            fetch(part).wait()

        return whole_rows(weight.at[part], places)

    def put(which):
        rows = pl.ds(first * patches, patches)
        return pltpu.make_async_copy(held[which], outs[which].at[rows], out_sems.at[which])

    flow = x_ref[...].astype(f32)
    if keep:
        flow = flow + received_ref[...].astype(f32)
    mod = mod_ref[0]
    normed = (flow * inverse_rms(flow) * (1.0 + mod[1:2]) + mod[0:1]).astype(bf16)
    cos, sin = dot(cos_ref[...], repeat_ref[...]), dot(sin_ref[...], repeat_ref[...])
    tables = (cos, sin, gain_ref, sum_ref[...], spread_ref[...], head_size)
    raw = dot(normed, whole_rows(query_weight, places))
    if keep:
        held[7][...] = flow.astype(bf16)
        held[0][...] = normed
        held[1][:, :width] = raw
        put(7).start()
        put(0).start()
    queries = rotated(raw, 0, tables)
    raw = dot(normed, arrived(0))
    if keep:
        held[1][:, width:] = raw
        put(1).start()
    keys = rotated(raw, 1, tables)
    values = dot(normed, arrived(1)).astype(bf16)
    if keep:
        held[2][...] = values
        put(2).start()
    mixed[...] = jnp.zeros_like(mixed)
    factor = head_size ** (-0.5) * math.log2(math.e)
    for start, span, members in head_groups(heads, head_size):
        window = slice(start, start + span)
        probs, parts = [], []
        for head in members:
            mask = head_mask(head, head_size, start, span)
            expon = jnp.exp2(dot_right(queries[:, window], keys[:, window] * mask) * factor)
            total = jnp.sum(expon, axis=-1, keepdims=True)
            probs.append((expon * (1.0 / total)).astype(bf16))
            parts.append(values[:, window] * mask)
        mixed[:, window] += dot(side_by_side(probs), one_above_other(parts))
    attended = mixed[...].astype(bf16)
    if keep:
        held[3][...] = attended
        put(3).start()
    branch = dot(attended, arrived(2))
    middle = flow + mod[2:3] * branch
    normed_two = (middle * inverse_rms(middle) * (1.0 + mod[4:5]) + mod[3:4]).astype(bf16)
    if keep:
        for which, value in ((4, branch), (5, middle), (6, normed_two)):
            held[which][...] = value
            put(which).start()
        for which in range(8):
            put(which).wait()
    else:
        middle_ref[...] = middle
        normed_two_ref[...] = normed_two


def attention_forward(x, received, mod, tables, gain, joined, walked, first, count, made=None):
    keep = received is not None
    images, unused, width = mod.shape
    tokens = x.shape[0]
    patches = tokens // images
    heads = width // tables[-1]
    cos, sin, *matrices, unused = tables
    parts, rows, unused = joined.shape
    row = lambda columns: pl.BlockSpec((patches, columns), lambda image: (first + image, 0))
    fixed = lambda array: pl.BlockSpec(array.shape, lambda image: (0,) * array.ndim)
    anywhere = pl.BlockSpec(memory_space=pl.ANY)
    shapes = [(width, f32), (width, bf16)]
    if keep:
        shapes = [
            (width, bf16),
            (2 * width, f32),
            (width, bf16),
            (width, bf16),
            (width, f32),
            (width, f32),
            (width, bf16),
            (width, bf16),
        ]
    made = [] if made is None else list(made)
    extra = [received] if keep else []
    inputs = 10 + len(extra)
    scratch = [
        pltpu.VMEM((3, parts, rows, width), bf16),
        pltpu.VMEM((patches, width), f32),
        pltpu.SemaphoreType.DMA((3,)),
    ]
    if keep:
        scratch += [pltpu.VMEM((patches, columns), kind) for columns, kind in shapes]
        scratch += [pltpu.SemaphoreType.DMA((len(shapes),))]

    def body(*refs):
        refs = refs[:inputs] + refs[inputs + len(made) :]
        attention_forward_kernel(heads, places_of(parts, walked), first, keep, refs)

    return pl.pallas_call(
        body,
        grid=(count,),
        in_specs=[pl.BlockSpec((patches, width), lambda image: (image, 0))] * len(extra)
        + [
            row(width),
            pl.BlockSpec((1, 8, width), lambda image: (first + image, 0, 0)),
            row(cos.shape[1]),
            row(sin.shape[1]),
            fixed(gain),
        ]
        + [fixed(matrix) for matrix in matrices]
        + [pl.BlockSpec((parts, rows, width), lambda image: (0, 0, 0))]
        + [anywhere] * (1 + len(made)),
        out_specs=[anywhere if keep else row(columns) for columns, kind in shapes],
        out_shape=[jax.ShapeDtypeStruct((tokens, columns), kind) for columns, kind in shapes],
        input_output_aliases={inputs + index: index for index in range(len(made))},
        scratch_shapes=scratch,
        compiler_params=params(),
        cost_estimate=cost(
            2 * count * patches * width * (4 * width + 2 * patches),
            8 * width * width + count * patches * width * 20,
        ),
    )(*extra, x, mod, cos, sin, gain, *matrices, joined, joined, *made)


def walk_chip(place, chips):
    return jnp.where(place < chips // 2, 2 * place, 2 * (chips - 1 - place) + 1)


def column_specs(joined, first, hidden, chips, step):
    parts, rows, unused = joined.shape
    if not chips:
        return [pl.BlockSpec((parts, rows, step), lambda i: (0, 0, first // step + i))]
    each = hidden // chips
    number = step // each

    def spec(which):
        return pl.BlockSpec(
            (parts, rows, each),
            lambda i: (0, 0, first // each + walk_chip(i * number + which, chips)),
        )

    return [spec(which) for which in range(number)]


def step_matrix(refs, places):
    return side_by_side([whole_rows(ref, places) for ref in refs])


def gate_up(normed_two, joined, hidden, walked, chips):
    tokens, width = normed_two.shape
    step = 768
    places = places_of(joined.shape[0], walked)
    gate_specs = column_specs(joined, 4 * width, hidden, chips, step)
    up_specs = column_specs(joined, 4 * width + hidden, hidden, chips, step)
    number = len(gate_specs)

    def body(normed_ref, *refs):
        normed = normed_ref[...]
        gate = dot(normed, step_matrix(refs[:number], places))
        up = dot(normed, step_matrix(refs[number : 2 * number], places))
        refs[-1][...] = (gate * (1.0 / (1.0 + jnp.exp(-gate))) * up).astype(bf16)

    return pl.pallas_call(
        body,
        grid=(hidden // step,),
        in_specs=[pl.BlockSpec((tokens, width), lambda i: (0, 0))] + gate_specs + up_specs,
        out_specs=pl.BlockSpec((tokens, step), lambda i: (0, i)),
        out_shape=jax.ShapeDtypeStruct((tokens, hidden), bf16),
        compiler_params=params(),
        cost_estimate=cost(4 * tokens * width * hidden, 4 * width * hidden + 2 * tokens * hidden),
    )(normed_two, *[joined] * (2 * number))


def down_projection(active, act, down, middle, mod, first, count, keep, step):
    hidden = act.shape[1]
    images, unused, width = mod.shape
    patches = act.shape[0] // images
    tokens = count * patches
    outs = [jax.ShapeDtypeStruct((tokens, width), bf16)]
    scratch = [pltpu.VMEM((tokens, width), f32)]
    if keep:
        outs.append(jax.ShapeDtypeStruct((tokens, width), f32))
        scratch = []

    def body(active_ref, act_ref, middle_ref, mod_ref, down_ref, result_ref, total):
        index = pl.program_id(0)

        @pl.when(active_ref[0] == 0)
        def _():
            result_ref[...] = jnp.zeros_like(result_ref)

        @pl.when(active_ref[0] != 0)
        def _():
            term = dot(act_ref[...], down_ref[...])

            @pl.when(index == 0)
            def _():
                total[...] = term

            @pl.when(index > 0)
            def _():
                total[...] += term

            @pl.when(index == hidden // step - 1)
            def _():
                for image in range(count):
                    at = slice(image * patches, (image + 1) * patches)
                    gate = mod_ref[first + image, 5:6]
                    result_ref[at] = (middle_ref[at] + gate * total[at]).astype(bf16)

    return pl.pallas_call(
        body,
        grid_spec=pltpu.PrefetchScalarGridSpec(
            num_scalar_prefetch=1,
            grid=(hidden // step,),
            in_specs=[
                pl.BlockSpec((tokens, step), lambda i, active: (first // count, i * active[0])),
                pl.BlockSpec((tokens, width), lambda i, active: (first // count, 0)),
                pl.BlockSpec(mod.shape, lambda i, active: (0, 0, 0)),
                pl.BlockSpec((step, width), lambda i, active: (i * active[0], 0)),
            ],
            out_specs=[pl.BlockSpec((tokens, width), lambda i, active: (0, 0))] * len(outs),
            scratch_shapes=scratch,
        ),
        out_shape=outs,
        compiler_params=params(),
        cost_estimate=cost(2 * tokens * width * hidden, 2 * width * hidden + 8 * tokens * width),
    )(active, act, middle, mod, down)


def incoming(cot_ref, back_refs, image, at):
    value = cot_ref[at].astype(f32)
    return value + back_refs[image][...].astype(f32) if back_refs else value


def mlp_gradient(cot, backs, mod, first, count):
    images, unused, width = mod.shape
    patches = cot.shape[0] // images

    def body(cot_ref, mod_ref, *refs):
        for image in range(count):
            at = slice(image * patches, (image + 1) * patches)
            grads = incoming(cot_ref, refs[: len(backs)], image, at)
            refs[-1][at] = (mod_ref[first + image, 5:6] * grads).astype(bf16)

    return pl.pallas_call(
        body,
        grid=(1,),
        in_specs=[
            pl.BlockSpec((count * patches, width), lambda i: (first // count, 0)),
            pl.BlockSpec(mod.shape, lambda i: (0, 0, 0)),
        ]
        + [pl.BlockSpec((patches, width), lambda i: (0, 0))] * len(backs),
        out_specs=pl.BlockSpec((count * patches, width), lambda i: (0, 0)),
        out_shape=jax.ShapeDtypeStruct((count * patches, width), bf16),
        compiler_params=params(),
        cost_estimate=cost(0, 6 * count * patches * width),
    )(cot, mod, *backs)


def stacked(refs):
    return refs[0][...] if len(refs) == 1 else jnp.concatenate([ref[...] for ref in refs], axis=0)


def whole_specs(arrays):
    return [pl.BlockSpec(array.shape, lambda i: (0, 0)) for array in arrays]


def act_backward(active, mlp_grads, down, step):
    hidden, width = down.shape
    tokens = sum(grad.shape[0] for grad in mlp_grads)

    def body(active_ref, *refs):
        @pl.when(active_ref[0] == 0)
        def _():
            refs[-1][...] = jnp.zeros_like(refs[-1])

        @pl.when(active_ref[0] != 0)
        def _():
            refs[-1][...] = dot_right(stacked(refs[:-2]), refs[-2][...]).astype(bf16)

    return pl.pallas_call(
        body,
        grid_spec=pltpu.PrefetchScalarGridSpec(
            num_scalar_prefetch=1,
            grid=(hidden // step,),
            in_specs=[pl.BlockSpec(grad.shape, lambda i, active: (0, 0)) for grad in mlp_grads]
            + [pl.BlockSpec((step, width), lambda i, active: (i * active[0], 0))],
            out_specs=pl.BlockSpec((tokens, step), lambda i, active: (0, i)),
        ),
        out_shape=jax.ShapeDtypeStruct((tokens, hidden), bf16),
        compiler_params=params(),
        cost_estimate=cost(2 * tokens * width * hidden, 2 * width * hidden + 4 * tokens * width),
    )(active, *mlp_grads, down)


def mlp_backward(
    cot, backs, act_grad, forward, joined, middle, mod, walked, chips, sums_of
):
    tokens, hidden = act_grad.shape
    images, unused, width = mod.shape
    patches = tokens // images
    parts, rows, unused = joined.shape
    places = places_of(parts, walked)
    step = 768
    count = hidden // step
    gate_specs = column_specs(joined, 4 * width, hidden, chips, step)
    up_specs = column_specs(joined, 4 * width + hidden, hidden, chips, step)
    number = len(gate_specs)
    fresh, keep = len(forward) == 1, sums_of is not None
    whole = pl.BlockSpec((tokens, width), lambda i: (0, 0))
    block = pl.BlockSpec((tokens, step), lambda i: (0, i))
    anywhere = pl.BlockSpec(memory_space=pl.ANY)
    late = [cot, middle] + (list(sums_of) if keep else [])

    def body(act_grad_ref, mod_ref, joined_ref, *refs):
        refs = list(refs)

        def taken(size):
            first = refs[:size]
            del refs[:size]
            return first

        gate_refs, up_refs = taken(number), taken(number)

        forward_refs, back_refs, sources = taken(len(forward)), taken(len(backs)), taken(len(late))
        middle_grad_ref, mixed_grad_ref = taken(2)
        fresh_refs = taken(3 if fresh else 0)
        kept_refs = taken(4 if keep else 0)
        total, out_weight, sem = taken(3)
        copies, (sems,) = taken(len(late)), refs
        cot_ref, middle_ref = copies[:2]
        index = pl.program_id(0)
        fetches = [
            pltpu.make_async_copy(joined_ref.at[:, :, pl.ds(3 * width, width)], out_weight, sem)
        ] + [
            pltpu.make_async_copy(source, copies[which], sems.at[which])
            for which, source in enumerate(sources)
        ]

        @pl.when(index == 0)
        def _():
            for fetch in fetches:
                fetch.start()

        gate_weight = step_matrix(gate_refs, places)
        up_weight = step_matrix(up_refs, places)
        if fresh:
            normed = forward_refs[0][...]
            gate, up = dot(normed, gate_weight), dot(normed, up_weight)
        else:
            gate, up = (ref[...].astype(f32) for ref in forward_refs)
        sigma = 1.0 / (1.0 + jnp.exp(-gate))
        slope = act_grad_ref[...].astype(f32) * sigma
        gate_grad = (slope * up * (1.0 + gate * (1.0 - sigma))).astype(bf16)
        up_grad = (slope * gate).astype(bf16)
        if fresh:
            fresh_refs[0][...] = (gate * sigma * up).astype(bf16)
            fresh_refs[1][...] = gate.astype(bf16)
            fresh_refs[2][...] = up.astype(bf16)
        if keep:
            kept_refs[0][...] = gate_grad
            kept_refs[1][...] = up_grad
        term = dot_right(gate_grad, gate_weight) + dot_right(up_grad, up_weight)

        @pl.when(index == 0)
        def _():
            total[...] = term

        @pl.when(index > 0)
        def _():
            total[...] += term

        @pl.when(index == count - 1)
        def _():
            for fetch in fetches:
                fetch.wait()
            matrix = whole_rows(out_weight, places)
            for image in range(images):
                at = slice(image * patches, (image + 1) * patches)
                mod = mod_ref[image]
                grad, flow = total[at], middle_ref[at]
                inverse = inverse_rms(flow)
                normal = flow * inverse
                scaled = grad * (1.0 + mod[4:5])
                mean = jnp.mean(scaled * normal, axis=-1, keepdims=True)
                out_grad = incoming(cot_ref, back_refs, image, at)
                middle_grad = out_grad + (scaled - normal * mean) * inverse
                middle_grad_ref[at] = middle_grad
                branch_grad = (mod[2:3] * middle_grad).astype(bf16)
                mixed_grad_ref[at] = dot_right(branch_grad, matrix).astype(bf16)
                if keep:
                    mlp_ref, branch_ref = copies[2:]
                    kept_refs[2][at] = branch_grad
                    terms = [middle_grad * branch_ref[at], grad, grad * normal, out_grad * mlp_ref[at]]
                    for place, value in enumerate(terms):
                        kept_refs[3][image, place : place + 1] = jnp.sum(value, axis=0, keepdims=True)

    out_shapes = [
        jax.ShapeDtypeStruct((tokens, width), f32),
        jax.ShapeDtypeStruct((tokens, width), bf16),
    ]
    out_specs = [whole, whole]
    if fresh:
        out_shapes += [jax.ShapeDtypeStruct((tokens, hidden), bf16)] * 3
        out_specs += [block] * 3
    if keep:
        out_shapes += [jax.ShapeDtypeStruct((tokens, hidden), bf16)] * 2
        out_shapes += [jax.ShapeDtypeStruct((tokens, width), bf16)]
        out_shapes += [jax.ShapeDtypeStruct((images, 8, width), f32)]
        out_specs += [block, block, whole, pl.BlockSpec((images, 8, width), lambda i: (0, 0, 0))]
    return pl.pallas_call(
        body,
        grid=(count,),
        in_specs=[block, pl.BlockSpec(mod.shape, lambda i: (0, 0, 0)), anywhere]
        + gate_specs
        + up_specs
        + [whole if fresh else block] * len(forward)
        + [pl.BlockSpec((patches, width), lambda i: (0, 0))] * len(backs)
        + [anywhere] * len(late),
        out_specs=out_specs,
        out_shape=out_shapes,
        scratch_shapes=[
            pltpu.VMEM((tokens, width), f32),
            pltpu.VMEM((parts, rows, width), bf16),
            pltpu.SemaphoreType.DMA,
        ]
        + [pltpu.VMEM(array.shape, array.dtype) for array in late]
        + [pltpu.SemaphoreType.DMA((len(late),))],
        compiler_params=params(),
        cost_estimate=cost(
            2 * tokens * width * (4 * hidden + width), 4 * width * hidden + 6 * tokens * hidden
        ),
    )(act_grad, mod, joined, *[joined] * (2 * number), *forward, *backs, *late)


def attention_backward_kernel(heads, places, first, keep, refs):
    raw_hbm, value_hbm, mixed_grad_hbm, middle_grad_hbm, x_hbm = refs[:5]
    mod_ref, cos_ref, sin_ref, gain_ref, sum_ref, spread_ref, repeat_ref, joined_ref = refs[5:13]
    refs = refs[13:]
    if keep:
        flow_grad_ref, qkv_grad_ref, sums_ref = refs[:3]
        refs = refs[3:]
    else:
        back_ref = refs[0]
        refs = refs[1:]
    weight, scales, query_total, key_total, value_total = refs[:5]
    raw_ref, value_ref, mixed_grad_ref, middle_grad_ref, x_ref, sems = refs[5:]
    patches, width = x_ref.shape
    head_size = width // heads
    quarter = head_size // 4
    factor = head_size ** (-0.5)
    image = pl.program_id(0)
    rows = pl.ds((first + image) * patches, patches)
    sources = [
        raw_hbm.at[rows, pl.ds(0, width)],
        raw_hbm.at[rows, pl.ds(width, width)],
        value_hbm.at[rows],
        mixed_grad_hbm.at[rows],
        middle_grad_hbm.at[rows],
        x_hbm.at[rows],
    ]
    targets = [raw_ref.at[0], raw_ref.at[1], value_ref, mixed_grad_ref, middle_grad_ref, x_ref]
    copies = [
        pltpu.make_async_copy(source, target, sems.at[3 + which])
        for which, (source, target) in enumerate(zip(sources, targets))
    ]
    for copy in copies[:4]:
        copy.start()

    def fetch(part):
        return pltpu.make_async_copy(
            joined_ref.at[:, :, pl.ds(part * width, width)], weight.at[part], sems.at[part]
        )

    @pl.when(image == 0)
    def _():
        for part in range(3):
            fetch(part).start()

    for copy in copies[4:]:
        copy.start()
    first_half = first_half_mask((1, width), quarter)
    cos, sin = dot(cos_ref[...], repeat_ref[...]), dot(sin_ref[...], repeat_ref[...])
    summing, spreading = sum_ref[...], spread_ref[...]
    tables = (cos, sin, gain_ref, summing, spreading, head_size)
    copies[0].wait()
    queries = rotated(raw_ref[0], 0, tables, scales)
    copies[1].wait()
    keys = rotated(raw_ref[1], 1, tables, scales)
    for copy in copies[2:4]:
        copy.wait()
    values, mixed_grad = value_ref[...], mixed_grad_ref[...]
    query_total[...] = jnp.zeros_like(query_total)
    key_total[...] = jnp.zeros_like(key_total)
    value_total[...] = jnp.zeros_like(value_total)
    for start, span, members in head_groups(heads, head_size):
        window = slice(start, start + span)
        probs, slopes, key_parts, query_parts, grad_parts = [], [], [], [], []
        for head in members:
            mask = head_mask(head, head_size, start, span)
            key_part, query_part = keys[:, window] * mask, queries[:, window] * mask
            grad_part = mixed_grad[:, window] * mask
            scores = dot_right(key_part, queries[:, window])
            expon = jnp.exp2(scores * (factor * math.log2(math.e)))
            prob = expon * (1.0 / jnp.sum(expon, axis=0, keepdims=True))
            prob_grad = dot_right(values[:, window], grad_part)
            middle = jnp.sum(prob * prob_grad, axis=0, keepdims=True)
            probs.append(prob.astype(bf16))
            slopes.append((prob * (prob_grad - middle)).astype(bf16))
            key_parts.append(key_part)
            query_parts.append(query_part)
            grad_parts.append(grad_part)
        value_total[:, window] += dot(side_by_side(probs), one_above_other(grad_parts))
        key_total[:, window] += dot(side_by_side(slopes), one_above_other(query_parts))
        query_total[:, window] += dot_left(one_above_other(slopes), one_above_other(key_parts))

    def raw_grad(part, total):
        turned = total[...] * factor
        grad = turned * cos + partner(turned * sin, first_half, quarter)
        scale = scales[part]
        normal = raw_ref[part] * scale
        if keep:
            sums_ref[0, 2 + part : 3 + part] = jnp.sum(grad * normal, axis=0, keepdims=True)
        grad = grad * gain_ref[part : part + 1]
        mean = dot((grad * normal).astype(bf16), summing) * (1.0 / head_size)
        mean = dot(two_terms(mean), spreading)
        return (scale * (grad - normal * mean)).astype(bf16)

    def arrived(part):
        @pl.when(image == 0)
        def _():
            fetch(part).wait()

        return whole_rows(weight.at[part], places)

    parts = [raw_grad(0, query_total), raw_grad(1, key_total), value_total[...].astype(bf16)]
    grad = None
    for part in range(3):
        if keep:
            qkv_grad_ref[:, part * width : (part + 1) * width] = parts[part]
        term = dot_right(parts[part], arrived(part))
        grad = term if grad is None else grad + term
    for copy in copies[4:]:
        copy.wait()
    mod = mod_ref[0]
    flow = x_ref[...].astype(f32)
    inverse = inverse_rms(flow)
    normal = flow * inverse
    scaled = grad * (1.0 + mod[1:2])
    mean = jnp.mean(scaled * normal, axis=-1, keepdims=True)
    flow_grad = middle_grad_ref[...] + (scaled - normal * mean) * inverse
    if keep:
        flow_grad_ref[...] = flow_grad
        sums_ref[0, 0:1] = jnp.sum(grad, axis=0, keepdims=True)
        sums_ref[0, 1:2] = jnp.sum(grad * normal, axis=0, keepdims=True)
    else:
        back_ref[...] = flow_grad.astype(bf16)


def attention_backward(
    raw, value, mixed_grad, middle_grad, x, mod, tables, gain, joined, walked, first, count, keep
):
    images, unused, width = mod.shape
    patches = x.shape[0] // images
    tokens = count * patches
    heads = width // tables[-1]
    cos, sin, *matrices, unused = tables
    parts, rows, unused = joined.shape
    row = lambda columns: pl.BlockSpec((patches, columns), lambda image: (first + image, 0))
    token = lambda columns: pl.BlockSpec((patches, columns), lambda image: (image, 0))
    fixed = lambda array: pl.BlockSpec(array.shape, lambda image: (0,) * array.ndim)
    anywhere = pl.BlockSpec(memory_space=pl.ANY)
    out_shapes = [jax.ShapeDtypeStruct((tokens, width), bf16)]
    out_specs = [token(width)]
    if keep:
        out_shapes = [
            jax.ShapeDtypeStruct((tokens, width), f32),
            jax.ShapeDtypeStruct((tokens, 3 * width), bf16),
            jax.ShapeDtypeStruct((count, 8, width), f32),
        ]
        out_specs = [
            token(width),
            token(3 * width),
            pl.BlockSpec((1, 8, width), lambda image: (image, 0, 0)),
        ]

    def body(*refs):
        attention_backward_kernel(heads, places_of(parts, walked), first, keep, refs)

    return pl.pallas_call(
        body,
        grid=(count,),
        in_specs=[anywhere] * 5
        + [
            pl.BlockSpec((1, 8, width), lambda image: (first + image, 0, 0)),
            row(cos.shape[1]),
            row(sin.shape[1]),
            fixed(gain),
        ]
        + [fixed(matrix) for matrix in matrices]
        + [anywhere],
        out_specs=out_specs,
        out_shape=out_shapes,
        scratch_shapes=[
            pltpu.VMEM((3, parts, rows, width), bf16),
            pltpu.VMEM((2, patches, width), f32),
            pltpu.VMEM((patches, width), f32),
            pltpu.VMEM((patches, width), f32),
            pltpu.VMEM((patches, width), f32),
            pltpu.VMEM((2, patches, width), f32),
            pltpu.VMEM((patches, width), bf16),
            pltpu.VMEM((patches, width), bf16),
            pltpu.VMEM((patches, width), f32),
            pltpu.VMEM((patches, width), bf16),
            pltpu.SemaphoreType.DMA((9,)),
        ],
        compiler_params=params(),
        cost_estimate=cost(
            2 * tokens * width * (3 * width + 5 * patches),
            6 * width * width + tokens * width * 20,
        ),
    )(raw, value, mixed_grad, middle_grad, x, mod, cos, sin, gain, *matrices, joined)


def down_grad(mlp_grads, cot, back, act, mod, step):
    tokens, hidden = act.shape
    images, unused, width = mod.shape
    patches = tokens // images
    last = images - 1

    def body(act_ref, cot_ref, back_ref, mod_ref, *refs):
        given, (out_ref, last_ref, mlp_grad) = refs[:last], refs[last:]

        @pl.when(pl.program_id(0) == 0)
        def _():
            grads = incoming(cot_ref, [back_ref], 0, slice(0, patches))
            value = (mod_ref[last, 5:6] * grads).astype(bf16)
            last_ref[...] = value
            for image in range(last):
                mlp_grad[image * patches : (image + 1) * patches] = given[image][...]
            mlp_grad[last * patches :] = value

        out_ref[...] = dot_left(act_ref[...], mlp_grad[...]).astype(bf16)

    return pl.pallas_call(
        body,
        grid=(hidden // step,),
        in_specs=[
            pl.BlockSpec((tokens, step), lambda i: (0, i)),
            pl.BlockSpec((patches, width), lambda i: (last, 0)),
            pl.BlockSpec((patches, width), lambda i: (0, 0)),
            pl.BlockSpec(mod.shape, lambda i: (0, 0, 0)),
        ]
        + whole_specs(mlp_grads),
        out_specs=[
            pl.BlockSpec((step, width), lambda i: (i, 0)),
            pl.BlockSpec((patches, width), lambda i: (0, 0)),
        ],
        out_shape=[
            jax.ShapeDtypeStruct((hidden, width), bf16),
            jax.ShapeDtypeStruct((patches, width), bf16),
        ],
        scratch_shapes=[pltpu.VMEM((tokens, width), bf16)],
        compiler_params=params(),
        cost_estimate=cost(2 * tokens * width * hidden, 2 * width * hidden),
    )(act, cot, back, mod, *mlp_grads)


def matrix_grad_kernel(places, counts, *refs):
    pairs = len(counts)
    inputs, grads, out_ref = refs[:pairs], refs[pairs : 2 * pairs], refs[2 * pairs]
    rows = out_ref.shape[1]
    step = pl.program_id(0)
    first = 0
    for index in range(pairs):

        @pl.when(jnp.logical_and(step >= first, step < first + counts[index]))
        def _(index=index):
            product = dot_left(inputs[index][...], grads[index][...]).astype(bf16)
            for part, place in enumerate(places):
                out_ref[place] = product[part * rows : (part + 1) * rows]

        first += counts[index]


def matrix_grad(inputs, grads, step, parts, walked):
    tokens, width = inputs[0].shape
    counts = [grad.shape[1] // step for grad in grads]
    columns = sum(counts) * step
    rows = width // parts
    firsts = [sum(counts[:index]) for index in range(len(counts))]

    def grad_spec(first, count):
        return pl.BlockSpec((tokens, step), lambda i: (0, jnp.clip(i - first, 0, count - 1)))

    return pl.pallas_call(
        functools.partial(matrix_grad_kernel, places_of(parts, walked), counts),
        grid=(sum(counts),),
        in_specs=[pl.BlockSpec((tokens, width), lambda i: (0, 0))] * len(inputs)
        + [grad_spec(first, count) for first, count in zip(firsts, counts)],
        out_specs=pl.BlockSpec((parts, rows, step), lambda i: (0, 0, i)),
        out_shape=jax.ShapeDtypeStruct((parts, rows, columns), bf16),
        compiler_params=params(),
        cost_estimate=cost(2 * tokens * width * columns, 2 * width * columns),
    )(*inputs, *grads)


def walk_of(count):
    chips = count // 2
    order = [chip for chip in range(chips) if chip % 2 == 0]
    order += [chip for chip in reversed(range(chips)) if chip % 2 == 1]
    return [2 * chip + core for chip in order for core in (0, 1)]


def from_walk(rows, count):
    blocks = rows.reshape(count // 2, -1, rows.shape[-1])
    places = places_of(count // 2, True)
    return jnp.concatenate([blocks[place] for place in places], axis=0)


def columns_to_walk(matrix, count):
    each = matrix.shape[1] // (count // 2)
    chips = [device // 2 for device in walk_of(count)[::2]]
    return jnp.concatenate([matrix[:, chip * each : (chip + 1) * each] for chip in chips], axis=1)


def columns_from_walk(matrix, count):
    each = matrix.shape[1] // (count // 2)
    places = places_of(count // 2, True)
    return jnp.concatenate(
        [matrix[:, place * each : (place + 1) * each] for place in places], axis=1
    )


def to_walk(rows, count):
    blocks = rows.reshape(count // 2, -1, rows.shape[-1])
    return jnp.concatenate([blocks[device // 2] for device in walk_of(count)[::2]], axis=0)


def gather_walk(rows, count):
    return lax.all_gather(rows, "dp", axis=0, tiled=True, axis_index_groups=[walk_of(count)])


def scatter_walk(rows, groups):
    part = lax.psum_scatter(
        rows, "dp", scatter_dimension=0, tiled=True, axis_index_groups=groups
    )
    return lax.optimization_barrier(part)


def scatter_cores(rows, count):
    me = lax.axis_index("dp")
    width = rows.shape[-1]
    pairs = rows.reshape(count // 2, 2, -1, width)
    give = lax.dynamic_index_in_dim(pairs, 1 - me % 2, 1, keepdims=False)
    keep = lax.dynamic_index_in_dim(pairs, me % 2, 1, keepdims=False)
    both = keep.astype(f32) + swapped(give, 1, count).astype(f32)
    both = both.astype(bf16).reshape(-1, width)
    walk = walk_of(count)
    return both, [walk[0::2], walk[1::2]]


def as_parts(rows, count):
    each = rows.shape[0] // (count // 2)
    if each % 16 == 0:
        return rows.reshape(count // 2, each, rows.shape[1]), True
    whole = from_walk(rows, count)
    return whole[None], False


def swapped(block, bit, count):
    return lax.ppermute(block, "dp", [(device, device ^ bit) for device in range(count)])


def gather_small(block, count):
    me = lax.axis_index("dp")
    block = block[None]
    bit = count // 2
    while bit:
        other = swapped(block, bit, count)
        low = (me & bit) == 0
        pair = [jnp.where(low, block, other), jnp.where(low, other, block)]
        block = jnp.stack(pair, axis=1).reshape(2 * block.shape[0], *block.shape[1:])
        bit //= 2
    return block


def scatter_small(blocks, count):
    me = lax.axis_index("dp")
    bit = 1
    while bit < count:
        pairs = blocks.reshape(blocks.shape[0] // 2, 2, *blocks.shape[1:])
        mine = jnp.where((me & bit) == 0, 0, 1)
        give = lax.dynamic_index_in_dim(pairs, 1 - mine, 1, keepdims=False)
        keep = lax.dynamic_index_in_dim(pairs, mine, 1, keepdims=False)
        blocks = keep + swapped(give, bit, count)
        bit *= 2
    return blocks[0]


def time_features(timestep_ids, width):
    half_width = width // 2
    frequency = jnp.exp(-math.log(10000.0) * jnp.arange(half_width, dtype=f32) / half_width)
    angle_rows = timestep_ids.astype(f32)[:, None] * frequency[None, :]
    return jnp.concatenate([jnp.cos(angle_rows), jnp.sin(angle_rows)], axis=-1)


def rotation_tables(positions, width, head_size):
    quarter = head_size // 4
    frequency = jnp.exp(-math.log(10000.0) * jnp.arange(quarter, dtype=f32) / quarter)
    places = positions.reshape(-1, 1)
    row_angle = (places // GRID).astype(f32) * frequency
    col_angle = (places % GRID).astype(f32) * frequency
    row_cos, row_sin = jnp.cos(row_angle), jnp.sin(row_angle)
    col_cos, col_sin = jnp.cos(col_angle), jnp.sin(col_angle)
    cos = jnp.concatenate([row_cos, row_cos, col_cos, col_cos], axis=1)
    sin = jnp.concatenate([-row_sin, row_sin, -col_sin, col_sin], axis=1)
    padding = ((0, 0), (0, LANES - head_size))
    number = jnp.arange(LANES)
    column = jnp.arange(width)
    summing = (column[:, None] // head_size == number[None, :]).astype(bf16)
    spreading = (column[None, :] // head_size == number[:, None]).astype(bf16)
    repeating = (column[None, :] % head_size == number[:, None]).astype(bf16)
    return (
        two_terms(jnp.pad(cos, padding)),
        two_terms(jnp.pad(sin, padding)),
        summing,
        jnp.concatenate([spreading, spreading]),
        jnp.concatenate([repeating, repeating]),
    )


def per_device(
    tokens,
    cotangent,
    labels,
    timesteps,
    positions,
    label_table,
    ada_weight,
    qkv_weight,
    out_weight,
    gate_weight,
    up_weight,
    down_weight,
    q_gain,
    k_gain,
):
    first_section = lax.axis_index("section") == 0
    first_only = first_section.astype(jnp.int32).reshape(1)
    second_only = 1 - first_only
    always = jnp.ones((1,), jnp.int32)
    count = lax.axis_size("dp")
    me = lax.axis_index("dp")
    images, patches, width = tokens.shape
    hidden = gate_weight.shape[2]
    head_size = q_gain.shape[1]
    heads = width // head_size
    rows = ada_weight.shape[1]
    classes = label_table.shape[0]

    gate_matrix, up_matrix, chips = gate_weight[0], up_weight[0], count // 2
    if hidden // chips % LANES:
        gate_matrix, up_matrix = columns_to_walk(gate_matrix, count), columns_to_walk(up_matrix, count)
        chips = 0
    joined = gather_walk(
        jnp.concatenate([qkv_weight[0], out_weight[0], gate_matrix, up_matrix], axis=1), count
    )

    ids = gather_small(jnp.stack([labels, timesteps]), count)
    all_labels = ids[:, 0].reshape(-1)
    all_times = ids[:, 1].reshape(-1)
    label_hot = all_labels[:, None] == jnp.arange(classes, dtype=jnp.int32)[None, :]
    condition = dot(label_hot.astype(bf16), label_table) + time_features(all_times, width)
    sigma_cond = jax.nn.sigmoid(condition)
    silu_cond = (condition * sigma_cond).astype(bf16)
    silu_rows = lax.dynamic_slice_in_dim(silu_cond, me * rows, rows, 1)
    mod_part = dot(silu_rows, ada_weight[0])
    mod = scatter_small(mod_part.reshape(count, images, -1), count).reshape(images, 6, width)
    mod = jnp.pad(mod, ((0, 0), (0, 2), (0, 0)))
    tables = rotation_tables(positions, width, head_size)
    flat = tokens.reshape(images * patches, width)
    own = jnp.where(first_section, flat, jnp.zeros_like(flat))

    down, joined, mod, own, tables = lax.optimization_barrier(
        (down_weight[0], joined, mod, own, tables)
    )
    down = gather_walk(down, count)
    joined, walked = as_parts(joined, count)
    tables = (*tables, head_size)
    gain = jnp.pad(jnp.tile(jnp.concatenate([q_gain, k_gain]), (1, heads)), ((0, 6), (0, 0)))

    cot = cotangent[0].reshape(images * patches, width)
    middle, normed_two = attention_forward(
        flat, None, mod, tables, gain, joined, walked, 0, images
    )
    act = gate_up(normed_two, joined, hidden, walked, chips)
    received = []
    for image in range(images):
        (early,) = down_projection(
            first_only, act, down, middle, mod, image, 1, False, hidden // 2
        )
        received.append(lax.ppermute(early, "section", [(0, 1)]))
    mlp_grad, unused = lax.optimization_barrier((mlp_gradient(cot, [], mod, 0, images), early))
    mlp_grads = [mlp_grad]
    act_grad = act_backward(second_only, mlp_grads, down, hidden // 2)
    kept = None
    for image in range(images):
        kept = attention_forward(
            own, received[image], mod, tables, gain, joined, walked, image, 1, kept
        )
    normed, raw, values, attended, branch, middle, normed_two, layer_in = kept

    middle_grad, mixed_grad, act, gate, up = mlp_backward(
        cot, [], act_grad, [normed_two], joined, middle, mod, walked, chips, None
    )
    backs = []
    for image in range(images):
        (early,) = attention_backward(
            raw,
            values,
            mixed_grad,
            middle_grad,
            layer_in,
            mod,
            tables,
            gain,
            joined,
            walked,
            image,
            1,
            False,
        )
        backs.append(lax.ppermute(early, "section", [(1, 0)]))
    late_act, unused = lax.optimization_barrier((act, early))
    result, mlp = down_projection(
        always, late_act, down, middle, mod, 0, images, True, hidden // 2
    )

    late_cot, unused = lax.optimization_barrier((cot, mlp))
    mlp_grads = [
        mlp_gradient(late_cot, [back], mod, image, 1) for image, back in enumerate(backs[:-1])
    ]
    down_term, mlp_grad = down_grad(mlp_grads, late_cot, backs[-1], act, mod, hidden // 4)
    mlp_grads = [*mlp_grads, mlp_grad]
    down_term, mlp_grads = lax.optimization_barrier((down_term, mlp_grads))
    down_part = scatter_walk(down_term, [walk_of(count)])
    act_grad = act_backward(always, mlp_grads, down, hidden // 2)
    middle_grad, mixed_grad, gate_grad, up_grad, branch_grad, mlp_sums = mlp_backward(
        cot, backs, act_grad, [gate, up], joined, middle, mod, walked, chips, [mlp, branch]
    )

    def matrix_term(inputs, grads, step):
        term = matrix_grad(inputs, grads, step, joined.shape[0], walked).reshape(width, -1)
        return term if walked else to_walk(term, count)

    gate_up_term = matrix_term([normed_two, normed_two], [gate_grad, up_grad], hidden // 2)
    gate_up_term, down_part = lax.optimization_barrier((gate_up_term, down_part))
    gate_up_part = scatter_walk(gate_up_term, [walk_of(count)])
    flow_grad, qkv_grad, attention_sums = attention_backward(
        raw,
        values,
        mixed_grad,
        middle_grad,
        layer_in,
        mod,
        tables,
        gain,
        joined,
        walked,
        0,
        images,
        True,
    )
    rest_term = matrix_term([normed, attended], [qkv_grad, branch_grad], width)
    rest_term, attention_sums = lax.optimization_barrier((rest_term, attention_sums))
    rest_term, groups = scatter_cores(rest_term, count)
    mod_grad = jnp.concatenate([attention_sums[:, :2], mlp_sums[:, :4]], axis=1)
    mod_grad = mod_grad.reshape(images, -1).astype(bf16)
    mod_all = gather_small(mod_grad, count).reshape(-1, mod_grad.shape[1])
    rest_term, gate_up_part, mod_all = lax.optimization_barrier((rest_term, gate_up_part, mod_all))
    rest_part = scatter_walk(rest_term, groups)
    flow_grad = flow_grad.reshape(images, patches, width)
    input_grads = jnp.where(first_section, flow_grad, flow_grad.astype(bf16).astype(f32))

    head_sums = jnp.sum(attention_sums[:, 2:4], axis=0).reshape(2, heads, head_size)
    ada_part = dot_left(silu_rows, mod_all)
    silu_grad = dot_right(mod_all, ada_weight[0])
    silu_grad = silu_grad + lax.ppermute(silu_grad, "section", [(0, 1), (1, 0)])
    silu_all = gather_small(silu_grad, count)
    gain_all = jnp.sum(gather_small(jnp.sum(head_sums, axis=1), count), axis=0)
    silu_all = jnp.swapaxes(silu_all, 0, 1).reshape(condition.shape)
    cond_grad = silu_all * sigma_cond * (1.0 + condition * (1.0 - sigma_cond))
    table_grad = lax.dot_general(
        label_hot.astype(f32),
        cond_grad,
        (((0,), (0,)), ((), ())),
        precision=lax.Precision.HIGHEST,
        preferred_element_type=f32,
    )
    return (
        result.reshape(1, images, patches, width),
        input_grads[None],
        table_grad,
        ada_part[None],
        rest_part[None, :, : 3 * width].astype(f32),
        rest_part[None, :, 3 * width :].astype(f32),
        columns_from_walk(gate_up_part[:, :hidden], count)[None].astype(f32),
        columns_from_walk(gate_up_part[:, hidden:], count)[None].astype(f32),
        down_part[None].astype(f32),
        gain_all[None, 0],
        gain_all[None, 1],
    )


def solution(mesh):
    placed = (
        P("dp", None, None),
        P("section", "dp", None, None),
        P("dp"),
        P("dp"),
        P("dp", None),
        P(),
        P("section", "dp", None),
        P("section", "dp", None),
        P("section", "dp", None),
        P("section", "dp", None),
        P("section", "dp", None),
        P("section", "dp", None),
        P("section", None),
        P("section", None),
    )
    return jax.shard_map(
        per_device,
        mesh=mesh,
        in_specs=placed,
        out_specs=(
            P("section", "dp", None, None),
            P("section", "dp", None, None),
            P(),
            P("section", "dp", None),
            P("section", "dp", None),
            P("section", "dp", None),
            P("section", "dp", None),
            P("section", "dp", None),
            P("section", "dp", None),
            P("section", None),
            P("section", None),
        ),
        check_vma=False,
    )
```

```python
import functools
import math

import jax
import jax.numpy as jnp
from jax import lax
from jax.experimental import pallas as pl
from jax.experimental.pallas import tpu as pltpu
from jax.sharding import PartitionSpec as P

GRID = 16
epsilon = 1e-06
f32 = jnp.float32
bf16 = jnp.bfloat16
LANES = 128
VMEM_BYTES = 56 * 1024 * 1024


def params():
    return pltpu.CompilerParams(vmem_limit_bytes=VMEM_BYTES)


def cost(flops, moved):
    return pl.CostEstimate(flops=int(flops), bytes_accessed=int(moved), transcendentals=0)


def dot(left, right):
    return jnp.dot(left, right, preferred_element_type=f32)


def dot_right(left, right):
    return lax.dot_general(left, right, (((1,), (1,)), ((), ())), preferred_element_type=f32)


def dot_left(left, right):
    return lax.dot_general(left, right, (((0,), (0,)), ((), ())), preferred_element_type=f32)


def whole_rows(ref, places):
    if len(places) == 1:
        return ref[places[0]]
    return jnp.concatenate([ref[place] for place in places], axis=0)


def part_place(index, parts, walked):
    if not walked:
        return index
    return index // 2 + (index % 2) * (parts - 1 - 2 * (index // 2))


def places_of(parts, walked):
    return [part_place(index, parts, walked) for index in range(parts)]


def two_terms(values):
    high = values.astype(bf16)
    low = (values - high.astype(f32)).astype(bf16)
    return jnp.concatenate([high, low], axis=1)


def inverse_rms(values):
    return lax.rsqrt(jnp.mean(values * values, axis=-1, keepdims=True) + epsilon)


def partner(values, first_half, quarter):
    width = values.shape[1]
    return jnp.where(
        first_half, pltpu.roll(values, width - quarter, 1), pltpu.roll(values, quarter, 1)
    )


def first_half_mask(shape, quarter):
    lane = lax.broadcasted_iota(jnp.int32, shape, 1)
    return lane % (2 * quarter) < quarter


def head_groups(heads, head_size):
    width = heads * head_size
    span = min(2 * LANES, width)
    groups = []
    for head in range(heads):
        low, high = head * head_size, (head + 1) * head_size
        if groups and high <= groups[-1][0] + span:
            groups[-1][2].append(head)
        else:
            groups.append((min(low // LANES * LANES, width - span), span, [head]))
    return groups


def head_mask(head, head_size, start, span):
    lane = lax.broadcasted_iota(jnp.int32, (1, span), 1) + start
    inside = jnp.logical_and(lane >= head * head_size, lane < (head + 1) * head_size)
    return inside.astype(f32).astype(bf16)


def side_by_side(parts):
    return parts[0] if len(parts) == 1 else jnp.concatenate(parts, axis=1)


def one_above_other(parts):
    return parts[0] if len(parts) == 1 else jnp.concatenate(parts, axis=0)


def rotated(raw, part, tables, keep_scale=None):
    cos, sin, gain_ref, summing, spreading, head_size = tables
    quarter = head_size // 4
    squares = dot((raw * raw).astype(bf16), summing)
    scale = lax.rsqrt(squares * (1.0 / head_size) + epsilon)
    scale = dot(two_terms(scale), spreading)
    if keep_scale is not None:
        keep_scale[part] = scale
    scaled = raw * scale * gain_ref[part : part + 1]
    first_half = first_half_mask((1, raw.shape[1]), quarter)
    return (scaled * cos + partner(scaled, first_half, quarter) * sin).astype(bf16)


def attention_forward_kernel(heads, places, first, keep, refs):
    if keep:
        received_ref, refs = refs[0], refs[1:]
    x_ref, mod_ref, cos_ref, sin_ref, gain_ref, sum_ref, spread_ref, repeat_ref = refs[:8]
    query_weight, joined_ref = refs[8:10]
    refs = refs[10:]
    patches, width = x_ref.shape
    if keep:
        outs, refs = refs[:8], refs[8:]
        weight, mixed, sems = refs[:3]
        held, out_sems = refs[3:11], refs[11]
    else:
        middle_ref, normed_two_ref, weight, mixed, sems = refs
    head_size = width // heads

    def fetch(part):
        return pltpu.make_async_copy(
            joined_ref.at[:, :, pl.ds((part + 1) * width, width)], weight.at[part], sems.at[part]
        )

    @pl.when(pl.program_id(0) == 0)
    def _():
        for part in range(3):
            fetch(part).start()

    def arrived(part):
        @pl.when(pl.program_id(0) == 0)
        def _():
            fetch(part).wait()

        return whole_rows(weight.at[part], places)

    def put(which):
        rows = pl.ds(first * patches, patches)
        return pltpu.make_async_copy(held[which], outs[which].at[rows], out_sems.at[which])

    flow = x_ref[...].astype(f32)
    if keep:
        flow = flow + received_ref[...].astype(f32)
    mod = mod_ref[0]
    normed = (flow * inverse_rms(flow) * (1.0 + mod[1:2]) + mod[0:1]).astype(bf16)
    cos, sin = dot(cos_ref[...], repeat_ref[...]), dot(sin_ref[...], repeat_ref[...])
    tables = (cos, sin, gain_ref, sum_ref[...], spread_ref[...], head_size)
    raw = dot(normed, whole_rows(query_weight, places))
    if keep:
        held[7][...] = flow.astype(bf16)
        held[0][...] = normed
        held[1][:, :width] = raw
        put(7).start()
        put(0).start()
    queries = rotated(raw, 0, tables)
    raw = dot(normed, arrived(0))
    if keep:
        held[1][:, width:] = raw
        put(1).start()
    keys = rotated(raw, 1, tables)
    values = dot(normed, arrived(1)).astype(bf16)
    if keep:
        held[2][...] = values
        put(2).start()
    mixed[...] = jnp.zeros_like(mixed)
    factor = head_size ** (-0.5) * math.log2(math.e)
    for start, span, members in head_groups(heads, head_size):
        window = slice(start, start + span)
        probs, parts = [], []
        for head in members:
            mask = head_mask(head, head_size, start, span)
            expon = jnp.exp2(dot_right(queries[:, window], keys[:, window] * mask) * factor)
            total = jnp.sum(expon, axis=-1, keepdims=True)
            probs.append((expon * (1.0 / total)).astype(bf16))
            parts.append(values[:, window] * mask)
        mixed[:, window] += dot(side_by_side(probs), one_above_other(parts))
    attended = mixed[...].astype(bf16)
    if keep:
        held[3][...] = attended
        put(3).start()
    branch = dot(attended, arrived(2))
    middle = flow + mod[2:3] * branch
    normed_two = (middle * inverse_rms(middle) * (1.0 + mod[4:5]) + mod[3:4]).astype(bf16)
    if keep:
        for which, value in ((4, branch), (5, middle), (6, normed_two)):
            held[which][...] = value
            put(which).start()
        for which in range(8):
            put(which).wait()
    else:
        middle_ref[...] = middle
        normed_two_ref[...] = normed_two


def attention_forward(x, received, mod, tables, gain, joined, walked, first, count, made=None):
    keep = received is not None
    images, unused, width = mod.shape
    tokens = x.shape[0]
    patches = tokens // images
    heads = width // tables[-1]
    cos, sin, *matrices, unused = tables
    parts, rows, unused = joined.shape
    row = lambda columns: pl.BlockSpec((patches, columns), lambda image: (first + image, 0))
    fixed = lambda array: pl.BlockSpec(array.shape, lambda image: (0,) * array.ndim)
    anywhere = pl.BlockSpec(memory_space=pl.ANY)
    shapes = [(width, f32), (width, bf16)]
    if keep:
        shapes = [
            (width, bf16),
            (2 * width, f32),
            (width, bf16),
            (width, bf16),
            (width, f32),
            (width, f32),
            (width, bf16),
            (width, bf16),
        ]
    made = [] if made is None else list(made)
    extra = [received] if keep else []
    inputs = 10 + len(extra)
    scratch = [
        pltpu.VMEM((3, parts, rows, width), bf16),
        pltpu.VMEM((patches, width), f32),
        pltpu.SemaphoreType.DMA((3,)),
    ]
    if keep:
        scratch += [pltpu.VMEM((patches, columns), kind) for columns, kind in shapes]
        scratch += [pltpu.SemaphoreType.DMA((len(shapes),))]

    def body(*refs):
        refs = refs[:inputs] + refs[inputs + len(made) :]
        attention_forward_kernel(heads, places_of(parts, walked), first, keep, refs)

    return pl.pallas_call(
        body,
        grid=(count,),
        in_specs=[pl.BlockSpec((patches, width), lambda image: (image, 0))] * len(extra)
        + [
            row(width),
            pl.BlockSpec((1, 8, width), lambda image: (first + image, 0, 0)),
            row(cos.shape[1]),
            row(sin.shape[1]),
            fixed(gain),
        ]
        + [fixed(matrix) for matrix in matrices]
        + [pl.BlockSpec((parts, rows, width), lambda image: (0, 0, 0))]
        + [anywhere] * (1 + len(made)),
        out_specs=[anywhere if keep else row(columns) for columns, kind in shapes],
        out_shape=[jax.ShapeDtypeStruct((tokens, columns), kind) for columns, kind in shapes],
        input_output_aliases={inputs + index: index for index in range(len(made))},
        scratch_shapes=scratch,
        compiler_params=params(),
        cost_estimate=cost(
            2 * count * patches * width * (4 * width + 2 * patches),
            8 * width * width + count * patches * width * 20,
        ),
    )(*extra, x, mod, cos, sin, gain, *matrices, joined, joined, *made)


def walk_chip(place, chips):
    return jnp.where(place < chips // 2, 2 * place, 2 * (chips - 1 - place) + 1)


def column_specs(joined, first, hidden, chips, step):
    parts, rows, unused = joined.shape
    if not chips:
        return [pl.BlockSpec((parts, rows, step), lambda i: (0, 0, first // step + i))]
    each = hidden // chips
    number = step // each

    def spec(which):
        return pl.BlockSpec(
            (parts, rows, each),
            lambda i: (0, 0, first // each + walk_chip(i * number + which, chips)),
        )

    return [spec(which) for which in range(number)]


def step_matrix(refs, places):
    return side_by_side([whole_rows(ref, places) for ref in refs])


def gate_up(normed_two, joined, hidden, walked, chips):
    tokens, width = normed_two.shape
    step = 768
    places = places_of(joined.shape[0], walked)
    gate_specs = column_specs(joined, 4 * width, hidden, chips, step)
    up_specs = column_specs(joined, 4 * width + hidden, hidden, chips, step)
    number = len(gate_specs)

    def body(normed_ref, *refs):
        normed = normed_ref[...]
        gate = dot(normed, step_matrix(refs[:number], places))
        up = dot(normed, step_matrix(refs[number : 2 * number], places))
        refs[-1][...] = (gate * (1.0 / (1.0 + jnp.exp(-gate))) * up).astype(bf16)

    return pl.pallas_call(
        body,
        grid=(hidden // step,),
        in_specs=[pl.BlockSpec((tokens, width), lambda i: (0, 0))] + gate_specs + up_specs,
        out_specs=pl.BlockSpec((tokens, step), lambda i: (0, i)),
        out_shape=jax.ShapeDtypeStruct((tokens, hidden), bf16),
        compiler_params=params(),
        cost_estimate=cost(4 * tokens * width * hidden, 4 * width * hidden + 2 * tokens * hidden),
    )(normed_two, *[joined] * (2 * number))


def down_projection(active, act, down, middle, mod, first, count, keep, step):
    hidden = act.shape[1]
    images, unused, width = mod.shape
    patches = act.shape[0] // images
    tokens = count * patches
    outs = [jax.ShapeDtypeStruct((tokens, width), bf16)]
    scratch = [pltpu.VMEM((tokens, width), f32)]
    if keep:
        outs.append(jax.ShapeDtypeStruct((tokens, width), f32))
        scratch = []

    def body(active_ref, act_ref, middle_ref, mod_ref, down_ref, result_ref, total):
        index = pl.program_id(0)

        @pl.when(active_ref[0] == 0)
        def _():
            result_ref[...] = jnp.zeros_like(result_ref)

        @pl.when(active_ref[0] != 0)
        def _():
            term = dot(act_ref[...], down_ref[...])

            @pl.when(index == 0)
            def _():
                total[...] = term

            @pl.when(index > 0)
            def _():
                total[...] += term

            @pl.when(index == hidden // step - 1)
            def _():
                for image in range(count):
                    at = slice(image * patches, (image + 1) * patches)
                    gate = mod_ref[first + image, 5:6]
                    result_ref[at] = (middle_ref[at] + gate * total[at]).astype(bf16)

    return pl.pallas_call(
        body,
        grid_spec=pltpu.PrefetchScalarGridSpec(
            num_scalar_prefetch=1,
            grid=(hidden // step,),
            in_specs=[
                pl.BlockSpec((tokens, step), lambda i, active: (first // count, i * active[0])),
                pl.BlockSpec((tokens, width), lambda i, active: (first // count, 0)),
                pl.BlockSpec(mod.shape, lambda i, active: (0, 0, 0)),
                pl.BlockSpec((step, width), lambda i, active: (i * active[0], 0)),
            ],
            out_specs=[pl.BlockSpec((tokens, width), lambda i, active: (0, 0))] * len(outs),
            scratch_shapes=scratch,
        ),
        out_shape=outs,
        compiler_params=params(),
        cost_estimate=cost(2 * tokens * width * hidden, 2 * width * hidden + 8 * tokens * width),
    )(active, act, middle, mod, down)


def incoming(cot_ref, back_refs, image, at):
    value = cot_ref[at].astype(f32)
    return value + back_refs[image][...].astype(f32) if back_refs else value


def mlp_gradient(cot, backs, mod, first, count):
    images, unused, width = mod.shape
    patches = cot.shape[0] // images

    def body(cot_ref, mod_ref, *refs):
        for image in range(count):
            at = slice(image * patches, (image + 1) * patches)
            grads = incoming(cot_ref, refs[: len(backs)], image, at)
            refs[-1][at] = (mod_ref[first + image, 5:6] * grads).astype(bf16)

    return pl.pallas_call(
        body,
        grid=(1,),
        in_specs=[
            pl.BlockSpec((count * patches, width), lambda i: (first // count, 0)),
            pl.BlockSpec(mod.shape, lambda i: (0, 0, 0)),
        ]
        + [pl.BlockSpec((patches, width), lambda i: (0, 0))] * len(backs),
        out_specs=pl.BlockSpec((count * patches, width), lambda i: (0, 0)),
        out_shape=jax.ShapeDtypeStruct((count * patches, width), bf16),
        compiler_params=params(),
        cost_estimate=cost(0, 6 * count * patches * width),
    )(cot, mod, *backs)


def stacked(refs):
    return refs[0][...] if len(refs) == 1 else jnp.concatenate([ref[...] for ref in refs], axis=0)


def whole_specs(arrays):
    return [pl.BlockSpec(array.shape, lambda i: (0, 0)) for array in arrays]


def act_backward(active, mlp_grads, down, step):
    hidden, width = down.shape
    tokens = sum(grad.shape[0] for grad in mlp_grads)

    def body(active_ref, *refs):
        @pl.when(active_ref[0] == 0)
        def _():
            refs[-1][...] = jnp.zeros_like(refs[-1])

        @pl.when(active_ref[0] != 0)
        def _():
            refs[-1][...] = dot_right(stacked(refs[:-2]), refs[-2][...]).astype(bf16)

    return pl.pallas_call(
        body,
        grid_spec=pltpu.PrefetchScalarGridSpec(
            num_scalar_prefetch=1,
            grid=(hidden // step,),
            in_specs=[pl.BlockSpec(grad.shape, lambda i, active: (0, 0)) for grad in mlp_grads]
            + [pl.BlockSpec((step, width), lambda i, active: (i * active[0], 0))],
            out_specs=pl.BlockSpec((tokens, step), lambda i, active: (0, i)),
        ),
        out_shape=jax.ShapeDtypeStruct((tokens, hidden), bf16),
        compiler_params=params(),
        cost_estimate=cost(2 * tokens * width * hidden, 2 * width * hidden + 4 * tokens * width),
    )(active, *mlp_grads, down)


def mlp_backward(
    cot, backs, act_grad, forward, joined, middle, mod, walked, chips, sums_of
):
    tokens, hidden = act_grad.shape
    images, unused, width = mod.shape
    patches = tokens // images
    parts, rows, unused = joined.shape
    places = places_of(parts, walked)
    step = 768
    count = hidden // step
    gate_specs = column_specs(joined, 4 * width, hidden, chips, step)
    up_specs = column_specs(joined, 4 * width + hidden, hidden, chips, step)
    number = len(gate_specs)
    fresh, keep = len(forward) == 1, sums_of is not None
    whole = pl.BlockSpec((tokens, width), lambda i: (0, 0))
    block = pl.BlockSpec((tokens, step), lambda i: (0, i))
    anywhere = pl.BlockSpec(memory_space=pl.ANY)
    late = [cot, middle] + (list(sums_of) if keep else [])

    def body(act_grad_ref, mod_ref, joined_ref, *refs):
        refs = list(refs)

        def taken(size):
            first = refs[:size]
            del refs[:size]
            return first

        gate_refs, up_refs = taken(number), taken(number)

        forward_refs, back_refs, sources = taken(len(forward)), taken(len(backs)), taken(len(late))
        middle_grad_ref, mixed_grad_ref = taken(2)
        fresh_refs = taken(3 if fresh else 0)
        kept_refs = taken(4 if keep else 0)
        total, out_weight, sem = taken(3)
        copies, (sems,) = taken(len(late)), refs
        cot_ref, middle_ref = copies[:2]
        index = pl.program_id(0)
        fetches = [
            pltpu.make_async_copy(joined_ref.at[:, :, pl.ds(3 * width, width)], out_weight, sem)
        ] + [
            pltpu.make_async_copy(source, copies[which], sems.at[which])
            for which, source in enumerate(sources)
        ]

        @pl.when(index == 0)
        def _():
            for fetch in fetches:
                fetch.start()

        gate_weight = step_matrix(gate_refs, places)
        up_weight = step_matrix(up_refs, places)
        if fresh:
            normed = forward_refs[0][...]
            gate, up = dot(normed, gate_weight), dot(normed, up_weight)
        else:
            gate, up = (ref[...].astype(f32) for ref in forward_refs)
        sigma = 1.0 / (1.0 + jnp.exp(-gate))
        slope = act_grad_ref[...].astype(f32) * sigma
        gate_grad = (slope * up * (1.0 + gate * (1.0 - sigma))).astype(bf16)
        up_grad = (slope * gate).astype(bf16)
        if fresh:
            fresh_refs[0][...] = (gate * sigma * up).astype(bf16)
            fresh_refs[1][...] = gate.astype(bf16)
            fresh_refs[2][...] = up.astype(bf16)
        if keep:
            kept_refs[0][...] = gate_grad
            kept_refs[1][...] = up_grad
        term = dot_right(gate_grad, gate_weight) + dot_right(up_grad, up_weight)

        @pl.when(index == 0)
        def _():
            total[...] = term

        @pl.when(index > 0)
        def _():
            total[...] += term

        @pl.when(index == count - 1)
        def _():
            for fetch in fetches:
                fetch.wait()
            matrix = whole_rows(out_weight, places)
            for image in range(images):
                at = slice(image * patches, (image + 1) * patches)
                mod = mod_ref[image]
                grad, flow = total[at], middle_ref[at]
                inverse = inverse_rms(flow)
                normal = flow * inverse
                scaled = grad * (1.0 + mod[4:5])
                mean = jnp.mean(scaled * normal, axis=-1, keepdims=True)
                out_grad = incoming(cot_ref, back_refs, image, at)
                middle_grad = out_grad + (scaled - normal * mean) * inverse
                middle_grad_ref[at] = middle_grad
                branch_grad = (mod[2:3] * middle_grad).astype(bf16)
                mixed_grad_ref[at] = dot_right(branch_grad, matrix).astype(bf16)
                if keep:
                    mlp_ref, branch_ref = copies[2:]
                    kept_refs[2][at] = branch_grad
                    terms = [middle_grad * branch_ref[at], grad, grad * normal, out_grad * mlp_ref[at]]
                    for place, value in enumerate(terms):
                        kept_refs[3][image, place : place + 1] = jnp.sum(value, axis=0, keepdims=True)

    out_shapes = [
        jax.ShapeDtypeStruct((tokens, width), f32),
        jax.ShapeDtypeStruct((tokens, width), bf16),
    ]
    out_specs = [whole, whole]
    if fresh:
        out_shapes += [jax.ShapeDtypeStruct((tokens, hidden), bf16)] * 3
        out_specs += [block] * 3
    if keep:
        out_shapes += [jax.ShapeDtypeStruct((tokens, hidden), bf16)] * 2
        out_shapes += [jax.ShapeDtypeStruct((tokens, width), bf16)]
        out_shapes += [jax.ShapeDtypeStruct((images, 8, width), f32)]
        out_specs += [block, block, whole, pl.BlockSpec((images, 8, width), lambda i: (0, 0, 0))]
    return pl.pallas_call(
        body,
        grid=(count,),
        in_specs=[block, pl.BlockSpec(mod.shape, lambda i: (0, 0, 0)), anywhere]
        + gate_specs
        + up_specs
        + [whole if fresh else block] * len(forward)
        + [pl.BlockSpec((patches, width), lambda i: (0, 0))] * len(backs)
        + [anywhere] * len(late),
        out_specs=out_specs,
        out_shape=out_shapes,
        scratch_shapes=[
            pltpu.VMEM((tokens, width), f32),
            pltpu.VMEM((parts, rows, width), bf16),
            pltpu.SemaphoreType.DMA,
        ]
        + [pltpu.VMEM(array.shape, array.dtype) for array in late]
        + [pltpu.SemaphoreType.DMA((len(late),))],
        compiler_params=params(),
        cost_estimate=cost(
            2 * tokens * width * (4 * hidden + width), 4 * width * hidden + 6 * tokens * hidden
        ),
    )(act_grad, mod, joined, *[joined] * (2 * number), *forward, *backs, *late)


def attention_backward_kernel(heads, places, first, keep, refs):
    raw_hbm, value_hbm, mixed_grad_hbm, middle_grad_hbm, x_hbm = refs[:5]
    mod_ref, cos_ref, sin_ref, gain_ref, sum_ref, spread_ref, repeat_ref, joined_ref = refs[5:13]
    refs = refs[13:]
    if keep:
        flow_grad_ref, qkv_grad_ref, sums_ref = refs[:3]
        refs = refs[3:]
    else:
        back_ref = refs[0]
        refs = refs[1:]
    weight, scales, query_total, key_total, value_total = refs[:5]
    raw_ref, value_ref, mixed_grad_ref, middle_grad_ref, x_ref, sems = refs[5:]
    patches, width = x_ref.shape
    head_size = width // heads
    quarter = head_size // 4
    factor = head_size ** (-0.5)
    image = pl.program_id(0)
    rows = pl.ds((first + image) * patches, patches)
    sources = [
        raw_hbm.at[rows, pl.ds(0, width)],
        raw_hbm.at[rows, pl.ds(width, width)],
        value_hbm.at[rows],
        mixed_grad_hbm.at[rows],
        middle_grad_hbm.at[rows],
        x_hbm.at[rows],
    ]
    targets = [raw_ref.at[0], raw_ref.at[1], value_ref, mixed_grad_ref, middle_grad_ref, x_ref]
    copies = [
        pltpu.make_async_copy(source, target, sems.at[3 + which])
        for which, (source, target) in enumerate(zip(sources, targets))
    ]
    for copy in copies[:4]:
        copy.start()

    def fetch(part):
        return pltpu.make_async_copy(
            joined_ref.at[:, :, pl.ds(part * width, width)], weight.at[part], sems.at[part]
        )

    @pl.when(image == 0)
    def _():
        for part in range(3):
            fetch(part).start()

    for copy in copies[4:]:
        copy.start()
    first_half = first_half_mask((1, width), quarter)
    cos, sin = dot(cos_ref[...], repeat_ref[...]), dot(sin_ref[...], repeat_ref[...])
    summing, spreading = sum_ref[...], spread_ref[...]
    tables = (cos, sin, gain_ref, summing, spreading, head_size)
    copies[0].wait()
    queries = rotated(raw_ref[0], 0, tables, scales)
    copies[1].wait()
    keys = rotated(raw_ref[1], 1, tables, scales)
    for copy in copies[2:4]:
        copy.wait()
    values, mixed_grad = value_ref[...], mixed_grad_ref[...]
    query_total[...] = jnp.zeros_like(query_total)
    key_total[...] = jnp.zeros_like(key_total)
    value_total[...] = jnp.zeros_like(value_total)
    for start, span, members in head_groups(heads, head_size):
        window = slice(start, start + span)
        probs, slopes, key_parts, query_parts, grad_parts = [], [], [], [], []
        for head in members:
            mask = head_mask(head, head_size, start, span)
            key_part, query_part = keys[:, window] * mask, queries[:, window] * mask
            grad_part = mixed_grad[:, window] * mask
            scores = dot_right(key_part, queries[:, window])
            expon = jnp.exp2(scores * (factor * math.log2(math.e)))
            prob = expon * (1.0 / jnp.sum(expon, axis=0, keepdims=True))
            prob_grad = dot_right(values[:, window], grad_part)
            middle = jnp.sum(prob * prob_grad, axis=0, keepdims=True)
            probs.append(prob.astype(bf16))
            slopes.append((prob * (prob_grad - middle)).astype(bf16))
            key_parts.append(key_part)
            query_parts.append(query_part)
            grad_parts.append(grad_part)
        value_total[:, window] += dot(side_by_side(probs), one_above_other(grad_parts))
        key_total[:, window] += dot(side_by_side(slopes), one_above_other(query_parts))
        query_total[:, window] += dot_left(one_above_other(slopes), one_above_other(key_parts))

    def raw_grad(part, total):
        turned = total[...] * factor
        grad = turned * cos + partner(turned * sin, first_half, quarter)
        scale = scales[part]
        normal = raw_ref[part] * scale
        if keep:
            sums_ref[0, 2 + part : 3 + part] = jnp.sum(grad * normal, axis=0, keepdims=True)
        grad = grad * gain_ref[part : part + 1]
        mean = dot((grad * normal).astype(bf16), summing) * (1.0 / head_size)
        mean = dot(two_terms(mean), spreading)
        return (scale * (grad - normal * mean)).astype(bf16)

    def arrived(part):
        @pl.when(image == 0)
        def _():
            fetch(part).wait()

        return whole_rows(weight.at[part], places)

    parts = [raw_grad(0, query_total), raw_grad(1, key_total), value_total[...].astype(bf16)]
    grad = None
    for part in range(3):
        if keep:
            qkv_grad_ref[:, part * width : (part + 1) * width] = parts[part]
        term = dot_right(parts[part], arrived(part))
        grad = term if grad is None else grad + term
    for copy in copies[4:]:
        copy.wait()
    mod = mod_ref[0]
    flow = x_ref[...].astype(f32)
    inverse = inverse_rms(flow)
    normal = flow * inverse
    scaled = grad * (1.0 + mod[1:2])
    mean = jnp.mean(scaled * normal, axis=-1, keepdims=True)
    flow_grad = middle_grad_ref[...] + (scaled - normal * mean) * inverse
    if keep:
        flow_grad_ref[...] = flow_grad
        sums_ref[0, 0:1] = jnp.sum(grad, axis=0, keepdims=True)
        sums_ref[0, 1:2] = jnp.sum(grad * normal, axis=0, keepdims=True)
    else:
        back_ref[...] = flow_grad.astype(bf16)


def attention_backward(
    active, raw, value, mixed_grad, middle_grad, x, mod, tables, gain, joined, walked, first, count, keep
):
    images, unused, width = mod.shape
    patches = x.shape[0] // images
    tokens = count * patches
    heads = width // tables[-1]
    cos, sin, *matrices, unused = tables
    parts, rows, unused = joined.shape
    row = lambda columns: pl.BlockSpec((patches, columns), lambda image: (first + image, 0))
    token = lambda columns: pl.BlockSpec((patches, columns), lambda image: (image, 0))
    fixed = lambda array: pl.BlockSpec(array.shape, lambda image: (0,) * array.ndim)
    anywhere = pl.BlockSpec(memory_space=pl.ANY)
    out_shapes = [jax.ShapeDtypeStruct((tokens, width), bf16)]
    out_specs = [token(width)]
    if keep:
        out_shapes = [
            jax.ShapeDtypeStruct((tokens, width), f32),
            jax.ShapeDtypeStruct((tokens, 3 * width), bf16),
            jax.ShapeDtypeStruct((count, 8, width), f32),
        ]
        out_specs = [
            token(width),
            token(3 * width),
            pl.BlockSpec((1, 8, width), lambda image: (image, 0, 0)),
        ]

    def body(active_ref, *refs):
        @pl.when(active_ref[0] == 0)
        def _():
            for ref in refs[13 : 13 + len(out_shapes)]:
                ref[...] = jnp.zeros_like(ref)

        @pl.when(active_ref[0] != 0)
        def _():
            attention_backward_kernel(heads, places_of(parts, walked), first, keep, refs)

    return pl.pallas_call(
        body,
        grid=(count,),
        in_specs=[pl.BlockSpec(memory_space=pltpu.SMEM)]
        + [anywhere] * 5
        + [
            pl.BlockSpec((1, 8, width), lambda image: (first + image, 0, 0)),
            row(cos.shape[1]),
            row(sin.shape[1]),
            fixed(gain),
        ]
        + [fixed(matrix) for matrix in matrices]
        + [anywhere],
        out_specs=out_specs,
        out_shape=out_shapes,
        scratch_shapes=[
            pltpu.VMEM((3, parts, rows, width), bf16),
            pltpu.VMEM((2, patches, width), f32),
            pltpu.VMEM((patches, width), f32),
            pltpu.VMEM((patches, width), f32),
            pltpu.VMEM((patches, width), f32),
            pltpu.VMEM((2, patches, width), f32),
            pltpu.VMEM((patches, width), bf16),
            pltpu.VMEM((patches, width), bf16),
            pltpu.VMEM((patches, width), f32),
            pltpu.VMEM((patches, width), bf16),
            pltpu.SemaphoreType.DMA((9,)),
        ],
        compiler_params=params(),
        cost_estimate=cost(
            2 * tokens * width * (3 * width + 5 * patches),
            6 * width * width + tokens * width * 20,
        ),
    )(active, raw, value, mixed_grad, middle_grad, x, mod, cos, sin, gain, *matrices, joined)


def down_grad(mlp_grads, cot, back, act, mod, step):
    tokens, hidden = act.shape
    images, unused, width = mod.shape
    patches = tokens // images
    last = images - 1

    def body(act_ref, cot_ref, back_ref, mod_ref, *refs):
        given, (out_ref, last_ref, mlp_grad) = refs[:last], refs[last:]

        @pl.when(pl.program_id(0) == 0)
        def _():
            grads = incoming(cot_ref, [back_ref], 0, slice(0, patches))
            value = (mod_ref[last, 5:6] * grads).astype(bf16)
            last_ref[...] = value
            for image in range(last):
                mlp_grad[image * patches : (image + 1) * patches] = given[image][...]
            mlp_grad[last * patches :] = value

        out_ref[...] = dot_left(act_ref[...], mlp_grad[...]).astype(bf16)

    return pl.pallas_call(
        body,
        grid=(hidden // step,),
        in_specs=[
            pl.BlockSpec((tokens, step), lambda i: (0, i)),
            pl.BlockSpec((patches, width), lambda i: (last, 0)),
            pl.BlockSpec((patches, width), lambda i: (0, 0)),
            pl.BlockSpec(mod.shape, lambda i: (0, 0, 0)),
        ]
        + whole_specs(mlp_grads),
        out_specs=[
            pl.BlockSpec((step, width), lambda i: (i, 0)),
            pl.BlockSpec((patches, width), lambda i: (0, 0)),
        ],
        out_shape=[
            jax.ShapeDtypeStruct((hidden, width), bf16),
            jax.ShapeDtypeStruct((patches, width), bf16),
        ],
        scratch_shapes=[pltpu.VMEM((tokens, width), bf16)],
        compiler_params=params(),
        cost_estimate=cost(2 * tokens * width * hidden, 2 * width * hidden),
    )(act, cot, back, mod, *mlp_grads)


def matrix_grad_kernel(places, counts, *refs):
    pairs = len(counts)
    inputs, grads, out_ref = refs[:pairs], refs[pairs : 2 * pairs], refs[2 * pairs]
    rows = out_ref.shape[1]
    step = pl.program_id(0)
    first = 0
    for index in range(pairs):

        @pl.when(jnp.logical_and(step >= first, step < first + counts[index]))
        def _(index=index):
            product = dot_left(inputs[index][...], grads[index][...]).astype(bf16)
            for part, place in enumerate(places):
                out_ref[place] = product[part * rows : (part + 1) * rows]

        first += counts[index]


def matrix_grad(inputs, grads, step, parts, walked):
    tokens, width = inputs[0].shape
    counts = [grad.shape[1] // step for grad in grads]
    columns = sum(counts) * step
    rows = width // parts
    firsts = [sum(counts[:index]) for index in range(len(counts))]

    def grad_spec(first, count):
        return pl.BlockSpec((tokens, step), lambda i: (0, jnp.clip(i - first, 0, count - 1)))

    return pl.pallas_call(
        functools.partial(matrix_grad_kernel, places_of(parts, walked), counts),
        grid=(sum(counts),),
        in_specs=[pl.BlockSpec((tokens, width), lambda i: (0, 0))] * len(inputs)
        + [grad_spec(first, count) for first, count in zip(firsts, counts)],
        out_specs=pl.BlockSpec((parts, rows, step), lambda i: (0, 0, i)),
        out_shape=jax.ShapeDtypeStruct((parts, rows, columns), bf16),
        compiler_params=params(),
        cost_estimate=cost(2 * tokens * width * columns, 2 * width * columns),
    )(*inputs, *grads)


def walk_of(count):
    chips = count // 2
    order = [chip for chip in range(chips) if chip % 2 == 0]
    order += [chip for chip in reversed(range(chips)) if chip % 2 == 1]
    return [2 * chip + core for chip in order for core in (0, 1)]


def from_walk(rows, count):
    blocks = rows.reshape(count // 2, -1, rows.shape[-1])
    places = places_of(count // 2, True)
    return jnp.concatenate([blocks[place] for place in places], axis=0)


def columns_to_walk(matrix, count):
    each = matrix.shape[1] // (count // 2)
    chips = [device // 2 for device in walk_of(count)[::2]]
    return jnp.concatenate([matrix[:, chip * each : (chip + 1) * each] for chip in chips], axis=1)


def columns_from_walk(matrix, count):
    each = matrix.shape[1] // (count // 2)
    places = places_of(count // 2, True)
    return jnp.concatenate(
        [matrix[:, place * each : (place + 1) * each] for place in places], axis=1
    )


def to_walk(rows, count):
    blocks = rows.reshape(count // 2, -1, rows.shape[-1])
    return jnp.concatenate([blocks[device // 2] for device in walk_of(count)[::2]], axis=0)


def gather_walk(rows, count):
    return lax.all_gather(rows, "dp", axis=0, tiled=True, axis_index_groups=[walk_of(count)])


def scatter_walk(rows, groups):
    part = lax.psum_scatter(
        rows, "dp", scatter_dimension=0, tiled=True, axis_index_groups=groups
    )
    return lax.optimization_barrier(part)


def scatter_cores(rows, count):
    me = lax.axis_index("dp")
    width = rows.shape[-1]
    pairs = rows.reshape(count // 2, 2, -1, width)
    give = lax.dynamic_index_in_dim(pairs, 1 - me % 2, 1, keepdims=False)
    keep = lax.dynamic_index_in_dim(pairs, me % 2, 1, keepdims=False)
    both = keep.astype(f32) + swapped(give, 1, count).astype(f32)
    both = both.astype(bf16).reshape(-1, width)
    walk = walk_of(count)
    return both, [walk[0::2], walk[1::2]]


def as_parts(rows, count):
    each = rows.shape[0] // (count // 2)
    if each % 16 == 0:
        return rows.reshape(count // 2, each, rows.shape[1]), True
    whole = from_walk(rows, count)
    return whole[None], False


def swapped(block, bit, count):
    return lax.ppermute(block, "dp", [(device, device ^ bit) for device in range(count)])


def gather_small(block, count):
    me = lax.axis_index("dp")
    block = block[None]
    bit = count // 2
    while bit:
        other = swapped(block, bit, count)
        low = (me & bit) == 0
        pair = [jnp.where(low, block, other), jnp.where(low, other, block)]
        block = jnp.stack(pair, axis=1).reshape(2 * block.shape[0], *block.shape[1:])
        bit //= 2
    return block


def scatter_small(blocks, count):
    me = lax.axis_index("dp")
    bit = 1
    while bit < count:
        pairs = blocks.reshape(blocks.shape[0] // 2, 2, *blocks.shape[1:])
        mine = jnp.where((me & bit) == 0, 0, 1)
        give = lax.dynamic_index_in_dim(pairs, 1 - mine, 1, keepdims=False)
        keep = lax.dynamic_index_in_dim(pairs, mine, 1, keepdims=False)
        blocks = keep + swapped(give, bit, count)
        bit *= 2
    return blocks[0]


def time_features(timestep_ids, width):
    half_width = width // 2
    frequency = jnp.exp(-math.log(10000.0) * jnp.arange(half_width, dtype=f32) / half_width)
    angle_rows = timestep_ids.astype(f32)[:, None] * frequency[None, :]
    return jnp.concatenate([jnp.cos(angle_rows), jnp.sin(angle_rows)], axis=-1)


def rotation_tables(positions, width, head_size):
    quarter = head_size // 4
    frequency = jnp.exp(-math.log(10000.0) * jnp.arange(quarter, dtype=f32) / quarter)
    places = positions.reshape(-1, 1)
    row_angle = (places // GRID).astype(f32) * frequency
    col_angle = (places % GRID).astype(f32) * frequency
    row_cos, row_sin = jnp.cos(row_angle), jnp.sin(row_angle)
    col_cos, col_sin = jnp.cos(col_angle), jnp.sin(col_angle)
    cos = jnp.concatenate([row_cos, row_cos, col_cos, col_cos], axis=1)
    sin = jnp.concatenate([-row_sin, row_sin, -col_sin, col_sin], axis=1)
    padding = ((0, 0), (0, LANES - head_size))
    number = jnp.arange(LANES)
    column = jnp.arange(width)
    summing = (column[:, None] // head_size == number[None, :]).astype(bf16)
    spreading = (column[None, :] // head_size == number[:, None]).astype(bf16)
    repeating = (column[None, :] % head_size == number[:, None]).astype(bf16)
    return (
        two_terms(jnp.pad(cos, padding)),
        two_terms(jnp.pad(sin, padding)),
        summing,
        jnp.concatenate([spreading, spreading]),
        jnp.concatenate([repeating, repeating]),
    )


def per_device(
    tokens,
    cotangent,
    labels,
    timesteps,
    positions,
    label_table,
    ada_weight,
    qkv_weight,
    out_weight,
    gate_weight,
    up_weight,
    down_weight,
    q_gain,
    k_gain,
):
    first_section = lax.axis_index("section") == 0
    first_only = first_section.astype(jnp.int32).reshape(1)
    second_only = 1 - first_only
    always = jnp.ones((1,), jnp.int32)
    count = lax.axis_size("dp")
    me = lax.axis_index("dp")
    images, patches, width = tokens.shape
    hidden = gate_weight.shape[2]
    head_size = q_gain.shape[1]
    heads = width // head_size
    rows = ada_weight.shape[1]
    classes = label_table.shape[0]

    gate_matrix, up_matrix, chips = gate_weight[0], up_weight[0], count // 2
    if hidden // chips % LANES:
        gate_matrix, up_matrix = columns_to_walk(gate_matrix, count), columns_to_walk(up_matrix, count)
        chips = 0
    joined = gather_walk(
        jnp.concatenate([qkv_weight[0], out_weight[0], gate_matrix, up_matrix], axis=1), count
    )

    ids = gather_small(jnp.stack([labels, timesteps]), count)
    all_labels = ids[:, 0].reshape(-1)
    all_times = ids[:, 1].reshape(-1)
    label_hot = all_labels[:, None] == jnp.arange(classes, dtype=jnp.int32)[None, :]
    condition = dot(label_hot.astype(bf16), label_table) + time_features(all_times, width)
    sigma_cond = jax.nn.sigmoid(condition)
    silu_cond = (condition * sigma_cond).astype(bf16)
    silu_rows = lax.dynamic_slice_in_dim(silu_cond, me * rows, rows, 1)
    mod_part = dot(silu_rows, ada_weight[0])
    mod = scatter_small(mod_part.reshape(count, images, -1), count).reshape(images, 6, width)
    mod = jnp.pad(mod, ((0, 0), (0, 2), (0, 0)))
    tables = rotation_tables(positions, width, head_size)
    flat = tokens.reshape(images * patches, width)
    own = jnp.where(first_section, flat, jnp.zeros_like(flat))

    down, joined, mod, own, tables = lax.optimization_barrier(
        (down_weight[0], joined, mod, own, tables)
    )
    down = gather_walk(down, count)
    joined, walked = as_parts(joined, count)
    tables = (*tables, head_size)
    gain = jnp.pad(jnp.tile(jnp.concatenate([q_gain, k_gain]), (1, heads)), ((0, 6), (0, 0)))

    cot = cotangent[0].reshape(images * patches, width)
    middle, normed_two = attention_forward(
        flat, None, mod, tables, gain, joined, walked, 0, images
    )
    act = gate_up(normed_two, joined, hidden, walked, chips)
    received = []
    for image in range(images):
        (early,) = down_projection(
            first_only, act, down, middle, mod, image, 1, False, hidden // 2
        )
        received.append(lax.ppermute(early, "section", [(0, 1)]))
    mlp_grad, unused = lax.optimization_barrier((mlp_gradient(cot, [], mod, 0, images), early))
    mlp_grads = [mlp_grad]
    act_grad = act_backward(second_only, mlp_grads, down, hidden // 2)
    kept = None
    for image in range(images):
        kept = attention_forward(
            own, received[image], mod, tables, gain, joined, walked, image, 1, kept
        )
    normed, raw, values, attended, branch, middle, normed_two, layer_in = kept

    middle_grad, mixed_grad, act, gate, up = mlp_backward(
        cot, [], act_grad, [normed_two], joined, middle, mod, walked, chips, None
    )
    backs = []
    for image in range(images):
        (early,) = attention_backward(
            second_only,
            raw,
            values,
            mixed_grad,
            middle_grad,
            layer_in,
            mod,
            tables,
            gain,
            joined,
            walked,
            image,
            1,
            False,
        )
        backs.append(lax.ppermute(early, "section", [(1, 0)]))
    late_act, unused = lax.optimization_barrier((act, early))
    result, mlp = down_projection(
        always, late_act, down, middle, mod, 0, images, True, hidden // 2
    )

    late_cot, unused = lax.optimization_barrier((cot, mlp))
    mlp_grads = [
        mlp_gradient(late_cot, [back], mod, image, 1) for image, back in enumerate(backs[:-1])
    ]
    down_term, mlp_grad = down_grad(mlp_grads, late_cot, backs[-1], act, mod, hidden // 4)
    mlp_grads = [*mlp_grads, mlp_grad]
    down_term, mlp_grads = lax.optimization_barrier((down_term, mlp_grads))
    down_part = scatter_walk(down_term, [walk_of(count)])
    act_grad = act_backward(always, mlp_grads, down, hidden // 2)
    middle_grad, mixed_grad, gate_grad, up_grad, branch_grad, mlp_sums = mlp_backward(
        cot, backs, act_grad, [gate, up], joined, middle, mod, walked, chips, [mlp, branch]
    )

    def matrix_term(inputs, grads, step):
        term = matrix_grad(inputs, grads, step, joined.shape[0], walked).reshape(width, -1)
        return term if walked else to_walk(term, count)

    gate_up_term = matrix_term([normed_two, normed_two], [gate_grad, up_grad], hidden // 2)
    gate_up_term, down_part = lax.optimization_barrier((gate_up_term, down_part))
    gate_up_part = scatter_walk(gate_up_term, [walk_of(count)])
    flow_grad, qkv_grad, attention_sums = attention_backward(
        always,
        raw,
        values,
        mixed_grad,
        middle_grad,
        layer_in,
        mod,
        tables,
        gain,
        joined,
        walked,
        0,
        images,
        True,
    )
    rest_term = matrix_term([normed, attended], [qkv_grad, branch_grad], width)
    rest_term, attention_sums = lax.optimization_barrier((rest_term, attention_sums))
    rest_term, groups = scatter_cores(rest_term, count)
    mod_grad = jnp.concatenate([attention_sums[:, :2], mlp_sums[:, :4]], axis=1)
    mod_grad = mod_grad.reshape(images, -1).astype(bf16)
    mod_all = gather_small(mod_grad, count).reshape(-1, mod_grad.shape[1])
    rest_term, gate_up_part, mod_all = lax.optimization_barrier((rest_term, gate_up_part, mod_all))
    rest_part = scatter_walk(rest_term, groups)
    flow_grad = flow_grad.reshape(images, patches, width)
    input_grads = jnp.where(first_section, flow_grad, flow_grad.astype(bf16).astype(f32))

    head_sums = jnp.sum(attention_sums[:, 2:4], axis=0).reshape(2, heads, head_size)
    ada_part = dot_left(silu_rows, mod_all)
    silu_grad = dot_right(mod_all, ada_weight[0])
    silu_grad = silu_grad + lax.ppermute(silu_grad, "section", [(0, 1), (1, 0)])
    silu_all = gather_small(silu_grad, count)
    gain_all = jnp.sum(gather_small(jnp.sum(head_sums, axis=1), count), axis=0)
    silu_all = jnp.swapaxes(silu_all, 0, 1).reshape(condition.shape)
    cond_grad = silu_all * sigma_cond * (1.0 + condition * (1.0 - sigma_cond))
    table_grad = lax.dot_general(
        label_hot.astype(f32),
        cond_grad,
        (((0,), (0,)), ((), ())),
        precision=lax.Precision.HIGHEST,
        preferred_element_type=f32,
    )
    return (
        result.reshape(1, images, patches, width),
        input_grads[None],
        table_grad,
        ada_part[None],
        rest_part[None, :, : 3 * width].astype(f32),
        rest_part[None, :, 3 * width :].astype(f32),
        columns_from_walk(gate_up_part[:, :hidden], count)[None].astype(f32),
        columns_from_walk(gate_up_part[:, hidden:], count)[None].astype(f32),
        down_part[None].astype(f32),
        gain_all[None, 0],
        gain_all[None, 1],
    )


def solution(mesh):
    placed = (
        P("dp", None, None),
        P("section", "dp", None, None),
        P("dp"),
        P("dp"),
        P("dp", None),
        P(),
        P("section", "dp", None),
        P("section", "dp", None),
        P("section", "dp", None),
        P("section", "dp", None),
        P("section", "dp", None),
        P("section", "dp", None),
        P("section", None),
        P("section", None),
    )
    return jax.shard_map(
        per_device,
        mesh=mesh,
        in_specs=placed,
        out_specs=(
            P("section", "dp", None, None),
            P("section", "dp", None, None),
            P(),
            P("section", "dp", None),
            P("section", "dp", None),
            P("section", "dp", None),
            P("section", "dp", None),
            P("section", "dp", None),
            P("section", "dp", None),
            P("section", None),
            P("section", None),
        ),
        check_vma=False,
    )
```

```python
import functools
import math

import jax
import jax.numpy as jnp
from jax import lax
from jax.experimental import pallas as pl
from jax.experimental.pallas import tpu as pltpu
from jax.sharding import PartitionSpec as P

GRID = 16
epsilon = 1e-06
f32 = jnp.float32
bf16 = jnp.bfloat16
LANES = 128
VMEM_BYTES = 56 * 1024 * 1024


def params():
    return pltpu.CompilerParams(vmem_limit_bytes=VMEM_BYTES)


def cost(flops, moved):
    return pl.CostEstimate(flops=int(flops), bytes_accessed=int(moved), transcendentals=0)


def dot(left, right):
    return jnp.dot(left, right, preferred_element_type=f32)


def dot_right(left, right):
    return lax.dot_general(left, right, (((1,), (1,)), ((), ())), preferred_element_type=f32)


def dot_left(left, right):
    return lax.dot_general(left, right, (((0,), (0,)), ((), ())), preferred_element_type=f32)


def whole_rows(ref, places):
    if len(places) == 1:
        return ref[places[0]]
    return jnp.concatenate([ref[place] for place in places], axis=0)


def part_place(index, parts, walked):
    if not walked:
        return index
    return index // 2 + (index % 2) * (parts - 1 - 2 * (index // 2))


def places_of(parts, walked):
    return [part_place(index, parts, walked) for index in range(parts)]


def two_terms(values):
    high = values.astype(bf16)
    low = (values - high.astype(f32)).astype(bf16)
    return jnp.concatenate([high, low], axis=1)


def inverse_rms(values):
    return lax.rsqrt(jnp.mean(values * values, axis=-1, keepdims=True) + epsilon)


def partner(values, first_half, quarter):
    width = values.shape[1]
    return jnp.where(
        first_half, pltpu.roll(values, width - quarter, 1), pltpu.roll(values, quarter, 1)
    )


def first_half_mask(shape, quarter):
    lane = lax.broadcasted_iota(jnp.int32, shape, 1)
    return lane % (2 * quarter) < quarter


def head_groups(heads, head_size):
    width = heads * head_size
    span = min(2 * LANES, width)
    groups = []
    for head in range(heads):
        low, high = head * head_size, (head + 1) * head_size
        if groups and high <= groups[-1][0] + span:
            groups[-1][2].append(head)
        else:
            groups.append((min(low // LANES * LANES, width - span), span, [head]))
    return groups


def head_mask(head, head_size, start, span):
    lane = lax.broadcasted_iota(jnp.int32, (1, span), 1) + start
    inside = jnp.logical_and(lane >= head * head_size, lane < (head + 1) * head_size)
    return inside.astype(f32).astype(bf16)


def side_by_side(parts):
    return parts[0] if len(parts) == 1 else jnp.concatenate(parts, axis=1)


def one_above_other(parts):
    return parts[0] if len(parts) == 1 else jnp.concatenate(parts, axis=0)


def rotated(raw, part, tables, keep_scale=None):
    cos, sin, gain_ref, summing, spreading, head_size = tables
    quarter = head_size // 4
    squares = dot((raw * raw).astype(bf16), summing)
    scale = lax.rsqrt(squares * (1.0 / head_size) + epsilon)
    scale = dot(two_terms(scale), spreading)
    if keep_scale is not None:
        keep_scale[part] = scale
    scaled = raw * scale * gain_ref[part : part + 1]
    first_half = first_half_mask((1, raw.shape[1]), quarter)
    return (scaled * cos + partner(scaled, first_half, quarter) * sin).astype(bf16)


def attention_forward_kernel(heads, places, first, keep, refs):
    if keep:
        received_ref, refs = refs[0], refs[1:]
    x_ref, mod_ref, cos_ref, sin_ref, gain_ref, sum_ref, spread_ref, repeat_ref = refs[:8]
    query_weight, joined_ref = refs[8:10]
    refs = refs[10:]
    patches, width = x_ref.shape
    if keep:
        outs, refs = refs[:8], refs[8:]
        weight, mixed, sems = refs[:3]
        held, out_sems = refs[3:11], refs[11]
    else:
        middle_ref, normed_two_ref, weight, mixed, sems = refs
    head_size = width // heads

    def fetch(part):
        return pltpu.make_async_copy(
            joined_ref.at[:, :, pl.ds((part + 1) * width, width)], weight.at[part], sems.at[part]
        )

    @pl.when(pl.program_id(0) == 0)
    def _():
        for part in range(3):
            fetch(part).start()

    def arrived(part):
        @pl.when(pl.program_id(0) == 0)
        def _():
            fetch(part).wait()

        return whole_rows(weight.at[part], places)

    def put(which):
        rows = pl.ds(first * patches, patches)
        return pltpu.make_async_copy(held[which], outs[which].at[rows], out_sems.at[which])

    flow = x_ref[...].astype(f32)
    if keep:
        flow = flow + received_ref[...].astype(f32)
    mod = mod_ref[0]
    normed = (flow * inverse_rms(flow) * (1.0 + mod[1:2]) + mod[0:1]).astype(bf16)
    cos, sin = dot(cos_ref[...], repeat_ref[...]), dot(sin_ref[...], repeat_ref[...])
    tables = (cos, sin, gain_ref, sum_ref[...], spread_ref[...], head_size)
    raw = dot(normed, whole_rows(query_weight, places))
    if keep:
        held[7][...] = flow.astype(bf16)
        held[0][...] = normed
        held[1][:, :width] = raw
        put(7).start()
        put(0).start()
    queries = rotated(raw, 0, tables)
    raw = dot(normed, arrived(0))
    if keep:
        held[1][:, width:] = raw
        put(1).start()
    keys = rotated(raw, 1, tables)
    values = dot(normed, arrived(1)).astype(bf16)
    if keep:
        held[2][...] = values
        put(2).start()
    mixed[...] = jnp.zeros_like(mixed)
    factor = head_size ** (-0.5) * math.log2(math.e)
    for start, span, members in head_groups(heads, head_size):
        window = slice(start, start + span)
        probs, parts = [], []
        for head in members:
            mask = head_mask(head, head_size, start, span)
            expon = jnp.exp2(dot_right(queries[:, window], keys[:, window] * mask) * factor)
            total = jnp.sum(expon, axis=-1, keepdims=True)
            probs.append((expon * (1.0 / total)).astype(bf16))
            parts.append(values[:, window] * mask)
        mixed[:, window] += dot(side_by_side(probs), one_above_other(parts))
    attended = mixed[...].astype(bf16)
    if keep:
        held[3][...] = attended
        put(3).start()
    branch = dot(attended, arrived(2))
    middle = flow + mod[2:3] * branch
    normed_two = (middle * inverse_rms(middle) * (1.0 + mod[4:5]) + mod[3:4]).astype(bf16)
    if keep:
        for which, value in ((4, branch), (5, middle), (6, normed_two)):
            held[which][...] = value
            put(which).start()
        for which in range(8):
            put(which).wait()
    else:
        middle_ref[...] = middle
        normed_two_ref[...] = normed_two


def attention_forward(x, received, mod, tables, gain, joined, walked, first, count, made=None):
    keep = received is not None
    images, unused, width = mod.shape
    tokens = x.shape[0]
    patches = tokens // images
    heads = width // tables[-1]
    cos, sin, *matrices, unused = tables
    parts, rows, unused = joined.shape
    row = lambda columns: pl.BlockSpec((patches, columns), lambda image: (first + image, 0))
    fixed = lambda array: pl.BlockSpec(array.shape, lambda image: (0,) * array.ndim)
    anywhere = pl.BlockSpec(memory_space=pl.ANY)
    shapes = [(width, f32), (width, bf16)]
    if keep:
        shapes = [
            (width, bf16),
            (2 * width, f32),
            (width, bf16),
            (width, bf16),
            (width, f32),
            (width, f32),
            (width, bf16),
            (width, bf16),
        ]
    made = [] if made is None else list(made)
    extra = [received] if keep else []
    inputs = 10 + len(extra)
    scratch = [
        pltpu.VMEM((3, parts, rows, width), bf16),
        pltpu.VMEM((patches, width), f32),
        pltpu.SemaphoreType.DMA((3,)),
    ]
    if keep:
        scratch += [pltpu.VMEM((patches, columns), kind) for columns, kind in shapes]
        scratch += [pltpu.SemaphoreType.DMA((len(shapes),))]

    def body(*refs):
        refs = refs[:inputs] + refs[inputs + len(made) :]
        attention_forward_kernel(heads, places_of(parts, walked), first, keep, refs)

    return pl.pallas_call(
        body,
        grid=(count,),
        in_specs=[pl.BlockSpec((patches, width), lambda image: (image, 0))] * len(extra)
        + [
            row(width),
            pl.BlockSpec((1, 8, width), lambda image: (first + image, 0, 0)),
            row(cos.shape[1]),
            row(sin.shape[1]),
            fixed(gain),
        ]
        + [fixed(matrix) for matrix in matrices]
        + [pl.BlockSpec((parts, rows, width), lambda image: (0, 0, 0))]
        + [anywhere] * (1 + len(made)),
        out_specs=[anywhere if keep else row(columns) for columns, kind in shapes],
        out_shape=[jax.ShapeDtypeStruct((tokens, columns), kind) for columns, kind in shapes],
        input_output_aliases={inputs + index: index for index in range(len(made))},
        scratch_shapes=scratch,
        compiler_params=params(),
        cost_estimate=cost(
            2 * count * patches * width * (4 * width + 2 * patches),
            8 * width * width + count * patches * width * 20,
        ),
    )(*extra, x, mod, cos, sin, gain, *matrices, joined, joined, *made)


def walk_chip(place, chips):
    return jnp.where(place < chips // 2, 2 * place, 2 * (chips - 1 - place) + 1)


def column_specs(joined, first, hidden, chips, step):
    parts, rows, unused = joined.shape
    if not chips:
        return [pl.BlockSpec((parts, rows, step), lambda i: (0, 0, first // step + i))]
    each = hidden // chips
    number = step // each

    def spec(which):
        return pl.BlockSpec(
            (parts, rows, each),
            lambda i: (0, 0, first // each + walk_chip(i * number + which, chips)),
        )

    return [spec(which) for which in range(number)]


def step_matrix(refs, places):
    return side_by_side([whole_rows(ref, places) for ref in refs])


def gate_up(normed_two, joined, hidden, walked, chips):
    tokens, width = normed_two.shape
    step = 768
    places = places_of(joined.shape[0], walked)
    gate_specs = column_specs(joined, 4 * width, hidden, chips, step)
    up_specs = column_specs(joined, 4 * width + hidden, hidden, chips, step)
    number = len(gate_specs)

    def body(normed_ref, *refs):
        normed = normed_ref[...]
        gate = dot(normed, step_matrix(refs[:number], places))
        up = dot(normed, step_matrix(refs[number : 2 * number], places))
        refs[-1][...] = (gate * (1.0 / (1.0 + jnp.exp(-gate))) * up).astype(bf16)

    return pl.pallas_call(
        body,
        grid=(hidden // step,),
        in_specs=[pl.BlockSpec((tokens, width), lambda i: (0, 0))] + gate_specs + up_specs,
        out_specs=pl.BlockSpec((tokens, step), lambda i: (0, i)),
        out_shape=jax.ShapeDtypeStruct((tokens, hidden), bf16),
        compiler_params=params(),
        cost_estimate=cost(4 * tokens * width * hidden, 4 * width * hidden + 2 * tokens * hidden),
    )(normed_two, *[joined] * (2 * number))


def down_projection(active, act, down, middle, mod, first, count, keep, step):
    hidden = act.shape[1]
    images, unused, width = mod.shape
    patches = act.shape[0] // images
    tokens = count * patches
    outs = [jax.ShapeDtypeStruct((tokens, width), bf16)]
    scratch = [pltpu.VMEM((tokens, width), f32)]
    if keep:
        outs.append(jax.ShapeDtypeStruct((tokens, width), f32))
        scratch = []

    def body(active_ref, act_ref, middle_ref, mod_ref, down_ref, result_ref, total):
        index = pl.program_id(0)

        @pl.when(active_ref[0] == 0)
        def _():
            result_ref[...] = jnp.zeros_like(result_ref)

        @pl.when(active_ref[0] != 0)
        def _():
            term = dot(act_ref[...], down_ref[...])

            @pl.when(index == 0)
            def _():
                total[...] = term

            @pl.when(index > 0)
            def _():
                total[...] += term

            @pl.when(index == hidden // step - 1)
            def _():
                for image in range(count):
                    at = slice(image * patches, (image + 1) * patches)
                    gate = mod_ref[first + image, 5:6]
                    result_ref[at] = (middle_ref[at] + gate * total[at]).astype(bf16)

    return pl.pallas_call(
        body,
        grid_spec=pltpu.PrefetchScalarGridSpec(
            num_scalar_prefetch=1,
            grid=(hidden // step,),
            in_specs=[
                pl.BlockSpec((tokens, step), lambda i, active: (first // count, i * active[0])),
                pl.BlockSpec((tokens, width), lambda i, active: (first // count, 0)),
                pl.BlockSpec(mod.shape, lambda i, active: (0, 0, 0)),
                pl.BlockSpec((step, width), lambda i, active: (i * active[0], 0)),
            ],
            out_specs=[pl.BlockSpec((tokens, width), lambda i, active: (0, 0))] * len(outs),
            scratch_shapes=scratch,
        ),
        out_shape=outs,
        compiler_params=params(),
        cost_estimate=cost(2 * tokens * width * hidden, 2 * width * hidden + 8 * tokens * width),
    )(active, act, middle, mod, down)


def incoming(cot_ref, back_refs, image, at):
    value = cot_ref[at].astype(f32)
    return value + back_refs[image][...].astype(f32) if back_refs else value


def mlp_gradient(cot, backs, mod, first, count):
    images, unused, width = mod.shape
    patches = cot.shape[0] // images

    def body(cot_ref, mod_ref, *refs):
        for image in range(count):
            at = slice(image * patches, (image + 1) * patches)
            grads = incoming(cot_ref, refs[: len(backs)], image, at)
            refs[-1][at] = (mod_ref[first + image, 5:6] * grads).astype(bf16)

    return pl.pallas_call(
        body,
        grid=(1,),
        in_specs=[
            pl.BlockSpec((count * patches, width), lambda i: (first // count, 0)),
            pl.BlockSpec(mod.shape, lambda i: (0, 0, 0)),
        ]
        + [pl.BlockSpec((patches, width), lambda i: (0, 0))] * len(backs),
        out_specs=pl.BlockSpec((count * patches, width), lambda i: (0, 0)),
        out_shape=jax.ShapeDtypeStruct((count * patches, width), bf16),
        compiler_params=params(),
        cost_estimate=cost(0, 6 * count * patches * width),
    )(cot, mod, *backs)


def stacked(refs):
    return refs[0][...] if len(refs) == 1 else jnp.concatenate([ref[...] for ref in refs], axis=0)


def whole_specs(arrays):
    return [pl.BlockSpec(array.shape, lambda i: (0, 0)) for array in arrays]


def act_backward(active, mlp_grads, down, step):
    hidden, width = down.shape
    tokens = sum(grad.shape[0] for grad in mlp_grads)

    def body(active_ref, *refs):
        @pl.when(active_ref[0] == 0)
        def _():
            refs[-1][...] = jnp.zeros_like(refs[-1])

        @pl.when(active_ref[0] != 0)
        def _():
            refs[-1][...] = dot_right(stacked(refs[:-2]), refs[-2][...]).astype(bf16)

    return pl.pallas_call(
        body,
        grid_spec=pltpu.PrefetchScalarGridSpec(
            num_scalar_prefetch=1,
            grid=(hidden // step,),
            in_specs=[pl.BlockSpec(grad.shape, lambda i, active: (0, 0)) for grad in mlp_grads]
            + [pl.BlockSpec((step, width), lambda i, active: (i * active[0], 0))],
            out_specs=pl.BlockSpec((tokens, step), lambda i, active: (0, i)),
        ),
        out_shape=jax.ShapeDtypeStruct((tokens, hidden), bf16),
        compiler_params=params(),
        cost_estimate=cost(2 * tokens * width * hidden, 2 * width * hidden + 4 * tokens * width),
    )(active, *mlp_grads, down)


def mlp_backward(
    cot, backs, act_grad, forward, joined, middle, mod, walked, chips, sums_of
):
    tokens, hidden = act_grad.shape
    images, unused, width = mod.shape
    patches = tokens // images
    parts, rows, unused = joined.shape
    places = places_of(parts, walked)
    step = 768
    count = hidden // step
    gate_specs = column_specs(joined, 4 * width, hidden, chips, step)
    up_specs = column_specs(joined, 4 * width + hidden, hidden, chips, step)
    number = len(gate_specs)
    fresh, keep = len(forward) == 1, sums_of is not None
    whole = pl.BlockSpec((tokens, width), lambda i: (0, 0))
    block = pl.BlockSpec((tokens, step), lambda i: (0, i))
    anywhere = pl.BlockSpec(memory_space=pl.ANY)
    late = [cot, middle] + (list(sums_of) if keep else [])

    def body(act_grad_ref, mod_ref, joined_ref, *refs):
        refs = list(refs)

        def taken(size):
            first = refs[:size]
            del refs[:size]
            return first

        gate_refs, up_refs = taken(number), taken(number)

        forward_refs, back_refs, sources = taken(len(forward)), taken(len(backs)), taken(len(late))
        middle_grad_ref, mixed_grad_ref = taken(2)
        fresh_refs = taken(3 if fresh else 0)
        kept_refs = taken(4 if keep else 0)
        total, out_weight, sem = taken(3)
        copies, (sems,) = taken(len(late)), refs
        cot_ref, middle_ref = copies[:2]
        index = pl.program_id(0)
        fetches = [
            pltpu.make_async_copy(joined_ref.at[:, :, pl.ds(3 * width, width)], out_weight, sem)
        ] + [
            pltpu.make_async_copy(source, copies[which], sems.at[which])
            for which, source in enumerate(sources)
        ]

        @pl.when(index == 0)
        def _():
            for fetch in fetches:
                fetch.start()

        gate_weight = step_matrix(gate_refs, places)
        up_weight = step_matrix(up_refs, places)
        if fresh:
            normed = forward_refs[0][...]
            gate, up = dot(normed, gate_weight), dot(normed, up_weight)
        else:
            gate, up = (ref[...].astype(f32) for ref in forward_refs)
        sigma = 1.0 / (1.0 + jnp.exp(-gate))
        slope = act_grad_ref[...].astype(f32) * sigma
        gate_grad = (slope * up * (1.0 + gate * (1.0 - sigma))).astype(bf16)
        up_grad = (slope * gate).astype(bf16)
        if fresh:
            fresh_refs[0][...] = (gate * sigma * up).astype(bf16)
            fresh_refs[1][...] = gate.astype(bf16)
            fresh_refs[2][...] = up.astype(bf16)
        if keep:
            kept_refs[0][...] = gate_grad
            kept_refs[1][...] = up_grad
        term = dot_right(side_by_side([gate_grad, up_grad]), side_by_side([gate_weight, up_weight]))

        @pl.when(index == 0)
        def _():
            total[...] = term

        @pl.when(index > 0)
        def _():
            total[...] += term

        @pl.when(index == count - 1)
        def _():
            for fetch in fetches:
                fetch.wait()
            matrix = whole_rows(out_weight, places)
            for image in range(images):
                at = slice(image * patches, (image + 1) * patches)
                mod = mod_ref[image]
                grad, flow = total[at], middle_ref[at]
                inverse = inverse_rms(flow)
                normal = flow * inverse
                scaled = grad * (1.0 + mod[4:5])
                mean = jnp.mean(scaled * normal, axis=-1, keepdims=True)
                out_grad = incoming(cot_ref, back_refs, image, at)
                middle_grad = out_grad + (scaled - normal * mean) * inverse
                middle_grad_ref[at] = middle_grad
                branch_grad = (mod[2:3] * middle_grad).astype(bf16)
                mixed_grad_ref[at] = dot_right(branch_grad, matrix).astype(bf16)
                if keep:
                    mlp_ref, branch_ref = copies[2:]
                    kept_refs[2][at] = branch_grad
                    terms = [middle_grad * branch_ref[at], grad, grad * normal, out_grad * mlp_ref[at]]
                    for place, value in enumerate(terms):
                        kept_refs[3][image, place : place + 1] = jnp.sum(value, axis=0, keepdims=True)

    out_shapes = [
        jax.ShapeDtypeStruct((tokens, width), f32),
        jax.ShapeDtypeStruct((tokens, width), bf16),
    ]
    out_specs = [whole, whole]
    if fresh:
        out_shapes += [jax.ShapeDtypeStruct((tokens, hidden), bf16)] * 3
        out_specs += [block] * 3
    if keep:
        out_shapes += [jax.ShapeDtypeStruct((tokens, hidden), bf16)] * 2
        out_shapes += [jax.ShapeDtypeStruct((tokens, width), bf16)]
        out_shapes += [jax.ShapeDtypeStruct((images, 8, width), f32)]
        out_specs += [block, block, whole, pl.BlockSpec((images, 8, width), lambda i: (0, 0, 0))]
    return pl.pallas_call(
        body,
        grid=(count,),
        in_specs=[block, pl.BlockSpec(mod.shape, lambda i: (0, 0, 0)), anywhere]
        + gate_specs
        + up_specs
        + [whole if fresh else block] * len(forward)
        + [pl.BlockSpec((patches, width), lambda i: (0, 0))] * len(backs)
        + [anywhere] * len(late),
        out_specs=out_specs,
        out_shape=out_shapes,
        scratch_shapes=[
            pltpu.VMEM((tokens, width), f32),
            pltpu.VMEM((parts, rows, width), bf16),
            pltpu.SemaphoreType.DMA,
        ]
        + [pltpu.VMEM(array.shape, array.dtype) for array in late]
        + [pltpu.SemaphoreType.DMA((len(late),))],
        compiler_params=params(),
        cost_estimate=cost(
            2 * tokens * width * (4 * hidden + width), 4 * width * hidden + 6 * tokens * hidden
        ),
    )(act_grad, mod, joined, *[joined] * (2 * number), *forward, *backs, *late)


def attention_backward_kernel(heads, places, first, keep, refs):
    raw_hbm, value_hbm, mixed_grad_hbm, middle_grad_hbm, x_hbm = refs[:5]
    mod_ref, cos_ref, sin_ref, gain_ref, sum_ref, spread_ref, repeat_ref, joined_ref = refs[5:13]
    refs = refs[13:]
    if keep:
        flow_grad_ref, qkv_grad_ref, sums_ref = refs[:3]
        refs = refs[3:]
    else:
        back_ref = refs[0]
        refs = refs[1:]
    weight, scales, query_total, key_total, value_total = refs[:5]
    raw_ref, value_ref, mixed_grad_ref, middle_grad_ref, x_ref, sems = refs[5:]
    patches, width = x_ref.shape
    head_size = width // heads
    quarter = head_size // 4
    factor = head_size ** (-0.5)
    image = pl.program_id(0)
    rows = pl.ds((first + image) * patches, patches)
    sources = [
        raw_hbm.at[rows, pl.ds(0, width)],
        raw_hbm.at[rows, pl.ds(width, width)],
        value_hbm.at[rows],
        mixed_grad_hbm.at[rows],
        middle_grad_hbm.at[rows],
        x_hbm.at[rows],
    ]
    targets = [raw_ref.at[0], raw_ref.at[1], value_ref, mixed_grad_ref, middle_grad_ref, x_ref]
    copies = [
        pltpu.make_async_copy(source, target, sems.at[3 + which])
        for which, (source, target) in enumerate(zip(sources, targets))
    ]
    for copy in copies[:4]:
        copy.start()

    def fetch(part):
        return pltpu.make_async_copy(
            joined_ref.at[:, :, pl.ds(part * width, width)], weight.at[part], sems.at[part]
        )

    @pl.when(image == 0)
    def _():
        for part in range(3):
            fetch(part).start()

    for copy in copies[4:]:
        copy.start()
    first_half = first_half_mask((1, width), quarter)
    cos, sin = dot(cos_ref[...], repeat_ref[...]), dot(sin_ref[...], repeat_ref[...])
    summing, spreading = sum_ref[...], spread_ref[...]
    tables = (cos, sin, gain_ref, summing, spreading, head_size)
    copies[0].wait()
    queries = rotated(raw_ref[0], 0, tables, scales)
    copies[1].wait()
    keys = rotated(raw_ref[1], 1, tables, scales)
    for copy in copies[2:4]:
        copy.wait()
    values, mixed_grad = value_ref[...], mixed_grad_ref[...]
    query_total[...] = jnp.zeros_like(query_total)
    key_total[...] = jnp.zeros_like(key_total)
    value_total[...] = jnp.zeros_like(value_total)
    for start, span, members in head_groups(heads, head_size):
        window = slice(start, start + span)
        probs, slopes, key_parts, query_parts, grad_parts = [], [], [], [], []
        for head in members:
            mask = head_mask(head, head_size, start, span)
            key_part, query_part = keys[:, window] * mask, queries[:, window] * mask
            grad_part = mixed_grad[:, window] * mask
            scores = dot_right(key_part, queries[:, window])
            expon = jnp.exp2(scores * (factor * math.log2(math.e)))
            prob = expon * (1.0 / jnp.sum(expon, axis=0, keepdims=True))
            prob_grad = dot_right(values[:, window], grad_part)
            middle = jnp.sum(prob * prob_grad, axis=0, keepdims=True)
            probs.append(prob.astype(bf16))
            slopes.append((prob * (prob_grad - middle)).astype(bf16))
            key_parts.append(key_part)
            query_parts.append(query_part)
            grad_parts.append(grad_part)
        value_total[:, window] += dot(side_by_side(probs), one_above_other(grad_parts))
        key_total[:, window] += dot(side_by_side(slopes), one_above_other(query_parts))
        query_total[:, window] += dot_left(one_above_other(slopes), one_above_other(key_parts))

    def raw_grad(part, total):
        turned = total[...] * factor
        grad = turned * cos + partner(turned * sin, first_half, quarter)
        scale = scales[part]
        normal = raw_ref[part] * scale
        if keep:
            sums_ref[0, 2 + part : 3 + part] = jnp.sum(grad * normal, axis=0, keepdims=True)
        grad = grad * gain_ref[part : part + 1]
        mean = dot((grad * normal).astype(bf16), summing) * (1.0 / head_size)
        mean = dot(two_terms(mean), spreading)
        return (scale * (grad - normal * mean)).astype(bf16)

    def arrived(part):
        @pl.when(image == 0)
        def _():
            fetch(part).wait()

        return whole_rows(weight.at[part], places)

    parts = [raw_grad(0, query_total), raw_grad(1, key_total), value_total[...].astype(bf16)]
    grad = None
    for part in range(3):
        if keep:
            qkv_grad_ref[:, part * width : (part + 1) * width] = parts[part]
        term = dot_right(parts[part], arrived(part))
        grad = term if grad is None else grad + term
    for copy in copies[4:]:
        copy.wait()
    mod = mod_ref[0]
    flow = x_ref[...].astype(f32)
    inverse = inverse_rms(flow)
    normal = flow * inverse
    scaled = grad * (1.0 + mod[1:2])
    mean = jnp.mean(scaled * normal, axis=-1, keepdims=True)
    flow_grad = middle_grad_ref[...] + (scaled - normal * mean) * inverse
    if keep:
        flow_grad_ref[...] = flow_grad
        sums_ref[0, 0:1] = jnp.sum(grad, axis=0, keepdims=True)
        sums_ref[0, 1:2] = jnp.sum(grad * normal, axis=0, keepdims=True)
    else:
        back_ref[...] = flow_grad.astype(bf16)


def attention_backward(
    active, raw, value, mixed_grad, middle_grad, x, mod, tables, gain, joined, walked, first, count, keep
):
    images, unused, width = mod.shape
    patches = x.shape[0] // images
    tokens = count * patches
    heads = width // tables[-1]
    cos, sin, *matrices, unused = tables
    parts, rows, unused = joined.shape
    row = lambda columns: pl.BlockSpec((patches, columns), lambda image: (first + image, 0))
    token = lambda columns: pl.BlockSpec((patches, columns), lambda image: (image, 0))
    fixed = lambda array: pl.BlockSpec(array.shape, lambda image: (0,) * array.ndim)
    anywhere = pl.BlockSpec(memory_space=pl.ANY)
    out_shapes = [jax.ShapeDtypeStruct((tokens, width), bf16)]
    out_specs = [token(width)]
    if keep:
        out_shapes = [
            jax.ShapeDtypeStruct((tokens, width), f32),
            jax.ShapeDtypeStruct((tokens, 3 * width), bf16),
            jax.ShapeDtypeStruct((count, 8, width), f32),
        ]
        out_specs = [
            token(width),
            token(3 * width),
            pl.BlockSpec((1, 8, width), lambda image: (image, 0, 0)),
        ]

    def body(active_ref, *refs):
        @pl.when(active_ref[0] == 0)
        def _():
            for ref in refs[13 : 13 + len(out_shapes)]:
                ref[...] = jnp.zeros_like(ref)

        @pl.when(active_ref[0] != 0)
        def _():
            attention_backward_kernel(heads, places_of(parts, walked), first, keep, refs)

    return pl.pallas_call(
        body,
        grid=(count,),
        in_specs=[pl.BlockSpec(memory_space=pltpu.SMEM)]
        + [anywhere] * 5
        + [
            pl.BlockSpec((1, 8, width), lambda image: (first + image, 0, 0)),
            row(cos.shape[1]),
            row(sin.shape[1]),
            fixed(gain),
        ]
        + [fixed(matrix) for matrix in matrices]
        + [anywhere],
        out_specs=out_specs,
        out_shape=out_shapes,
        scratch_shapes=[
            pltpu.VMEM((3, parts, rows, width), bf16),
            pltpu.VMEM((2, patches, width), f32),
            pltpu.VMEM((patches, width), f32),
            pltpu.VMEM((patches, width), f32),
            pltpu.VMEM((patches, width), f32),
            pltpu.VMEM((2, patches, width), f32),
            pltpu.VMEM((patches, width), bf16),
            pltpu.VMEM((patches, width), bf16),
            pltpu.VMEM((patches, width), f32),
            pltpu.VMEM((patches, width), bf16),
            pltpu.SemaphoreType.DMA((9,)),
        ],
        compiler_params=params(),
        cost_estimate=cost(
            2 * tokens * width * (3 * width + 5 * patches),
            6 * width * width + tokens * width * 20,
        ),
    )(active, raw, value, mixed_grad, middle_grad, x, mod, cos, sin, gain, *matrices, joined)


def down_grad(mlp_grads, cot, back, act, mod, step):
    tokens, hidden = act.shape
    images, unused, width = mod.shape
    patches = tokens // images
    last = images - 1

    def body(act_ref, cot_ref, back_ref, mod_ref, *refs):
        given, (out_ref, last_ref, mlp_grad) = refs[:last], refs[last:]

        @pl.when(pl.program_id(0) == 0)
        def _():
            grads = incoming(cot_ref, [back_ref], 0, slice(0, patches))
            value = (mod_ref[last, 5:6] * grads).astype(bf16)
            last_ref[...] = value
            for image in range(last):
                mlp_grad[image * patches : (image + 1) * patches] = given[image][...]
            mlp_grad[last * patches :] = value

        out_ref[...] = dot_left(act_ref[...], mlp_grad[...]).astype(bf16)

    return pl.pallas_call(
        body,
        grid=(hidden // step,),
        in_specs=[
            pl.BlockSpec((tokens, step), lambda i: (0, i)),
            pl.BlockSpec((patches, width), lambda i: (last, 0)),
            pl.BlockSpec((patches, width), lambda i: (0, 0)),
            pl.BlockSpec(mod.shape, lambda i: (0, 0, 0)),
        ]
        + whole_specs(mlp_grads),
        out_specs=[
            pl.BlockSpec((step, width), lambda i: (i, 0)),
            pl.BlockSpec((patches, width), lambda i: (0, 0)),
        ],
        out_shape=[
            jax.ShapeDtypeStruct((hidden, width), bf16),
            jax.ShapeDtypeStruct((patches, width), bf16),
        ],
        scratch_shapes=[pltpu.VMEM((tokens, width), bf16)],
        compiler_params=params(),
        cost_estimate=cost(2 * tokens * width * hidden, 2 * width * hidden),
    )(act, cot, back, mod, *mlp_grads)


def matrix_grad_kernel(places, counts, *refs):
    pairs = len(counts)
    inputs, grads, out_ref = refs[:pairs], refs[pairs : 2 * pairs], refs[2 * pairs]
    rows = out_ref.shape[1]
    step = pl.program_id(0)
    first = 0
    for index in range(pairs):

        @pl.when(jnp.logical_and(step >= first, step < first + counts[index]))
        def _(index=index):
            product = dot_left(inputs[index][...], grads[index][...]).astype(bf16)
            for part, place in enumerate(places):
                out_ref[place] = product[part * rows : (part + 1) * rows]

        first += counts[index]


def matrix_grad(inputs, grads, step, parts, walked):
    tokens, width = inputs[0].shape
    counts = [grad.shape[1] // step for grad in grads]
    columns = sum(counts) * step
    rows = width // parts
    firsts = [sum(counts[:index]) for index in range(len(counts))]

    def grad_spec(first, count):
        return pl.BlockSpec((tokens, step), lambda i: (0, jnp.clip(i - first, 0, count - 1)))

    return pl.pallas_call(
        functools.partial(matrix_grad_kernel, places_of(parts, walked), counts),
        grid=(sum(counts),),
        in_specs=[pl.BlockSpec((tokens, width), lambda i: (0, 0))] * len(inputs)
        + [grad_spec(first, count) for first, count in zip(firsts, counts)],
        out_specs=pl.BlockSpec((parts, rows, step), lambda i: (0, 0, i)),
        out_shape=jax.ShapeDtypeStruct((parts, rows, columns), bf16),
        compiler_params=params(),
        cost_estimate=cost(2 * tokens * width * columns, 2 * width * columns),
    )(*inputs, *grads)


def walk_of(count):
    chips = count // 2
    order = [chip for chip in range(chips) if chip % 2 == 0]
    order += [chip for chip in reversed(range(chips)) if chip % 2 == 1]
    return [2 * chip + core for chip in order for core in (0, 1)]


def from_walk(rows, count):
    blocks = rows.reshape(count // 2, -1, rows.shape[-1])
    places = places_of(count // 2, True)
    return jnp.concatenate([blocks[place] for place in places], axis=0)


def columns_to_walk(matrix, count):
    each = matrix.shape[1] // (count // 2)
    chips = [device // 2 for device in walk_of(count)[::2]]
    return jnp.concatenate([matrix[:, chip * each : (chip + 1) * each] for chip in chips], axis=1)


def columns_from_walk(matrix, count):
    each = matrix.shape[1] // (count // 2)
    places = places_of(count // 2, True)
    return jnp.concatenate(
        [matrix[:, place * each : (place + 1) * each] for place in places], axis=1
    )


def to_walk(rows, count):
    blocks = rows.reshape(count // 2, -1, rows.shape[-1])
    return jnp.concatenate([blocks[device // 2] for device in walk_of(count)[::2]], axis=0)


def gather_walk(rows, count):
    return lax.all_gather(rows, "dp", axis=0, tiled=True, axis_index_groups=[walk_of(count)])


def scatter_walk(rows, groups):
    part = lax.psum_scatter(
        rows, "dp", scatter_dimension=0, tiled=True, axis_index_groups=groups
    )
    return lax.optimization_barrier(part)


def scatter_cores(rows, count):
    me = lax.axis_index("dp")
    width = rows.shape[-1]
    pairs = rows.reshape(count // 2, 2, -1, width)
    give = lax.dynamic_index_in_dim(pairs, 1 - me % 2, 1, keepdims=False)
    keep = lax.dynamic_index_in_dim(pairs, me % 2, 1, keepdims=False)
    both = keep.astype(f32) + swapped(give, 1, count).astype(f32)
    both = both.astype(bf16).reshape(-1, width)
    walk = walk_of(count)
    return both, [walk[0::2], walk[1::2]]


def as_parts(rows, count):
    each = rows.shape[0] // (count // 2)
    if each % 16 == 0:
        return rows.reshape(count // 2, each, rows.shape[1]), True
    whole = from_walk(rows, count)
    return whole[None], False


def swapped(block, bit, count):
    return lax.ppermute(block, "dp", [(device, device ^ bit) for device in range(count)])


def gather_small(block, count):
    me = lax.axis_index("dp")
    block = block[None]
    bit = count // 2
    while bit:
        other = swapped(block, bit, count)
        low = (me & bit) == 0
        pair = [jnp.where(low, block, other), jnp.where(low, other, block)]
        block = jnp.stack(pair, axis=1).reshape(2 * block.shape[0], *block.shape[1:])
        bit //= 2
    return block


def scatter_small(blocks, count):
    me = lax.axis_index("dp")
    bit = 1
    while bit < count:
        pairs = blocks.reshape(blocks.shape[0] // 2, 2, *blocks.shape[1:])
        mine = jnp.where((me & bit) == 0, 0, 1)
        give = lax.dynamic_index_in_dim(pairs, 1 - mine, 1, keepdims=False)
        keep = lax.dynamic_index_in_dim(pairs, mine, 1, keepdims=False)
        blocks = keep + swapped(give, bit, count)
        bit *= 2
    return blocks[0]


def time_features(timestep_ids, width):
    half_width = width // 2
    frequency = jnp.exp(-math.log(10000.0) * jnp.arange(half_width, dtype=f32) / half_width)
    angle_rows = timestep_ids.astype(f32)[:, None] * frequency[None, :]
    return jnp.concatenate([jnp.cos(angle_rows), jnp.sin(angle_rows)], axis=-1)


def rotation_tables(positions, width, head_size):
    quarter = head_size // 4
    frequency = jnp.exp(-math.log(10000.0) * jnp.arange(quarter, dtype=f32) / quarter)
    places = positions.reshape(-1, 1)
    row_angle = (places // GRID).astype(f32) * frequency
    col_angle = (places % GRID).astype(f32) * frequency
    row_cos, row_sin = jnp.cos(row_angle), jnp.sin(row_angle)
    col_cos, col_sin = jnp.cos(col_angle), jnp.sin(col_angle)
    cos = jnp.concatenate([row_cos, row_cos, col_cos, col_cos], axis=1)
    sin = jnp.concatenate([-row_sin, row_sin, -col_sin, col_sin], axis=1)
    padding = ((0, 0), (0, LANES - head_size))
    number = jnp.arange(LANES)
    column = jnp.arange(width)
    summing = (column[:, None] // head_size == number[None, :]).astype(bf16)
    spreading = (column[None, :] // head_size == number[:, None]).astype(bf16)
    repeating = (column[None, :] % head_size == number[:, None]).astype(bf16)
    return (
        two_terms(jnp.pad(cos, padding)),
        two_terms(jnp.pad(sin, padding)),
        summing,
        jnp.concatenate([spreading, spreading]),
        jnp.concatenate([repeating, repeating]),
    )


def per_device(
    tokens,
    cotangent,
    labels,
    timesteps,
    positions,
    label_table,
    ada_weight,
    qkv_weight,
    out_weight,
    gate_weight,
    up_weight,
    down_weight,
    q_gain,
    k_gain,
):
    first_section = lax.axis_index("section") == 0
    first_only = first_section.astype(jnp.int32).reshape(1)
    second_only = 1 - first_only
    always = jnp.ones((1,), jnp.int32)
    count = lax.axis_size("dp")
    me = lax.axis_index("dp")
    images, patches, width = tokens.shape
    hidden = gate_weight.shape[2]
    head_size = q_gain.shape[1]
    heads = width // head_size
    rows = ada_weight.shape[1]
    classes = label_table.shape[0]

    gate_matrix, up_matrix, chips = gate_weight[0], up_weight[0], count // 2
    if hidden // chips % LANES:
        gate_matrix, up_matrix = columns_to_walk(gate_matrix, count), columns_to_walk(up_matrix, count)
        chips = 0
    joined = gather_walk(
        jnp.concatenate([qkv_weight[0], out_weight[0], gate_matrix, up_matrix], axis=1), count
    )

    ids = gather_small(jnp.stack([labels, timesteps]), count)
    all_labels = ids[:, 0].reshape(-1)
    all_times = ids[:, 1].reshape(-1)
    label_hot = all_labels[:, None] == jnp.arange(classes, dtype=jnp.int32)[None, :]
    condition = dot(label_hot.astype(bf16), label_table) + time_features(all_times, width)
    sigma_cond = jax.nn.sigmoid(condition)
    silu_cond = (condition * sigma_cond).astype(bf16)
    silu_rows = lax.dynamic_slice_in_dim(silu_cond, me * rows, rows, 1)
    mod_part = dot(silu_rows, ada_weight[0])
    mod = scatter_small(mod_part.reshape(count, images, -1), count).reshape(images, 6, width)
    mod = jnp.pad(mod, ((0, 0), (0, 2), (0, 0)))
    tables = rotation_tables(positions, width, head_size)
    flat = tokens.reshape(images * patches, width)
    own = jnp.where(first_section, flat, jnp.zeros_like(flat))

    down, joined, mod, own, tables = lax.optimization_barrier(
        (down_weight[0], joined, mod, own, tables)
    )
    down = gather_walk(down, count)
    joined, walked = as_parts(joined, count)
    tables = (*tables, head_size)
    gain = jnp.pad(jnp.tile(jnp.concatenate([q_gain, k_gain]), (1, heads)), ((0, 6), (0, 0)))

    cot = cotangent[0].reshape(images * patches, width)
    middle, normed_two = attention_forward(
        flat, None, mod, tables, gain, joined, walked, 0, images
    )
    act = gate_up(normed_two, joined, hidden, walked, chips)
    received = []
    for image in range(images):
        (early,) = down_projection(
            first_only, act, down, middle, mod, image, 1, False, hidden // 2
        )
        received.append(lax.ppermute(early, "section", [(0, 1)]))
    mlp_grad, unused = lax.optimization_barrier((mlp_gradient(cot, [], mod, 0, images), early))
    mlp_grads = [mlp_grad]
    act_grad = act_backward(second_only, mlp_grads, down, hidden // 2)
    kept = None
    for image in range(images):
        kept = attention_forward(
            own, received[image], mod, tables, gain, joined, walked, image, 1, kept
        )
    normed, raw, values, attended, branch, middle, normed_two, layer_in = kept

    middle_grad, mixed_grad, act, gate, up = mlp_backward(
        cot, [], act_grad, [normed_two], joined, middle, mod, walked, chips, None
    )
    backs = []
    for image in range(images):
        (early,) = attention_backward(
            second_only,
            raw,
            values,
            mixed_grad,
            middle_grad,
            layer_in,
            mod,
            tables,
            gain,
            joined,
            walked,
            image,
            1,
            False,
        )
        backs.append(lax.ppermute(early, "section", [(1, 0)]))
    late_act, unused = lax.optimization_barrier((act, early))
    result, mlp = down_projection(
        always, late_act, down, middle, mod, 0, images, True, hidden // 2
    )

    late_cot, unused = lax.optimization_barrier((cot, mlp))
    mlp_grads = [
        mlp_gradient(late_cot, [back], mod, image, 1) for image, back in enumerate(backs[:-1])
    ]
    down_term, mlp_grad = down_grad(mlp_grads, late_cot, backs[-1], act, mod, hidden // 4)
    mlp_grads = [*mlp_grads, mlp_grad]
    down_term, mlp_grads = lax.optimization_barrier((down_term, mlp_grads))
    down_part = scatter_walk(down_term, [walk_of(count)])
    act_grad = act_backward(always, mlp_grads, down, hidden // 2)
    middle_grad, mixed_grad, gate_grad, up_grad, branch_grad, mlp_sums = mlp_backward(
        cot, backs, act_grad, [gate, up], joined, middle, mod, walked, chips, [mlp, branch]
    )

    def matrix_term(inputs, grads, step):
        term = matrix_grad(inputs, grads, step, joined.shape[0], walked).reshape(width, -1)
        return term if walked else to_walk(term, count)

    gate_up_term = matrix_term([normed_two, normed_two], [gate_grad, up_grad], hidden // 2)
    gate_up_term, down_part = lax.optimization_barrier((gate_up_term, down_part))
    gate_up_part = scatter_walk(gate_up_term, [walk_of(count)])
    flow_grad, qkv_grad, attention_sums = attention_backward(
        always,
        raw,
        values,
        mixed_grad,
        middle_grad,
        layer_in,
        mod,
        tables,
        gain,
        joined,
        walked,
        0,
        images,
        True,
    )
    rest_term = matrix_term([normed, attended], [qkv_grad, branch_grad], width)
    rest_term, attention_sums = lax.optimization_barrier((rest_term, attention_sums))
    rest_term, groups = scatter_cores(rest_term, count)
    mod_grad = jnp.concatenate([attention_sums[:, :2], mlp_sums[:, :4]], axis=1)
    mod_grad = mod_grad.reshape(images, -1).astype(bf16)
    mod_all = gather_small(mod_grad, count).reshape(-1, mod_grad.shape[1])
    rest_term, gate_up_part, mod_all = lax.optimization_barrier((rest_term, gate_up_part, mod_all))
    rest_part = scatter_walk(rest_term, groups)
    flow_grad = flow_grad.reshape(images, patches, width)
    input_grads = jnp.where(first_section, flow_grad, flow_grad.astype(bf16).astype(f32))

    head_sums = jnp.sum(attention_sums[:, 2:4], axis=0).reshape(2, heads, head_size)
    ada_part = dot_left(silu_rows, mod_all)
    silu_grad = dot_right(mod_all, ada_weight[0])
    silu_grad = silu_grad + lax.ppermute(silu_grad, "section", [(0, 1), (1, 0)])
    silu_all = gather_small(silu_grad, count)
    gain_all = jnp.sum(gather_small(jnp.sum(head_sums, axis=1), count), axis=0)
    silu_all = jnp.swapaxes(silu_all, 0, 1).reshape(condition.shape)
    cond_grad = silu_all * sigma_cond * (1.0 + condition * (1.0 - sigma_cond))
    table_grad = lax.dot_general(
        label_hot.astype(f32),
        cond_grad,
        (((0,), (0,)), ((), ())),
        precision=lax.Precision.HIGHEST,
        preferred_element_type=f32,
    )
    return (
        result.reshape(1, images, patches, width),
        input_grads[None],
        table_grad,
        ada_part[None],
        rest_part[None, :, : 3 * width].astype(f32),
        rest_part[None, :, 3 * width :].astype(f32),
        columns_from_walk(gate_up_part[:, :hidden], count)[None].astype(f32),
        columns_from_walk(gate_up_part[:, hidden:], count)[None].astype(f32),
        down_part[None].astype(f32),
        gain_all[None, 0],
        gain_all[None, 1],
    )


def solution(mesh):
    placed = (
        P("dp", None, None),
        P("section", "dp", None, None),
        P("dp"),
        P("dp"),
        P("dp", None),
        P(),
        P("section", "dp", None),
        P("section", "dp", None),
        P("section", "dp", None),
        P("section", "dp", None),
        P("section", "dp", None),
        P("section", "dp", None),
        P("section", None),
        P("section", None),
    )
    return jax.shard_map(
        per_device,
        mesh=mesh,
        in_specs=placed,
        out_specs=(
            P("section", "dp", None, None),
            P("section", "dp", None, None),
            P(),
            P("section", "dp", None),
            P("section", "dp", None),
            P("section", "dp", None),
            P("section", "dp", None),
            P("section", "dp", None),
            P("section", "dp", None),
            P("section", None),
            P("section", None),
        ),
        check_vma=False,
    )
```
